32 devices in a mesh: groups: 1, replica: 32 (over z, y, x, core).
Axes of the slice: x: 2, y: 2, z: 4, core: 2. Of those that a mesh axis runs over, the one named last changes fastest.
Arguments:
- queries: bfloat16 [8192, 1024], P(('groups', 'replica')), may hold values from -15 to 15
- suffix_kv: bfloat16 [8192, 256], P(('groups', 'replica')), may hold values from -6 to 6
- own_cache: bfloat16 [16384, 256], P(('groups', 'replica')), may hold values from -6 to 6
- ctx_len: int32 [32], P(('groups', 'replica')), may hold values from 64 to 512, as said below
- prefix_cache: bfloat16 [131072, 256], P(('groups', 'replica')), may hold values from -18 to 18
- owners: int32 [2], P('groups'), may hold values from 0 to 31, as said below
- readers: int32 [32], P('groups'), may hold values from 0 to 1
- kv_pool: bfloat16 [1024, 128, 256], P(('groups', 'replica')), may hold values from -6 to 6
- mig_target: int32 [32, 32], P(('groups', 'replica')), may hold values from 0 to 31, as said below
- mig_block: int32 [32, 32], P(('groups', 'replica')), may hold values from 0 to 31, each once within a row
- mig_count: int32 [32], P(('groups', 'replica')), may hold values from 8 to 32, as said below
Outputs:
- attended: bfloat16 [8192, 1024], P(('groups', 'replica'))
The draws below stay inside these ranges and needn't reach their ends.
Inputs may be any that keep to these rules, and one draw needn't show every extreme that they name: `owners`: 2 different replicas; replica 32 - 1 owns one prefix in every draw. `ctx_len`: the largest value is 512 in every draw. `mig_target`: each row names every replica once, so one source sends at most one block to one target; in every draw one replica is the first entry of every row. `mig_block`: each row names every block of the source's pool once. `mig_count`: the largest value is 32 in every draw.
All inputs are finite; a program needn't handle non-finite values.
Results may differ from the reference program's by a relative error of at most 0.0019.
Values may be sent and summed in bfloat16 or wider, within the bound.
No kernel may reach another device: no remote copies, remote signals or barrier semaphores. Data moves between devices by JAX's collectives and lax.ppermute only.
A program may use at most 128 MiB of HBM per device.

```python
import math
import jax
import jax.numpy as jnp
import numpy as np
from jax import lax

HD = 128
HQ = 8
SUF = 256
PL = 4096
CTX = 512
BLK = 128
NP = 2
NB = 32
N_REPLICA = 32


def sign_pattern(key):
    flips = jax.random.bernoulli(jax.random.fold_in(key, 991), 0.5, (HD,))
    return jnp.where(flips, 1.0, -1.0).astype(jnp.float32)


def crossing_pattern(key):
    balanced = jnp.where(jnp.arange(HD) < HD // 2, 1.0, -1.0).astype(jnp.float32)
    mixed = jax.random.permutation(jax.random.fold_in(key, 993), balanced)
    return (sign_pattern(key) * mixed).astype(jnp.float32)


def column_scale():
    return jnp.where(jnp.arange(2 * HD) < HD, 0.6, 1.0).astype(jnp.float32)


def cache_rows(key, salt, shape):
    drawn = jnp.clip(jax.random.normal(jax.random.fold_in(key, salt), shape, jnp.float32), -6.0, 6.0)
    return (drawn * column_scale()).astype(jnp.bfloat16)


def draw_suffix_kv(key, part):
    return cache_rows(key, 41, (N_REPLICA * SUF, 2 * HD))


def draw_own_cache(key, part):
    return cache_rows(key, 43, (N_REPLICA * CTX, 2 * HD))


def draw_kv_pool(key, part):
    return cache_rows(key, 47, (N_REPLICA * NB, BLK, 2 * HD))


def draw_queries(key, part):
    drawn = jnp.clip(4.0 * jax.random.normal(jax.random.fold_in(key, 11), (N_REPLICA, SUF, HQ, HD), jnp.float32), -15.0, 15.0)
    return drawn.reshape(N_REPLICA * SUF, HQ * HD).astype(jnp.bfloat16)


def draw_prefix_cache(key, part):
    drawn = jnp.clip(jax.random.normal(jax.random.fold_in(key, 23), (N_REPLICA, PL, 2 * HD), jnp.float32), -6.0, 6.0)
    drawn = drawn * column_scale()[None, None, :]
    planted = jax.random.randint(jax.random.fold_in(key, 53), (N_REPLICA,), 2, PL).astype(jnp.int32)
    rows = jnp.arange(PL, dtype=jnp.int32)
    columns = jnp.arange(2 * HD, dtype=jnp.int32)
    large_key = jnp.concatenate([18.0 * crossing_pattern(key), jnp.zeros((HD,), jnp.float32)])
    select = (rows[None, :, None] == planted[:, None, None]) & (columns[None, None, :] < HD)
    drawn = jnp.where(select, large_key[None, None, :], drawn)
    return drawn.reshape(N_REPLICA * PL, 2 * HD).astype(jnp.bfloat16)


def draw_owners(key, part):
    others = jax.random.permutation(jax.random.fold_in(key, 31), N_REPLICA - 1)[:NP - 1].astype(jnp.int32)
    listed = jnp.concatenate([others, jnp.full((1,), N_REPLICA - 1, jnp.int32)])
    order = jax.random.permutation(jax.random.fold_in(key, 37), NP)
    return listed[order].astype(jnp.int32)


def draw_ctx_len(key, part):
    lengths = jax.random.randint(jax.random.fold_in(key, 3), (N_REPLICA,), CTX // 8, CTX + 1).astype(jnp.int32)
    picked = jax.random.randint(jax.random.fold_in(key, 4), (), 0, N_REPLICA)
    return lengths.at[picked].set(CTX).astype(jnp.int32)


def draw_mig_target(key, part):
    first = jax.random.randint(jax.random.fold_in(key, 5), (), 0, N_REPLICA)
    columns = jnp.arange(N_REPLICA, dtype=jnp.int32)
    ranking = jax.random.randint(jax.random.fold_in(key, 6), (N_REPLICA, N_REPLICA), 0, 2 ** 20) * N_REPLICA + columns[None, :]
    ranking = jnp.where(columns[None, :] == first, -1, ranking)
    return jnp.argsort(ranking, axis=1, stable=True).astype(jnp.int32)


def draw_mig_count(key, part):
    counts = jax.random.randint(jax.random.fold_in(key, 7), (N_REPLICA,), N_REPLICA // 4, N_REPLICA + 1).astype(jnp.int32)
    picked = jax.random.randint(jax.random.fold_in(key, 8), (), 0, N_REPLICA)
    return counts.at[picked].set(N_REPLICA).astype(jnp.int32)


def plant(values, rng, least, top_value):
    extent = values.shape
    place = [jax.random.randint(jax.random.fold_in(rng, axis), (), 0, extent[axis]) for axis in range(len(extent))]
    values = values.at[tuple(place)].set(least)
    longest = extent.index(max(extent))
    place[longest] = (place[longest] + 1) % extent[longest]
    return values.at[tuple(place)].set(top_value)


def rank_bounds(count, lean):
    weights = [(1 << 20) // math.isqrt(rank ** lean) + 1 for rank in range(1, count + 1)]
    width = 1 + sum(weights) // (1 << 30)
    return np.cumsum(np.array([max(1, weight // width) for weight in weights]))


def ranked(key, extent, count, slope):
    listing = rank_bounds(count, slope)
    lot = jax.random.randint(jax.random.fold_in(key, 1), extent, 0, int(listing[count - 1]))
    standing = jnp.searchsorted(jnp.asarray(listing, jnp.int32), lot, side="right")
    return jax.random.permutation(jax.random.fold_in(key, 2), count)[standing].astype(jnp.int32)


def setup_inputs(seed: int = 0, part: int = 0) -> dict:
    key_list = jax.random.split(jax.random.key(seed), 12)
    part_splits = jax.random.split(jax.random.fold_in(key_list[11], part), 12)
    queries = draw_queries(jax.random.fold_in(jax.random.fold_in(key_list[11], part), 71), part)
    suffix_kv = draw_suffix_kv(jax.random.fold_in(jax.random.fold_in(key_list[11], part), 71), part)
    own_cache = draw_own_cache(jax.random.fold_in(jax.random.fold_in(key_list[11], part), 71), part)
    ctx_len = draw_ctx_len(jax.random.fold_in(jax.random.fold_in(key_list[11], part), 71), part)
    prefix_cache = draw_prefix_cache(jax.random.fold_in(jax.random.fold_in(key_list[11], part), 71), part)
    owners = draw_owners(jax.random.fold_in(jax.random.fold_in(key_list[11], part), 71), part)
    readers = plant(ranked(part_splits[6], (N_REPLICA,), NP, 2), jax.random.fold_in(part_splits[6], 3), 0, NP - 1).astype(jnp.int32)
    kv_pool = draw_kv_pool(jax.random.fold_in(jax.random.fold_in(key_list[11], part), 71), part)
    mig_target = draw_mig_target(jax.random.fold_in(jax.random.fold_in(key_list[11], part), 71), part)
    mig_block = jax.vmap(lambda own: jax.random.permutation(own, NB))(jax.random.split(part_splits[9], N_REPLICA)).reshape((N_REPLICA, NB)).astype(jnp.int32)
    mig_count = draw_mig_count(jax.random.fold_in(jax.random.fold_in(key_list[11], part), 71), part)
    return {"queries": queries, "suffix_kv": suffix_kv, "own_cache": own_cache, "ctx_len": ctx_len, "prefix_cache": prefix_cache, "owners": owners, "readers": readers, "kv_pool": kv_pool, "mig_target": mig_target, "mig_block": mig_block, "mig_count": mig_count}


def reference(queries, suffix_kv, own_cache, ctx_len, prefix_cache, owners, readers, kv_pool, mig_target, mig_block, mig_count):
    prefixes = prefix_cache.reshape(N_REPLICA, PL, 2 * HD)
    pools = kv_pool.reshape(N_REPLICA, NB, BLK, 2 * HD)
    owned = own_cache.reshape(N_REPLICA, CTX, 2 * HD)
    suffixes = suffix_kv.reshape(N_REPLICA, SUF, 2 * HD)
    query_sets = queries.reshape(N_REPLICA, SUF * HQ, HD)
    entries = jnp.arange(N_REPLICA, dtype=jnp.int32)
    source_ids = jnp.arange(N_REPLICA, dtype=jnp.int32)
    entry_live = entries[None, :] < mig_count[:, None]
    row_count = SUF * HQ
    positions = jnp.arange(row_count, dtype=jnp.int32) // HQ
    score_scale = HD ** -0.5

    def attend_replica(replica):
        prefix_rows = prefixes[owners[readers[replica]]]
        matching = (mig_target == replica) & entry_live
        entry_pos = jnp.sum(jnp.where(matching, entries[None, :], 0), axis=1).astype(jnp.int32)
        received = jnp.any(matching, axis=1)
        block_ids = jnp.take_along_axis(mig_block, entry_pos[:, None], axis=1)[:, 0]
        moved = pools[source_ids, block_ids].reshape(N_REPLICA * BLK, 2 * HD)
        moved_mask = jnp.repeat(received, BLK)
        own_rows = owned[replica]
        own_mask = jnp.arange(CTX, dtype=jnp.int32) < ctx_len[replica]
        suffix_rows = suffixes[replica]
        key_values = jnp.concatenate([prefix_rows, moved, own_rows, suffix_rows], axis=0)
        column_mask = jnp.concatenate([jnp.ones((PL,), bool), moved_mask, own_mask, jnp.ones((SUF,), bool)])
        causal = jnp.arange(SUF, dtype=jnp.int32)[None, :] <= positions[:, None]
        allowed = jnp.concatenate([jnp.ones((row_count, PL + N_REPLICA * BLK + CTX), bool), causal], axis=1)
        allowed = allowed & column_mask[None, :]
        scores = lax.dot_general(query_sets[replica], key_values[:, :HD], (((1,), (1,)), ((), ())), preferred_element_type=jnp.float32) * score_scale
        scores = jnp.where(allowed, scores, -jnp.inf)
        row_max = jnp.max(scores, axis=1, keepdims=True)
        exponent = jnp.exp(scores - row_max)
        denominator = jnp.sum(exponent, axis=1, keepdims=True)
        numerator = jnp.dot(exponent.astype(jnp.bfloat16), key_values[:, HD:], preferred_element_type=jnp.float32)
        return (numerator / denominator).astype(jnp.bfloat16).reshape(SUF, HQ * HD)

    attended = lax.map(attend_replica, jnp.arange(N_REPLICA, dtype=jnp.int32))
    return attended.reshape(N_REPLICA * SUF, HQ * HD)
```

```python
import functools

import jax
import jax.numpy as jnp
from jax import lax
from jax.experimental import pallas as pl
from jax.experimental.pallas import tpu as pltpu
from jax.sharding import PartitionSpec as P

LOG2E = 1.4426950408889634
DEAD_MARK = 1024.0
DEAD_ABOVE = 512.0
NEG = -1e30
VMEM_BYTES = 40 * 1024 * 1024


def fold_keys(q_ref, m_ref, acc_ref, keys, values, factor, mask=None):
    heads, tokens, width = acc_ref.shape
    size = keys.shape[1]
    for head in range(heads):
        rows = q_ref[:, head * size:(head + 1) * size]
        scores = lax.dot_general(
            rows, keys, (((1,), (1,)), ((), ())), preferred_element_type=jnp.float32
        )
        if mask is not None:
            scores = jnp.where(mask, scores, NEG)
        old_max = m_ref[head]
        new_max = jnp.maximum(old_max, jnp.max(scores, axis=1, keepdims=True))
        shrink = jnp.exp2((old_max - new_max) * factor)
        weights = jnp.exp2((scores - jnp.tile(new_max, (1, keys.shape[0] // size))) * factor)
        m_ref[head] = new_max
        acc_ref[head] = acc_ref[head] * jnp.tile(shrink, (1, width // size)) + jnp.dot(
            weights.astype(jnp.bfloat16), values, preferred_element_type=jnp.float32
        )


def finish(acc_ref, out_ref):
    heads, tokens, width = acc_ref.shape
    size = width // 2
    for head in range(heads):
        out_ref[:, head * size:(head + 1) * size] = (
            acc_ref[head, :, :size] / acc_ref[head, :, size:]
        ).astype(out_ref.dtype)


def local_kernel(factor, len_ref, q_ref, suffix_ref, own_ref, m_ref, acc_ref, values_ref):
    size = q_ref.shape[1] // acc_ref.shape[0]
    suffix = suffix_ref.shape[0]
    own = own_ref.shape[0]
    m_ref[...] = jnp.full(m_ref.shape, NEG, jnp.float32)
    acc_ref[...] = jnp.zeros(acc_ref.shape, jnp.float32)
    values_ref[:suffix, :size] = suffix_ref[:, size:]
    values_ref[:suffix, size:] = jnp.ones((suffix, size), jnp.bfloat16)
    causal = lax.broadcasted_iota(jnp.int32, (suffix, suffix), 1) <= lax.broadcasted_iota(
        jnp.int32, (suffix, suffix), 0
    )
    fold_keys(
        q_ref, m_ref, acc_ref, suffix_ref[:, :size], values_ref[:suffix, :], factor, causal
    )
    live = lax.broadcasted_iota(jnp.int32, (own, size), 0) < len_ref[0]
    zeros = jnp.zeros((own, size), jnp.float32)
    spare = jnp.broadcast_to(suffix_ref[:1, :size].astype(jnp.float32), (own, size))
    keys = jnp.where(live, own_ref[:, :size].astype(jnp.float32), spare).astype(jnp.bfloat16)
    values_ref[:own, :size] = jnp.where(
        live, own_ref[:, size:].astype(jnp.float32), zeros
    ).astype(jnp.bfloat16)
    values_ref[:own, size:] = jnp.where(live, 1.0, zeros).astype(jnp.bfloat16)
    fold_keys(q_ref, m_ref, acc_ref, keys, values_ref[:own, :], factor)


def prefix_kernel(factor, which_ref, q_ref, kv_ref, m_in, acc_in, m_ref, acc_ref, values_ref):
    size = q_ref.shape[1] // acc_ref.shape[0]

    @pl.when(pl.program_id(0) == 0)
    def _():
        m_ref[...] = m_in[...]
        acc_ref[...] = acc_in[...]

    values_ref[:, :size] = kv_ref[:, size:]
    values_ref[:, size:] = jnp.ones((kv_ref.shape[0], size), jnp.bfloat16)
    fold_keys(q_ref, m_ref, acc_ref, kv_ref[:, :size], values_ref[...], factor)


def moved_kernel(
    factor, q_ref, kv_ref, suffix_ref, m_in, acc_in, out_ref, m_ref, acc_ref, keys_ref, values_ref
):
    size = q_ref.shape[1] // acc_ref.shape[0]

    @pl.when(pl.program_id(0) == 0)
    def _():
        m_ref[...] = m_in[...]
        acc_ref[...] = acc_in[...]

    rows = kv_ref[...].reshape(-1, kv_ref.shape[-1]).astype(jnp.float32)
    live = jnp.broadcast_to(rows[:, size:size + 1] < DEAD_ABOVE, (rows.shape[0], size))
    zeros = jnp.zeros((rows.shape[0], size), jnp.float32)
    spare = jnp.broadcast_to(suffix_ref[:1, :size].astype(jnp.float32), zeros.shape)
    keys_ref[...] = jnp.where(live, rows[:, :size], spare).astype(jnp.bfloat16)
    values_ref[:, :size] = jnp.where(live, rows[:, size:], zeros).astype(jnp.bfloat16)
    values_ref[:, size:] = jnp.where(live, 1.0, zeros).astype(jnp.bfloat16)
    fold_keys(q_ref, m_ref, acc_ref, keys_ref[...], values_ref[...], factor)

    @pl.when(pl.program_id(0) == pl.num_programs(0) - 1)
    def _():
        finish(acc_ref, out_ref)


def whole(shape):
    return pl.BlockSpec(shape, lambda *args: (0,) * len(shape))


def cost(rows, keys, size):
    return pl.CostEstimate(
        flops=6 * rows * keys * size, bytes_accessed=4 * keys * size, transcendentals=rows * keys
    )


def on_device(
    queries,
    suffix_kv,
    own_cache,
    ctx_len,
    prefix_cache,
    owners,
    readers,
    kv_pool,
    mig_target,
    mig_block,
    mig_count,
):
    replicas = lax.axis_size("replica")
    me = lax.axis_index("replica")
    size = suffix_kv.shape[1] // 2
    tokens = queries.shape[0]
    heads = queries.shape[1] // size
    prefixes = owners.shape[0]
    factor = size ** (-0.5) * LOG2E
    row_count = tokens * heads
    state = (
        jax.ShapeDtypeStruct((heads, tokens, size), jnp.float32),
        jax.ShapeDtypeStruct((heads, tokens, 2 * size), jnp.float32),
    )
    state_specs = (whole(state[0].shape), whole(state[1].shape))
    params = pltpu.CompilerParams(vmem_limit_bytes=VMEM_BYTES)

    targets = mig_target[0]
    entry_live = jnp.arange(targets.shape[0], dtype=jnp.int32) < mig_count[0]
    matching = (targets[None, :] == jnp.arange(replicas, dtype=jnp.int32)[:, None]) & entry_live[
        None, :
    ]
    slot_ids = jnp.sum(jnp.where(matching, mig_block[0][None, :], 0), axis=1)
    slot_live = jnp.any(matching, axis=1)
    outgoing = jnp.where(
        slot_live[:, None, None], kv_pool[slot_ids], jnp.asarray(DEAD_MARK, kv_pool.dtype)
    )
    arrived = lax.all_to_all(outgoing, "replica", split_axis=0, concat_axis=0, tiled=True)

    offered = jnp.where(
        (owners == me)[:, None, None], prefix_cache[None], jnp.zeros((), prefix_cache.dtype)
    )
    shared = lax.psum(offered, "replica")

    state_now = pl.pallas_call(
        functools.partial(local_kernel, factor),
        out_shape=state,
        in_specs=[
            pl.BlockSpec(memory_space=pltpu.SMEM),
            whole(queries.shape),
            whole(suffix_kv.shape),
            whole(own_cache.shape),
        ],
        out_specs=state_specs,
        grid=(1,),
        scratch_shapes=[
            pltpu.VMEM((max(tokens, own_cache.shape[0]), 2 * size), jnp.bfloat16)
        ],
        compiler_params=params,
        cost_estimate=cost(row_count, tokens + own_cache.shape[0], size),
        name="local_keys",
    )(ctx_len, queries, suffix_kv, own_cache)

    rows = min(1024, shared.shape[1])
    state_now = pl.pallas_call(
        functools.partial(prefix_kernel, factor),
        out_shape=state,
        grid_spec=pltpu.PrefetchScalarGridSpec(
            num_scalar_prefetch=1,
            grid=(shared.shape[1] // rows,),
            in_specs=[
                whole(queries.shape),
                pl.BlockSpec((None, rows, 2 * size), lambda i, which: (which[0], i, 0)),
                *state_specs,
            ],
            out_specs=state_specs,
            scratch_shapes=[pltpu.VMEM((rows, 2 * size), jnp.bfloat16)],
        ),
        compiler_params=params,
        cost_estimate=cost(row_count, shared.shape[1], size),
        name="prefix_keys",
    )(readers[me][None], queries, shared, *state_now)

    rows = arrived.shape[1]
    group = max(1, 1024 // rows)
    return pl.pallas_call(
        functools.partial(moved_kernel, factor),
        out_shape=jax.ShapeDtypeStruct(queries.shape, queries.dtype),
        grid=(replicas // group,),
        in_specs=[
            whole(queries.shape),
            pl.BlockSpec((group, rows, 2 * size), lambda i: (i, 0, 0)),
            whole(suffix_kv.shape),
            *state_specs,
        ],
        out_specs=whole(queries.shape),
        scratch_shapes=[
            pltpu.VMEM(state[0].shape, jnp.float32),
            pltpu.VMEM(state[1].shape, jnp.float32),
            pltpu.VMEM((group * rows, size), jnp.bfloat16),
            pltpu.VMEM((group * rows, 2 * size), jnp.bfloat16),
        ],
        compiler_params=params,
        cost_estimate=cost(row_count, replicas * rows, size),
        name="moved_keys",
    )(queries, arrived, suffix_kv, *state_now)


def solution(mesh):
    in_specs = (
        P(("groups", "replica"), None),
        P(("groups", "replica"), None),
        P(("groups", "replica"), None),
        P(("groups", "replica")),
        P(("groups", "replica"), None),
        P("groups"),
        P("groups"),
        P(("groups", "replica"), None, None),
        P(("groups", "replica"), None),
        P(("groups", "replica"), None),
        P(("groups", "replica")),
    )
    out_specs = P(("groups", "replica"), None)
    return jax.shard_map(
        on_device, mesh=mesh, in_specs=in_specs, out_specs=out_specs, check_vma=False
    )
```

```python
import functools

import jax
import jax.numpy as jnp
from jax import lax
from jax.experimental import pallas as pl
from jax.experimental.pallas import tpu as pltpu
from jax.sharding import PartitionSpec as P

LOG2E = 1.4426950408889634
DEAD_MARK = 1024.0
DEAD_ABOVE = 512.0
NEG = -1e30
VMEM_BYTES = 40 * 1024 * 1024


def fold_keys(q_ref, m_ref, acc_ref, keys, values, factor, mask=None):
    heads, tokens, width = acc_ref.shape
    size = keys.shape[1]
    for head in range(heads):
        rows = q_ref[:, head * size:(head + 1) * size]
        scores = lax.dot_general(
            rows, keys, (((1,), (1,)), ((), ())), preferred_element_type=jnp.float32
        )
        if mask is not None:
            scores = jnp.where(mask, scores, NEG)
        old_max = m_ref[head]
        new_max = jnp.maximum(old_max, jnp.max(scores, axis=1, keepdims=True))
        shrink = jnp.exp2((old_max - new_max) * factor)
        weights = jnp.exp2((scores - jnp.tile(new_max, (1, keys.shape[0] // size))) * factor)
        m_ref[head] = new_max
        acc_ref[head] = acc_ref[head] * jnp.tile(shrink, (1, width // size)) + jnp.dot(
            weights.astype(jnp.bfloat16), values, preferred_element_type=jnp.float32
        )


def finish(acc_ref, out_ref):
    heads, tokens, width = acc_ref.shape
    size = width // 2
    for head in range(heads):
        out_ref[:, head * size:(head + 1) * size] = (
            acc_ref[head, :, :size] / acc_ref[head, :, size:]
        ).astype(out_ref.dtype)


def local_kernel(factor, len_ref, q_ref, suffix_ref, own_ref, m_ref, acc_ref, values_ref):
    size = q_ref.shape[1] // acc_ref.shape[0]
    suffix = suffix_ref.shape[0]
    own = own_ref.shape[0]
    m_ref[...] = jnp.full(m_ref.shape, NEG, jnp.float32)
    acc_ref[...] = jnp.zeros(acc_ref.shape, jnp.float32)
    values_ref[:suffix, :size] = suffix_ref[:, size:]
    values_ref[:suffix, size:] = jnp.ones((suffix, size), jnp.bfloat16)
    causal = lax.broadcasted_iota(jnp.int32, (suffix, suffix), 1) <= lax.broadcasted_iota(
        jnp.int32, (suffix, suffix), 0
    )
    fold_keys(
        q_ref, m_ref, acc_ref, suffix_ref[:, :size], values_ref[:suffix, :], factor, causal
    )
    live = lax.broadcasted_iota(jnp.int32, (own, size), 0) < len_ref[0]
    zeros = jnp.zeros((own, size), jnp.float32)
    spare = jnp.broadcast_to(suffix_ref[:1, :size].astype(jnp.float32), (own, size))
    keys = jnp.where(live, own_ref[:, :size].astype(jnp.float32), spare).astype(jnp.bfloat16)
    values_ref[:own, :size] = jnp.where(
        live, own_ref[:, size:].astype(jnp.float32), zeros
    ).astype(jnp.bfloat16)
    values_ref[:own, size:] = jnp.where(live, 1.0, zeros).astype(jnp.bfloat16)
    fold_keys(q_ref, m_ref, acc_ref, keys, values_ref[:own, :], factor)


def prefix_kernel(factor, q_ref, kv_ref, m_in, acc_in, m_ref, acc_ref, values_ref):
    size = q_ref.shape[1] // acc_ref.shape[0]

    @pl.when(pl.program_id(0) == 0)
    def _():
        m_ref[...] = m_in[...]
        acc_ref[...] = acc_in[...]

    values_ref[:, :size] = kv_ref[:, size:]
    values_ref[:, size:] = jnp.ones((kv_ref.shape[0], size), jnp.bfloat16)
    fold_keys(q_ref, m_ref, acc_ref, kv_ref[:, :size], values_ref[...], factor)


def moved_kernel(
    factor, q_ref, kv_ref, suffix_ref, m_in, acc_in, out_ref, m_ref, acc_ref, keys_ref, values_ref
):
    size = q_ref.shape[1] // acc_ref.shape[0]

    @pl.when(pl.program_id(0) == 0)
    def _():
        m_ref[...] = m_in[...]
        acc_ref[...] = acc_in[...]

    rows = kv_ref[...].reshape(-1, kv_ref.shape[-1]).astype(jnp.float32)
    live = jnp.broadcast_to(rows[:, size:size + 1] < DEAD_ABOVE, (rows.shape[0], size))
    zeros = jnp.zeros((rows.shape[0], size), jnp.float32)
    spare = jnp.broadcast_to(suffix_ref[:1, :size].astype(jnp.float32), zeros.shape)
    keys_ref[...] = jnp.where(live, rows[:, :size], spare).astype(jnp.bfloat16)
    values_ref[:, :size] = jnp.where(live, rows[:, size:], zeros).astype(jnp.bfloat16)
    values_ref[:, size:] = jnp.where(live, 1.0, zeros).astype(jnp.bfloat16)
    fold_keys(q_ref, m_ref, acc_ref, keys_ref[...], values_ref[...], factor)

    @pl.when(pl.program_id(0) == pl.num_programs(0) - 1)
    def _():
        finish(acc_ref, out_ref)


def whole(shape):
    return pl.BlockSpec(shape, lambda *args: (0,) * len(shape))


def cost(rows, keys, size):
    return pl.CostEstimate(
        flops=6 * rows * keys * size, bytes_accessed=4 * keys * size, transcendentals=rows * keys
    )


def multicast(prefix_cache, owners, readers):
    replicas = lax.axis_size("replica")
    me = lax.axis_index("replica")
    half = replicas // 2
    mine = me // half
    halves = [list(range(half)), list(range(half, replicas))]
    exchange = functools.partial(
        lax.all_to_all,
        axis_name="replica",
        split_axis=0,
        concat_axis=0,
        axis_index_groups=halves,
        tiled=True,
    )
    pieces = prefix_cache.reshape(half, -1, prefix_cache.shape[1])
    found = exchange(pieces)[owners % half]
    passed = lax.ppermute(found, "replica", [(i, (i + half) % replicas) for i in range(replicas)])
    held = jnp.where((owners // half == mine)[:, None, None], found, passed)
    wanted = lax.dynamic_slice_in_dim(readers, mine * half, half)
    return exchange(held[wanted]).reshape(prefix_cache.shape)


def on_device(
    queries,
    suffix_kv,
    own_cache,
    ctx_len,
    prefix_cache,
    owners,
    readers,
    kv_pool,
    mig_target,
    mig_block,
    mig_count,
):
    replicas = lax.axis_size("replica")
    size = suffix_kv.shape[1] // 2
    tokens = queries.shape[0]
    heads = queries.shape[1] // size
    factor = size ** (-0.5) * LOG2E
    row_count = tokens * heads
    state = (
        jax.ShapeDtypeStruct((heads, tokens, size), jnp.float32),
        jax.ShapeDtypeStruct((heads, tokens, 2 * size), jnp.float32),
    )
    state_specs = (whole(state[0].shape), whole(state[1].shape))
    params = pltpu.CompilerParams(vmem_limit_bytes=VMEM_BYTES)

    targets = mig_target[0]
    entry_live = jnp.arange(targets.shape[0], dtype=jnp.int32) < mig_count[0]
    matching = (targets[None, :] == jnp.arange(replicas, dtype=jnp.int32)[:, None]) & entry_live[
        None, :
    ]
    slot_ids = jnp.sum(jnp.where(matching, mig_block[0][None, :], 0), axis=1)
    slot_live = jnp.any(matching, axis=1)
    outgoing = jnp.where(
        slot_live[:, None, None], kv_pool[slot_ids], jnp.asarray(DEAD_MARK, kv_pool.dtype)
    )
    arrived = lax.all_to_all(outgoing, "replica", split_axis=0, concat_axis=0, tiled=True)

    shared = multicast(prefix_cache, owners, readers)

    state_now = pl.pallas_call(
        functools.partial(local_kernel, factor),
        out_shape=state,
        in_specs=[
            pl.BlockSpec(memory_space=pltpu.SMEM),
            whole(queries.shape),
            whole(suffix_kv.shape),
            whole(own_cache.shape),
        ],
        out_specs=state_specs,
        grid=(1,),
        scratch_shapes=[
            pltpu.VMEM((max(tokens, own_cache.shape[0]), 2 * size), jnp.bfloat16)
        ],
        compiler_params=params,
        cost_estimate=cost(row_count, tokens + own_cache.shape[0], size),
        name="local_keys",
    )(ctx_len, queries, suffix_kv, own_cache)

    rows = min(1024, shared.shape[0])
    state_now = pl.pallas_call(
        functools.partial(prefix_kernel, factor),
        out_shape=state,
        grid=(shared.shape[0] // rows,),
        in_specs=[
            whole(queries.shape),
            pl.BlockSpec((rows, 2 * size), lambda i: (i, 0)),
            *state_specs,
        ],
        out_specs=state_specs,
        scratch_shapes=[pltpu.VMEM((rows, 2 * size), jnp.bfloat16)],
        compiler_params=params,
        cost_estimate=cost(row_count, shared.shape[0], size),
        name="prefix_keys",
    )(queries, shared, *state_now)

    rows = arrived.shape[1]
    group = max(1, 1024 // rows)
    return pl.pallas_call(
        functools.partial(moved_kernel, factor),
        out_shape=jax.ShapeDtypeStruct(queries.shape, queries.dtype),
        grid=(replicas // group,),
        in_specs=[
            whole(queries.shape),
            pl.BlockSpec((group, rows, 2 * size), lambda i: (i, 0, 0)),
            whole(suffix_kv.shape),
            *state_specs,
        ],
        out_specs=whole(queries.shape),
        scratch_shapes=[
            pltpu.VMEM(state[0].shape, jnp.float32),
            pltpu.VMEM(state[1].shape, jnp.float32),
            pltpu.VMEM((group * rows, size), jnp.bfloat16),
            pltpu.VMEM((group * rows, 2 * size), jnp.bfloat16),
        ],
        compiler_params=params,
        cost_estimate=cost(row_count, replicas * rows, size),
        name="moved_keys",
    )(queries, arrived, suffix_kv, *state_now)


def solution(mesh):
    in_specs = (
        P(("groups", "replica"), None),
        P(("groups", "replica"), None),
        P(("groups", "replica"), None),
        P(("groups", "replica")),
        P(("groups", "replica"), None),
        P("groups"),
        P("groups"),
        P(("groups", "replica"), None, None),
        P(("groups", "replica"), None),
        P(("groups", "replica"), None),
        P(("groups", "replica")),
    )
    out_specs = P(("groups", "replica"), None)
    return jax.shard_map(
        on_device, mesh=mesh, in_specs=in_specs, out_specs=out_specs, check_vma=False
    )
```

```python
import functools

import jax
import jax.numpy as jnp
from jax import lax
from jax.experimental import pallas as pl
from jax.experimental.pallas import tpu as pltpu
from jax.sharding import PartitionSpec as P

LOG2E = 1.4426950408889634
DEAD_MARK = 1024.0
DEAD_ABOVE = 512.0
NEG = -1e30
VMEM_BYTES = 40 * 1024 * 1024


def fold_keys(q_ref, m_ref, acc_ref, keys, values, factor, mask=None):
    heads, tokens, width = acc_ref.shape
    size = keys.shape[1]
    for head in range(heads):
        rows = q_ref[:, head * size:(head + 1) * size]
        scores = lax.dot_general(
            rows, keys, (((1,), (1,)), ((), ())), preferred_element_type=jnp.float32
        )
        if mask is not None:
            scores = jnp.where(mask, scores, NEG)
        old_max = m_ref[head]
        new_max = jnp.maximum(old_max, jnp.max(scores, axis=1, keepdims=True))
        shrink = jnp.exp2((old_max - new_max) * factor)
        weights = jnp.exp2((scores - jnp.tile(new_max, (1, keys.shape[0] // size))) * factor)
        m_ref[head] = new_max
        acc_ref[head] = acc_ref[head] * jnp.tile(shrink, (1, width // size)) + jnp.dot(
            weights.astype(jnp.bfloat16), values, preferred_element_type=jnp.float32
        )


def finish(acc_ref, out_ref):
    heads, tokens, width = acc_ref.shape
    size = width // 2
    for head in range(heads):
        out_ref[:, head * size:(head + 1) * size] = (
            acc_ref[head, :, :size] / acc_ref[head, :, size:]
        ).astype(out_ref.dtype)


def local_kernel(factor, len_ref, q_ref, suffix_ref, own_ref, m_ref, acc_ref, values_ref):
    size = q_ref.shape[1] // acc_ref.shape[0]
    suffix = suffix_ref.shape[0]
    own = own_ref.shape[0]
    m_ref[...] = jnp.full(m_ref.shape, NEG, jnp.float32)
    acc_ref[...] = jnp.zeros(acc_ref.shape, jnp.float32)
    values_ref[:suffix, :size] = suffix_ref[:, size:]
    values_ref[:suffix, size:] = jnp.ones((suffix, size), jnp.bfloat16)
    causal = lax.broadcasted_iota(jnp.int32, (suffix, suffix), 1) <= lax.broadcasted_iota(
        jnp.int32, (suffix, suffix), 0
    )
    fold_keys(
        q_ref, m_ref, acc_ref, suffix_ref[:, :size], values_ref[:suffix, :], factor, causal
    )
    live = lax.broadcasted_iota(jnp.int32, (own, size), 0) < len_ref[0]
    zeros = jnp.zeros((own, size), jnp.float32)
    spare = jnp.broadcast_to(suffix_ref[:1, :size].astype(jnp.float32), (own, size))
    keys = jnp.where(live, own_ref[:, :size].astype(jnp.float32), spare).astype(jnp.bfloat16)
    values_ref[:own, :size] = jnp.where(
        live, own_ref[:, size:].astype(jnp.float32), zeros
    ).astype(jnp.bfloat16)
    values_ref[:own, size:] = jnp.where(live, 1.0, zeros).astype(jnp.bfloat16)
    fold_keys(q_ref, m_ref, acc_ref, keys, values_ref[:own, :], factor)


def prefix_kernel(factor, q_ref, kv_ref, m_in, acc_in, m_ref, acc_ref, values_ref):
    size = q_ref.shape[1] // acc_ref.shape[0]

    @pl.when(pl.program_id(0) == 0)
    def _():
        m_ref[...] = m_in[...]
        acc_ref[...] = acc_in[...]

    values_ref[:, :size] = kv_ref[:, size:]
    values_ref[:, size:] = jnp.ones((kv_ref.shape[0], size), jnp.bfloat16)
    fold_keys(q_ref, m_ref, acc_ref, kv_ref[:, :size], values_ref[...], factor)


def moved_kernel(
    factor, q_ref, kv_ref, suffix_ref, m_in, acc_in, out_ref, m_ref, acc_ref, keys_ref, values_ref
):
    size = q_ref.shape[1] // acc_ref.shape[0]

    @pl.when(pl.program_id(0) == 0)
    def _():
        m_ref[...] = m_in[...]
        acc_ref[...] = acc_in[...]

    rows = kv_ref[...].reshape(-1, kv_ref.shape[-1]).astype(jnp.float32)
    live = jnp.broadcast_to(rows[:, size:size + 1] < DEAD_ABOVE, (rows.shape[0], size))
    zeros = jnp.zeros((rows.shape[0], size), jnp.float32)
    spare = jnp.broadcast_to(suffix_ref[:1, :size].astype(jnp.float32), zeros.shape)
    keys_ref[...] = jnp.where(live, rows[:, :size], spare).astype(jnp.bfloat16)
    values_ref[:, :size] = jnp.where(live, rows[:, size:], zeros).astype(jnp.bfloat16)
    values_ref[:, size:] = jnp.where(live, 1.0, zeros).astype(jnp.bfloat16)
    fold_keys(q_ref, m_ref, acc_ref, keys_ref[...], values_ref[...], factor)

    @pl.when(pl.program_id(0) == pl.num_programs(0) - 1)
    def _():
        finish(acc_ref, out_ref)


def whole(shape):
    return pl.BlockSpec(shape, lambda *args: (0,) * len(shape))


def cost(rows, keys, size):
    return pl.CostEstimate(
        flops=6 * rows * keys * size, bytes_accessed=4 * keys * size, transcendentals=rows * keys
    )


def multicast(prefix_cache, owners, readers):
    replicas = lax.axis_size("replica")
    me = lax.axis_index("replica")
    half = replicas // 2
    chips = half // 2
    core = me % 2
    chip = me // 2 % chips
    side = me // half
    width = prefix_cache.shape[1]

    def swap_cores(rows):
        return lax.ppermute(rows, "replica", [(i, i ^ 1) for i in range(replicas)])

    def to_peer(rows, step):
        return lax.ppermute(rows, "replica", [(i, i ^ (2 * step)) for i in range(replicas)])

    split = prefix_cache.reshape(2, chips, -1, width)
    kept = lax.dynamic_index_in_dim(split, core, 0, keepdims=False)
    swapped = swap_cores(lax.dynamic_index_in_dim(split, 1 - core, 0, keepdims=False))
    gathered = []
    for prefix in range(owners.shape[0]):
        owner = owners[prefix]
        own_core = owner % 2 == core
        held = None
        for step in range(chips):
            there = chip ^ step
            rows = jnp.where(
                own_core,
                lax.dynamic_index_in_dim(kept, there, 0, keepdims=False),
                lax.dynamic_index_in_dim(swapped, there, 0, keepdims=False),
            )
            if step:
                rows = to_peer(rows, step)
            held = rows if held is None else jnp.where(owner // 2 % chips == there, rows, held)
        passed = lax.ppermute(
            held, "replica", [(i, (i + half) % replicas) for i in range(replicas)]
        )
        held = jnp.where(owner // half == side, held, passed)
        gathered.append([held] + [to_peer(held, step) for step in range(1, chips)])

    def pick(wanted):
        picked = []
        for step in range(chips):
            rows = gathered[0][step]
            for prefix in range(1, owners.shape[0]):
                rows = jnp.where(wanted == prefix, gathered[prefix][step], rows)
            picked.append(rows)
        return jnp.concatenate(picked)

    return pick(readers[me]), swap_cores(pick(readers[me ^ 1]))


def on_device(
    queries,
    suffix_kv,
    own_cache,
    ctx_len,
    prefix_cache,
    owners,
    readers,
    kv_pool,
    mig_target,
    mig_block,
    mig_count,
):
    replicas = lax.axis_size("replica")
    size = suffix_kv.shape[1] // 2
    tokens = queries.shape[0]
    heads = queries.shape[1] // size
    factor = size ** (-0.5) * LOG2E
    row_count = tokens * heads
    state = (
        jax.ShapeDtypeStruct((heads, tokens, size), jnp.float32),
        jax.ShapeDtypeStruct((heads, tokens, 2 * size), jnp.float32),
    )
    state_specs = (whole(state[0].shape), whole(state[1].shape))
    params = pltpu.CompilerParams(vmem_limit_bytes=VMEM_BYTES)

    targets = mig_target[0]
    entry_live = jnp.arange(targets.shape[0], dtype=jnp.int32) < mig_count[0]
    matching = (targets[None, :] == jnp.arange(replicas, dtype=jnp.int32)[:, None]) & entry_live[
        None, :
    ]
    slot_ids = jnp.sum(jnp.where(matching, mig_block[0][None, :], 0), axis=1)
    slot_live = jnp.any(matching, axis=1)
    outgoing = jnp.where(
        slot_live[:, None, None], kv_pool[slot_ids], jnp.asarray(DEAD_MARK, kv_pool.dtype)
    )
    arrived = lax.all_to_all(outgoing, "replica", split_axis=0, concat_axis=0, tiled=True)

    shared = multicast(prefix_cache, owners, readers)

    state_now = pl.pallas_call(
        functools.partial(local_kernel, factor),
        out_shape=state,
        in_specs=[
            pl.BlockSpec(memory_space=pltpu.SMEM),
            whole(queries.shape),
            whole(suffix_kv.shape),
            whole(own_cache.shape),
        ],
        out_specs=state_specs,
        grid=(1,),
        scratch_shapes=[
            pltpu.VMEM((max(tokens, own_cache.shape[0]), 2 * size), jnp.bfloat16)
        ],
        compiler_params=params,
        cost_estimate=cost(row_count, tokens + own_cache.shape[0], size),
        name="local_keys",
    )(ctx_len, queries, suffix_kv, own_cache)

    for part in shared:
        rows = min(1024, part.shape[0])
        state_now = pl.pallas_call(
            functools.partial(prefix_kernel, factor),
            out_shape=state,
            grid=(part.shape[0] // rows,),
            in_specs=[
                whole(queries.shape),
                pl.BlockSpec((rows, 2 * size), lambda i: (i, 0)),
                *state_specs,
            ],
            out_specs=state_specs,
            scratch_shapes=[pltpu.VMEM((rows, 2 * size), jnp.bfloat16)],
            compiler_params=params,
            cost_estimate=cost(row_count, part.shape[0], size),
            name="prefix_keys",
        )(queries, part, *state_now)

    rows = arrived.shape[1]
    group = max(1, 1024 // rows)
    return pl.pallas_call(
        functools.partial(moved_kernel, factor),
        out_shape=jax.ShapeDtypeStruct(queries.shape, queries.dtype),
        grid=(replicas // group,),
        in_specs=[
            whole(queries.shape),
            pl.BlockSpec((group, rows, 2 * size), lambda i: (i, 0, 0)),
            whole(suffix_kv.shape),
            *state_specs,
        ],
        out_specs=whole(queries.shape),
        scratch_shapes=[
            pltpu.VMEM(state[0].shape, jnp.float32),
            pltpu.VMEM(state[1].shape, jnp.float32),
            pltpu.VMEM((group * rows, size), jnp.bfloat16),
            pltpu.VMEM((group * rows, 2 * size), jnp.bfloat16),
        ],
        compiler_params=params,
        cost_estimate=cost(row_count, replicas * rows, size),
        name="moved_keys",
    )(queries, arrived, suffix_kv, *state_now)


def solution(mesh):
    in_specs = (
        P(("groups", "replica"), None),
        P(("groups", "replica"), None),
        P(("groups", "replica"), None),
        P(("groups", "replica")),
        P(("groups", "replica"), None),
        P("groups"),
        P("groups"),
        P(("groups", "replica"), None, None),
        P(("groups", "replica"), None),
        P(("groups", "replica"), None),
        P(("groups", "replica")),
    )
    out_specs = P(("groups", "replica"), None)
    return jax.shard_map(
        on_device, mesh=mesh, in_specs=in_specs, out_specs=out_specs, check_vma=False
    )
```

```python
import functools

import jax
import jax.numpy as jnp
from jax import lax
from jax.experimental import pallas as pl
from jax.experimental.pallas import tpu as pltpu
from jax.sharding import PartitionSpec as P

LOG2E = 1.4426950408889634
DEAD_MARK = 1024.0
DEAD_ABOVE = 512.0
NEG = -1e30
CHUNK = 1024
PARAMS = pltpu.CompilerParams(vmem_limit_bytes=56 * 1024 * 1024)


def fold_keys(q_ref, m_ref, acc_ref, keys, values, factor, mask=None):
    heads, tokens, width = acc_ref.shape
    size = keys.shape[1]
    for head in range(heads):
        rows = q_ref[:, head * size:(head + 1) * size]
        scores = lax.dot_general(
            rows, keys, (((1,), (1,)), ((), ())), preferred_element_type=jnp.float32
        )
        if mask is not None:
            scores = jnp.where(mask, scores, NEG)
        old_max = m_ref[head]
        new_max = jnp.maximum(old_max, jnp.max(scores, axis=1, keepdims=True))
        shrink = jnp.exp2((old_max - new_max) * factor)
        weights = jnp.exp2((scores - jnp.tile(new_max, (1, keys.shape[0] // size))) * factor)
        m_ref[head] = new_max
        acc_ref[head] = acc_ref[head] * jnp.tile(shrink, (1, width // size)) + jnp.dot(
            weights.astype(jnp.bfloat16), values, preferred_element_type=jnp.float32
        )


def load_state(sums_ref, stat_ref, m_ref, acc_ref):
    heads, tokens, size = m_ref.shape
    for head in range(heads):
        acc_ref[head, :, :size] = sums_ref[head]
        acc_ref[head, :, size:] = jnp.broadcast_to(stat_ref[head, :, :1], (tokens, size))
        m_ref[head] = jnp.broadcast_to(stat_ref[head, :, size - 1:], (tokens, size))


def save_state(m_ref, acc_ref, sums_ref, stat_ref):
    heads, tokens, size = m_ref.shape
    left = lax.broadcasted_iota(jnp.int32, (tokens, size), 1) < size // 2
    for head in range(heads):
        sums_ref[head] = acc_ref[head, :, :size]
        stat_ref[head] = jnp.where(left, acc_ref[head, :, size:], m_ref[head])


def finish(acc_ref, out_ref):
    heads, tokens, width = acc_ref.shape
    size = width // 2
    for head in range(heads):
        out_ref[:, head * size:(head + 1) * size] = (
            acc_ref[head, :, :size] / acc_ref[head, :, size:]
        ).astype(out_ref.dtype)


def stage_live(rows, live, suffix_ref, keys_ref, values_ref):
    size = suffix_ref.shape[1] // 2
    zeros = jnp.zeros((rows.shape[0], size), jnp.float32)
    spare = jnp.broadcast_to(suffix_ref[:1, :size].astype(jnp.float32), zeros.shape)
    keys_ref[:rows.shape[0], :] = jnp.where(live, rows[:, :size], spare).astype(jnp.bfloat16)
    values_ref[:rows.shape[0], :size] = jnp.where(live, rows[:, size:], zeros).astype(jnp.bfloat16)
    values_ref[:rows.shape[0], size:] = jnp.where(live, 1.0, zeros).astype(jnp.bfloat16)


def fold_moved(factor, q_ref, kv_ref, suffix_ref, m_ref, acc_ref, keys_ref, values_ref):
    rows = kv_ref[...].reshape(-1, kv_ref.shape[-1]).astype(jnp.float32)
    size = suffix_ref.shape[1] // 2
    live = jnp.broadcast_to(rows[:, size:size + 1] < DEAD_ABOVE, (rows.shape[0], size))
    stage_live(rows, live, suffix_ref, keys_ref, values_ref)
    fold_keys(
        q_ref, m_ref, acc_ref, keys_ref[:rows.shape[0], :], values_ref[:rows.shape[0], :], factor
    )


def first_kernel(
    factor, len_ref, q_ref, suffix_ref, own_ref, kv_ref, sums_ref, stat_ref, m_ref, acc_ref,
    keys_ref, values_ref
):
    size = suffix_ref.shape[1] // 2
    suffix = suffix_ref.shape[0]
    own = own_ref.shape[0]

    @pl.when(pl.program_id(0) == 0)
    def _():
        m_ref[...] = jnp.full(m_ref.shape, NEG, jnp.float32)
        acc_ref[...] = jnp.zeros(acc_ref.shape, jnp.float32)
        values_ref[:suffix, :size] = suffix_ref[:, size:]
        values_ref[:suffix, size:] = jnp.ones((suffix, size), jnp.bfloat16)
        causal = lax.broadcasted_iota(jnp.int32, (suffix, suffix), 1) <= lax.broadcasted_iota(
            jnp.int32, (suffix, suffix), 0
        )
        fold_keys(
            q_ref, m_ref, acc_ref, suffix_ref[:, :size], values_ref[:suffix, :], factor, causal
        )
        live = lax.broadcasted_iota(jnp.int32, (own, size), 0) < len_ref[0]
        stage_live(own_ref[...].astype(jnp.float32), live, suffix_ref, keys_ref, values_ref)
        fold_keys(q_ref, m_ref, acc_ref, keys_ref[:own, :], values_ref[:own, :], factor)

    fold_moved(factor, q_ref, kv_ref, suffix_ref, m_ref, acc_ref, keys_ref, values_ref)

    @pl.when(pl.program_id(0) == pl.num_programs(0) - 1)
    def _():
        save_state(m_ref, acc_ref, sums_ref, stat_ref)


def moved_kernel(
    factor, q_ref, suffix_ref, kv_ref, sums_in, stat_in, sums_ref, stat_ref, m_ref, acc_ref,
    keys_ref, values_ref
):
    @pl.when(pl.program_id(0) == 0)
    def _():
        load_state(sums_in, stat_in, m_ref, acc_ref)

    fold_moved(factor, q_ref, kv_ref, suffix_ref, m_ref, acc_ref, keys_ref, values_ref)

    @pl.when(pl.program_id(0) == pl.num_programs(0) - 1)
    def _():
        save_state(m_ref, acc_ref, sums_ref, stat_ref)


def prefix_kernel(factor, last, count, which_ref, q_ref, *refs):
    pieces, refs = refs[:count], refs[count:]
    sums_in, stat_in = refs[:2]
    m_ref, acc_ref, keys_ref, values_ref = refs[-4:]
    size = keys_ref.shape[1]
    load_state(sums_in, stat_in, m_ref, acc_ref)
    for place, piece in enumerate(pieces):
        rows = pl.ds(place * piece.shape[0], piece.shape[0])
        keys_ref[rows, :] = piece[:, :size]
        values_ref[rows, :size] = piece[:, size:]
    values_ref[:, size:] = jnp.ones((values_ref.shape[0], size), jnp.bfloat16)
    chunk = min(CHUNK, keys_ref.shape[0])

    @pl.loop(0, keys_ref.shape[0] // chunk)
    def _(step):
        rows = pl.ds(pl.multiple_of(step * chunk, chunk), chunk)
        fold_keys(q_ref, m_ref, acc_ref, keys_ref[rows, :], values_ref[rows, :], factor)

    if last:
        finish(acc_ref, refs[2])
    else:
        save_state(m_ref, acc_ref, refs[2], refs[3])


def pack_kernel(target_ref, block_ref, count_ref, pool_ref, out_ref, mark_ref, sems):
    entries = target_ref.shape[1]
    mark_ref[...] = jnp.full(mark_ref.shape, DEAD_MARK, mark_ref.dtype)

    @pl.loop(0, entries)
    def _(entry):
        slot = out_ref.at[target_ref[0, entry]]
        live = entry < count_ref[0]

        @pl.when(live)
        def _():
            pltpu.make_async_copy(pool_ref.at[block_ref[0, entry]], slot, sems.at[entry]).start()

        @pl.when(jnp.logical_not(live))
        def _():
            pltpu.make_async_copy(mark_ref, slot, sems.at[entry]).start()

    @pl.loop(0, entries)
    def _(entry):
        pltpu.make_async_copy(mark_ref, out_ref.at[0], sems.at[entry]).wait()


def stage_kernel(owner_ref, place_ref, kept_ref, swapped_ref, *refs):
    pieces, sems = refs[:-1], refs[-1]
    core, chip = place_ref[0], place_ref[1]
    prefixes = owner_ref.shape[0]

    def copies(source, step, prefix):
        return pltpu.make_async_copy(
            source.at[core, chip ^ step], pieces[step].at[prefix], sems.at[step, prefix]
        )

    for step in range(len(pieces)):
        for prefix in range(prefixes):
            here = owner_ref[prefix] % 2 == core

            @pl.when(here)
            def _():
                copies(kept_ref, step, prefix).start()

            @pl.when(jnp.logical_not(here))
            def _():
                copies(swapped_ref, step, prefix).start()

    for step in range(len(pieces)):
        for prefix in range(prefixes):
            copies(kept_ref, step, prefix).wait()


def multicast(prefix_cache, owners, outgoing):
    replicas = lax.axis_size("replica")
    me = lax.axis_index("replica")
    half = replicas // 2
    chips = half // 2
    bits = chips.bit_length() - 1
    chip = me // 2 % chips
    width = prefix_cache.shape[1]

    def swap_cores(rows):
        return lax.ppermute(rows, "replica", [(i, i ^ 1) for i in range(replicas)])

    def to_peer(rows, step):
        return lax.ppermute(rows, "replica", [(i, i ^ (2 * step)) for i in range(replicas)])

    split = prefix_cache.reshape(2, chips, -1, width)
    swapped, outgoing = lax.optimization_barrier((swap_cores(prefix_cache), outgoing))
    swapped = swapped.reshape(split.shape)
    piece = jax.ShapeDtypeStruct((owners.shape[0], split.shape[2], width), split.dtype)
    anywhere = pl.BlockSpec(memory_space=pl.ANY)
    staged = pl.pallas_call(
        stage_kernel,
        out_shape=(piece,) * chips,
        in_specs=[pl.BlockSpec(memory_space=pltpu.SMEM)] * 2 + [anywhere] * 2,
        out_specs=(anywhere,) * chips,
        scratch_shapes=[pltpu.SemaphoreType.DMA((chips, owners.shape[0]))],
        compiler_params=PARAMS,
        name="stage_prefix",
    )(owners, jnp.stack([me % 2, chip]), split, swapped)
    away = chip ^ (owners // 2 % chips)
    found = staged[0]
    for step in range(chips - 1, 0, -1):
        rows = to_peer(staged[step], step)
        found = jnp.where((away == step)[:, None, None], rows, found)
    passed = lax.ppermute(found, "replica", [(i, (i + half) % replicas) for i in range(replicas)])
    held = jnp.where((owners // half == me // half)[:, None, None], found, passed)

    gathered = {0: held}
    for step in sorted(range(1, chips), key=lambda step: (step.bit_count(), step)):
        members = [bit for bit in range(bits) if step >> bit & 1]
        linked = [bit for bit in members if step >> ((bit - 1) % bits) & 1]
        last = 1 << min(linked or members)
        gathered[step] = to_peer(gathered[step ^ last], last)
    ours = [gathered[step] for step in range(chips)]
    return ours, [swap_cores(rows) for rows in ours], outgoing


def whole(shape):
    return pl.BlockSpec(shape, lambda *args: (0,) * len(shape))


def cost(rows, keys, size):
    return pl.CostEstimate(
        flops=6 * rows * keys * size, bytes_accessed=4 * keys * size, transcendentals=rows * keys
    )


def on_device(
    queries,
    suffix_kv,
    own_cache,
    ctx_len,
    prefix_cache,
    owners,
    readers,
    kv_pool,
    mig_target,
    mig_block,
    mig_count,
):
    me = lax.axis_index("replica")
    replicas = lax.axis_size("replica")
    size = suffix_kv.shape[1] // 2
    tokens = queries.shape[0]
    heads = queries.shape[1] // size
    factor = size ** (-0.5) * LOG2E
    row_count = tokens * heads
    state = (jax.ShapeDtypeStruct((heads, tokens, size), jnp.float32),) * 2
    state_specs = (whole(state[0].shape),) * 2
    in_smem = pl.BlockSpec(memory_space=pltpu.SMEM)
    anywhere = pl.BlockSpec(memory_space=pl.ANY)

    def scratch(keys):
        return [
            pltpu.VMEM((heads, tokens, size), jnp.float32),
            pltpu.VMEM((heads, tokens, 2 * size), jnp.float32),
            pltpu.VMEM((keys, size), jnp.bfloat16),
            pltpu.VMEM((keys, 2 * size), jnp.bfloat16),
        ]

    outgoing = pl.pallas_call(
        pack_kernel,
        out_shape=jax.ShapeDtypeStruct((replicas, *kv_pool.shape[1:]), kv_pool.dtype),
        in_specs=[in_smem] * 3 + [anywhere],
        out_specs=anywhere,
        scratch_shapes=[
            pltpu.VMEM(kv_pool.shape[1:], kv_pool.dtype),
            pltpu.SemaphoreType.DMA((mig_target.shape[1],)),
        ],
        compiler_params=PARAMS,
        name="pack_moved",
    )(mig_target, mig_block, mig_count, kv_pool)
    ours, theirs, outgoing = multicast(prefix_cache, owners, outgoing)
    arrived = lax.all_to_all(outgoing, "replica", split_axis=0, concat_axis=0, tiled=True)

    rows = arrived.shape[1]
    group = max(1, CHUNK // rows)
    steps = replicas // group
    first = max(1, steps // 2)
    most = max(group * rows, own_cache.shape[0], tokens)
    state_now = pl.pallas_call(
        functools.partial(first_kernel, factor),
        out_shape=state,
        grid=(first,),
        in_specs=[
            in_smem,
            whole(queries.shape),
            whole(suffix_kv.shape),
            whole(own_cache.shape),
            pl.BlockSpec((group, rows, 2 * size), lambda i: (i, 0, 0)),
        ],
        out_specs=state_specs,
        scratch_shapes=scratch(most),
        compiler_params=PARAMS,
        cost_estimate=cost(row_count, tokens + own_cache.shape[0] + first * group * rows, size),
        name="first_keys",
    )(ctx_len, queries, suffix_kv, own_cache, arrived)
    state_now = pl.pallas_call(
        functools.partial(moved_kernel, factor),
        out_shape=state,
        grid=(steps - first,),
        in_specs=[
            whole(queries.shape),
            whole(suffix_kv.shape),
            pl.BlockSpec((group, rows, 2 * size), lambda i: (i + first, 0, 0)),
            *state_specs,
        ],
        out_specs=state_specs,
        scratch_shapes=scratch(most),
        compiler_params=PARAMS,
        cost_estimate=cost(row_count, (steps - first) * group * rows, size),
        name="moved_keys",
    )(queries, suffix_kv, arrived, *state_now)

    for last, pieces in enumerate((ours, theirs)):
        rows = pieces[0].shape[1]
        state_now = pl.pallas_call(
            functools.partial(prefix_kernel, factor, last, len(pieces)),
            out_shape=jax.ShapeDtypeStruct(queries.shape, queries.dtype) if last else state,
            grid_spec=pltpu.PrefetchScalarGridSpec(
                num_scalar_prefetch=1,
                grid=(1,),
                in_specs=[
                    whole(queries.shape),
                    *[pl.BlockSpec((None, rows, 2 * size), lambda i, which: (which[0], 0, 0))]
                    * len(pieces),
                    *state_specs,
                ],
                out_specs=whole(queries.shape) if last else state_specs,
                scratch_shapes=scratch(len(pieces) * rows),
            ),
            compiler_params=PARAMS,
            cost_estimate=cost(row_count, len(pieces) * rows, size),
            name="prefix_keys",
        )(readers[me][None], queries, *pieces, *state_now)
    return state_now


def solution(mesh):
    in_specs = (
        P(("groups", "replica"), None),
        P(("groups", "replica"), None),
        P(("groups", "replica"), None),
        P(("groups", "replica")),
        P(("groups", "replica"), None),
        P("groups"),
        P("groups"),
        P(("groups", "replica"), None, None),
        P(("groups", "replica"), None),
        P(("groups", "replica"), None),
        P(("groups", "replica")),
    )
    out_specs = P(("groups", "replica"), None)
    return jax.shard_map(
        on_device, mesh=mesh, in_specs=in_specs, out_specs=out_specs, check_vma=False
    )
```

```python
import functools

import jax
import jax.numpy as jnp
from jax import lax
from jax.experimental import pallas as pl
from jax.experimental.pallas import tpu as pltpu
from jax.sharding import PartitionSpec as P

LOG2E = 1.4426950408889634
DEAD_MARK = 1024.0
DEAD_ABOVE = 512.0
NEG = -1e30
CHUNK = 1024
PARAMS = pltpu.CompilerParams(vmem_limit_bytes=40 * 1024 * 1024)


def fold_keys(q_ref, m_ref, acc_ref, keys, values, factor, mask=None):
    heads, tokens, width = acc_ref.shape
    size = keys.shape[1]
    for head in range(heads):
        rows = q_ref[:, head * size:(head + 1) * size]
        scores = lax.dot_general(
            rows, keys, (((1,), (1,)), ((), ())), preferred_element_type=jnp.float32
        )
        if mask is not None:
            scores = jnp.where(mask, scores, NEG)
        old_max = m_ref[head]
        new_max = jnp.maximum(old_max, jnp.max(scores, axis=1, keepdims=True))
        shrink = jnp.exp2((old_max - new_max) * factor)
        weights = jnp.exp2((scores - jnp.tile(new_max, (1, keys.shape[0] // size))) * factor)
        m_ref[head] = new_max
        acc_ref[head] = acc_ref[head] * jnp.tile(shrink, (1, width // size)) + jnp.dot(
            weights.astype(jnp.bfloat16), values, preferred_element_type=jnp.float32
        )


def finish(acc_ref, out_ref):
    heads, tokens, width = acc_ref.shape
    size = width // 2
    for head in range(heads):
        out_ref[:, head * size:(head + 1) * size] = (
            acc_ref[head, :, :size] / acc_ref[head, :, size:]
        ).astype(out_ref.dtype)


def stage_live(rows, live, suffix_ref, keys_ref, values_ref):
    size = suffix_ref.shape[1] // 2
    zeros = jnp.zeros((rows.shape[0], size), jnp.float32)
    spare = jnp.broadcast_to(suffix_ref[:1, :size].astype(jnp.float32), zeros.shape)
    keys_ref[:rows.shape[0], :] = jnp.where(live, rows[:, :size], spare).astype(jnp.bfloat16)
    values_ref[:rows.shape[0], :size] = jnp.where(live, rows[:, size:], zeros).astype(jnp.bfloat16)
    values_ref[:rows.shape[0], size:] = jnp.where(live, 1.0, zeros).astype(jnp.bfloat16)


def fold_moved(factor, q_ref, kv_ref, suffix_ref, m_ref, acc_ref, keys_ref, values_ref):
    rows = kv_ref[...].reshape(-1, kv_ref.shape[-1]).astype(jnp.float32)
    size = suffix_ref.shape[1] // 2
    live = jnp.broadcast_to(rows[:, size:size + 1] < DEAD_ABOVE, (rows.shape[0], size))
    stage_live(rows, live, suffix_ref, keys_ref, values_ref)
    fold_keys(
        q_ref, m_ref, acc_ref, keys_ref[:rows.shape[0], :], values_ref[:rows.shape[0], :], factor
    )


def first_kernel(
    factor, len_ref, q_ref, suffix_ref, own_ref, kv_ref, m_ref, acc_ref, keys_ref, values_ref
):
    size = suffix_ref.shape[1] // 2
    suffix = suffix_ref.shape[0]
    own = own_ref.shape[0]

    @pl.when(pl.program_id(0) == 0)
    def _():
        m_ref[...] = jnp.full(m_ref.shape, NEG, jnp.float32)
        acc_ref[...] = jnp.zeros(acc_ref.shape, jnp.float32)
        values_ref[:suffix, :size] = suffix_ref[:, size:]
        values_ref[:suffix, size:] = jnp.ones((suffix, size), jnp.bfloat16)
        causal = lax.broadcasted_iota(jnp.int32, (suffix, suffix), 1) <= lax.broadcasted_iota(
            jnp.int32, (suffix, suffix), 0
        )
        fold_keys(
            q_ref, m_ref, acc_ref, suffix_ref[:, :size], values_ref[:suffix, :], factor, causal
        )
        live = lax.broadcasted_iota(jnp.int32, (own, size), 0) < len_ref[0]
        stage_live(own_ref[...].astype(jnp.float32), live, suffix_ref, keys_ref, values_ref)
        fold_keys(q_ref, m_ref, acc_ref, keys_ref[:own, :], values_ref[:own, :], factor)

    fold_moved(factor, q_ref, kv_ref, suffix_ref, m_ref, acc_ref, keys_ref, values_ref)


def prefix_kernel(factor, last, count, which_ref, q_ref, *refs):
    pieces, refs = refs[:count], refs[count:]
    m_in, acc_in, out_ref = refs[:3]
    m_ref, acc_ref, keys_ref, values_ref = refs[-4:]
    size = keys_ref.shape[1]
    chunk = min(CHUNK, keys_ref.shape[0])
    step = pl.program_id(0)

    @pl.when(step == 0)
    def _():
        m_ref[...] = m_in[...]
        acc_ref[...] = acc_in[...]
        for place, piece in enumerate(pieces):
            rows = pl.ds(place * piece.shape[0], piece.shape[0])
            keys_ref[rows, :] = piece[:, :size]
            values_ref[rows, :size] = piece[:, size:]
        values_ref[:, size:] = jnp.ones((values_ref.shape[0], size), jnp.bfloat16)

    rows = pl.ds(pl.multiple_of(step * chunk, chunk), chunk)
    fold_keys(q_ref, m_ref, acc_ref, keys_ref[rows, :], values_ref[rows, :], factor)
    if last:

        @pl.when(step == pl.num_programs(0) - 1)
        def _():
            finish(acc_ref, out_ref)


def pack_kernel(target_ref, block_ref, count_ref, pool_ref, out_ref, sems):
    entries = target_ref.shape[1]

    def block(entry):
        return pltpu.make_async_copy(
            pool_ref.at[block_ref[0, entry]], out_ref.at[target_ref[0, entry]], sems.at[entry]
        )

    @pl.loop(0, entries)
    def _(entry):
        live = entry < count_ref[0]

        @pl.when(live)
        def _():
            block(entry).start()

        @pl.when(jnp.logical_not(live))
        def _():
            out_ref[target_ref[0, entry]] = jnp.full(out_ref.shape[1:], DEAD_MARK, out_ref.dtype)

    @pl.loop(0, entries)
    def _(entry):
        @pl.when(entry < count_ref[0])
        def _():
            block(entry).wait()


def stage_kernel(owner_ref, place_ref, kept_ref, swapped_ref, *refs):
    pieces, sems = refs[:-1], refs[-1]
    core, chip = place_ref[0], place_ref[1]
    prefixes = owner_ref.shape[0]

    def copies(source, step, prefix):
        return pltpu.make_async_copy(
            source.at[core, chip ^ step], pieces[step].at[prefix], sems.at[step, prefix]
        )

    for step in range(len(pieces)):
        for prefix in range(prefixes):
            here = owner_ref[prefix] % 2 == core

            @pl.when(here)
            def _():
                copies(kept_ref, step, prefix).start()

            @pl.when(jnp.logical_not(here))
            def _():
                copies(swapped_ref, step, prefix).start()

    for step in range(len(pieces)):
        for prefix in range(prefixes):
            copies(kept_ref, step, prefix).wait()


def multicast(prefix_cache, owners, outgoing):
    replicas = lax.axis_size("replica")
    me = lax.axis_index("replica")
    half = replicas // 2
    chips = half // 2
    bits = chips.bit_length() - 1
    chip = me // 2 % chips
    width = prefix_cache.shape[1]

    def swap_cores(rows):
        return lax.ppermute(rows, "replica", [(i, i ^ 1) for i in range(replicas)])

    def to_peer(rows, step):
        return lax.ppermute(rows, "replica", [(i, i ^ (2 * step)) for i in range(replicas)])

    split = prefix_cache.reshape(2, chips, -1, width)
    swapped, outgoing = lax.optimization_barrier((swap_cores(prefix_cache), outgoing))
    swapped = swapped.reshape(split.shape)
    piece = jax.ShapeDtypeStruct((owners.shape[0], split.shape[2], width), split.dtype)
    anywhere = pl.BlockSpec(memory_space=pl.ANY)
    staged = pl.pallas_call(
        stage_kernel,
        out_shape=(piece,) * chips,
        in_specs=[pl.BlockSpec(memory_space=pltpu.SMEM)] * 2 + [anywhere] * 2,
        out_specs=(whole(piece.shape),) * chips,
        grid=(1,),
        scratch_shapes=[pltpu.SemaphoreType.DMA((chips, owners.shape[0]))],
        compiler_params=PARAMS,
        name="stage_prefix",
    )(owners, jnp.stack([me % 2, chip]), split, swapped)
    away = chip ^ (owners // 2 % chips)
    found = staged[0]
    for step in range(chips - 1, 0, -1):
        rows = to_peer(staged[step], step)
        found = jnp.where((away == step)[:, None, None], rows, found)
    passed = lax.ppermute(found, "replica", [(i, (i + half) % replicas) for i in range(replicas)])
    held = jnp.where((owners // half == me // half)[:, None, None], found, passed)

    gathered = {0: held}
    for step in sorted(range(1, chips), key=lambda step: (step.bit_count(), step)):
        members = [bit for bit in range(bits) if step >> bit & 1]
        linked = [bit for bit in members if step >> ((bit - 1) % bits) & 1]
        last = 1 << min(linked or members)
        gathered[step] = to_peer(gathered[step ^ last], last)
    parts = [[], []]
    for step, rows in gathered.items():
        parts[step.bit_count() > 1].extend((rows, swap_cores(rows)))
    return parts, outgoing


def whole(shape):
    return pl.BlockSpec(shape, lambda *args: (0,) * len(shape))


def cost(rows, keys, size):
    return pl.CostEstimate(
        flops=6 * rows * keys * size, bytes_accessed=4 * keys * size, transcendentals=rows * keys
    )


def on_device(
    queries,
    suffix_kv,
    own_cache,
    ctx_len,
    prefix_cache,
    owners,
    readers,
    kv_pool,
    mig_target,
    mig_block,
    mig_count,
):
    me = lax.axis_index("replica")
    replicas = lax.axis_size("replica")
    size = suffix_kv.shape[1] // 2
    tokens = queries.shape[0]
    heads = queries.shape[1] // size
    factor = size ** (-0.5) * LOG2E
    row_count = tokens * heads
    state = (
        jax.ShapeDtypeStruct((heads, tokens, size), jnp.float32),
        jax.ShapeDtypeStruct((heads, tokens, 2 * size), jnp.float32),
    )
    state_specs = (whole(state[0].shape), whole(state[1].shape))
    in_smem = pl.BlockSpec(memory_space=pltpu.SMEM)
    anywhere = pl.BlockSpec(memory_space=pl.ANY)

    def scratch(keys):
        return [
            pltpu.VMEM((keys, size), jnp.bfloat16),
            pltpu.VMEM((keys, 2 * size), jnp.bfloat16),
        ]

    outgoing = pl.pallas_call(
        pack_kernel,
        out_shape=jax.ShapeDtypeStruct((replicas, *kv_pool.shape[1:]), kv_pool.dtype),
        in_specs=[in_smem] * 3 + [anywhere],
        out_specs=whole((replicas, *kv_pool.shape[1:])),
        grid=(1,),
        scratch_shapes=[pltpu.SemaphoreType.DMA((mig_target.shape[1],))],
        compiler_params=PARAMS,
        name="pack_moved",
    )(mig_target, mig_block, mig_count, kv_pool)
    shared, outgoing = multicast(prefix_cache, owners, outgoing)
    arrived = lax.all_to_all(outgoing, "replica", split_axis=0, concat_axis=0, tiled=True)

    rows = arrived.shape[1]
    group = max(1, CHUNK // rows)
    state_now = pl.pallas_call(
        functools.partial(first_kernel, factor),
        out_shape=state,
        grid=(replicas // group,),
        in_specs=[
            in_smem,
            whole(queries.shape),
            whole(suffix_kv.shape),
            whole(own_cache.shape),
            pl.BlockSpec((group, rows, 2 * size), lambda i: (i, 0, 0)),
        ],
        out_specs=state_specs,
        scratch_shapes=scratch(max(group * rows, own_cache.shape[0], tokens)),
        compiler_params=PARAMS,
        cost_estimate=cost(row_count, tokens + own_cache.shape[0] + replicas * rows, size),
        name="moved_keys",
    )(ctx_len, queries, suffix_kv, own_cache, arrived)

    for last, pieces in enumerate(shared):
        rows = pieces[0].shape[1]
        keys = len(pieces) * rows
        state_now = pl.pallas_call(
            functools.partial(prefix_kernel, factor, last, len(pieces)),
            out_shape=jax.ShapeDtypeStruct(queries.shape, queries.dtype) if last else state,
            grid_spec=pltpu.PrefetchScalarGridSpec(
                num_scalar_prefetch=1,
                grid=(max(1, keys // CHUNK),),
                in_specs=[
                    whole(queries.shape),
                    *[pl.BlockSpec((None, rows, 2 * size), lambda i, which: (which[0], 0, 0))]
                    * len(pieces),
                    *state_specs,
                ],
                out_specs=whole(queries.shape) if last else state_specs,
                scratch_shapes=[pltpu.VMEM(part.shape, part.dtype) for part in state] * last
                + scratch(keys),
            ),
            compiler_params=PARAMS,
            cost_estimate=cost(row_count, keys, size),
            name="prefix_keys",
        )(readers[me][None], queries, *pieces, *state_now)
    return state_now


def solution(mesh):
    in_specs = (
        P(("groups", "replica"), None),
        P(("groups", "replica"), None),
        P(("groups", "replica"), None),
        P(("groups", "replica")),
        P(("groups", "replica"), None),
        P("groups"),
        P("groups"),
        P(("groups", "replica"), None, None),
        P(("groups", "replica"), None),
        P(("groups", "replica"), None),
        P(("groups", "replica")),
    )
    out_specs = P(("groups", "replica"), None)
    return jax.shard_map(
        on_device, mesh=mesh, in_specs=in_specs, out_specs=out_specs, check_vma=False
    )
```

```python
import functools

import jax
import jax.numpy as jnp
from jax import lax
from jax.experimental import pallas as pl
from jax.experimental.pallas import tpu as pltpu
from jax.sharding import PartitionSpec as P

LOG2E = 1.4426950408889634
DEAD_MARK = 1024.0
DEAD_ABOVE = 512.0
NEG = -1e30
CHUNK = 1024
PARAMS = pltpu.CompilerParams(vmem_limit_bytes=40 * 1024 * 1024)
COPY_PARAMS = pltpu.CompilerParams(vmem_limit_bytes=56 * 1024 * 1024)


def fold_keys(q_ref, m_ref, acc_ref, keys, values, factor, mask=None):
    heads, tokens, width = acc_ref.shape
    size = keys.shape[1]
    for head in range(heads):
        rows = q_ref[:, head * size:(head + 1) * size]
        scores = lax.dot_general(
            rows, keys, (((1,), (1,)), ((), ())), preferred_element_type=jnp.float32
        )
        if mask is not None:
            scores = jnp.where(mask, scores, NEG)
        old_max = m_ref[head]
        new_max = jnp.maximum(old_max, jnp.max(scores, axis=1, keepdims=True))
        shrink = jnp.exp2((old_max - new_max) * factor)
        weights = jnp.exp2((scores - jnp.tile(new_max, (1, keys.shape[0] // size))) * factor)
        m_ref[head] = new_max
        acc_ref[head] = acc_ref[head] * jnp.tile(shrink, (1, width // size)) + jnp.dot(
            weights.astype(jnp.bfloat16), values, preferred_element_type=jnp.float32
        )


def finish(acc_ref, out_ref):
    heads, tokens, width = acc_ref.shape
    size = width // 2
    for head in range(heads):
        out_ref[:, head * size:(head + 1) * size] = (
            acc_ref[head, :, :size] / acc_ref[head, :, size:]
        ).astype(out_ref.dtype)


def stage_live(rows, live, suffix_ref, keys_ref, values_ref):
    size = suffix_ref.shape[1] // 2
    zeros = jnp.zeros((rows.shape[0], size), jnp.float32)
    spare = jnp.broadcast_to(suffix_ref[:1, :size].astype(jnp.float32), zeros.shape)
    keys_ref[:rows.shape[0], :] = jnp.where(live, rows[:, :size], spare).astype(jnp.bfloat16)
    values_ref[:rows.shape[0], :size] = jnp.where(live, rows[:, size:], zeros).astype(jnp.bfloat16)
    values_ref[:rows.shape[0], size:] = jnp.where(live, 1.0, zeros).astype(jnp.bfloat16)


def local_kernel(
    factor, len_ref, q_ref, suffix_ref, own_ref, m_ref, acc_ref, keys_ref, values_ref
):
    size = suffix_ref.shape[1] // 2
    suffix = suffix_ref.shape[0]
    own = own_ref.shape[0]
    m_ref[...] = jnp.full(m_ref.shape, NEG, jnp.float32)
    acc_ref[...] = jnp.zeros(acc_ref.shape, jnp.float32)
    values_ref[:suffix, :size] = suffix_ref[:, size:]
    values_ref[:suffix, size:] = jnp.ones((suffix, size), jnp.bfloat16)
    causal = lax.broadcasted_iota(jnp.int32, (suffix, suffix), 1) <= lax.broadcasted_iota(
        jnp.int32, (suffix, suffix), 0
    )
    fold_keys(
        q_ref, m_ref, acc_ref, suffix_ref[:, :size], values_ref[:suffix, :], factor, causal
    )
    live = lax.broadcasted_iota(jnp.int32, (own, size), 0) < len_ref[0]
    stage_live(own_ref[...].astype(jnp.float32), live, suffix_ref, keys_ref, values_ref)
    fold_keys(q_ref, m_ref, acc_ref, keys_ref[:own, :], values_ref[:own, :], factor)


def moved_kernel(
    factor, q_ref, suffix_ref, kv_ref, m_in, acc_in, m_ref, acc_ref, keys_ref, values_ref
):
    @pl.when(pl.program_id(0) == 0)
    def _():
        m_ref[...] = m_in[...]
        acc_ref[...] = acc_in[...]

    rows = kv_ref[...].reshape(-1, kv_ref.shape[-1]).astype(jnp.float32)
    size = suffix_ref.shape[1] // 2
    live = jnp.broadcast_to(rows[:, size:size + 1] < DEAD_ABOVE, (rows.shape[0], size))
    stage_live(rows, live, suffix_ref, keys_ref, values_ref)
    fold_keys(q_ref, m_ref, acc_ref, keys_ref[...], values_ref[...], factor)


def prefix_kernel(factor, last, count, steps, which_ref, q_ref, *refs):
    pieces, refs = refs[:count], refs[count:]
    m_in, acc_in, out_ref = refs[:3]
    m_ref, acc_ref, keys_ref, values_ref = refs[-4:]
    size = keys_ref.shape[1]
    step = pl.program_id(0)
    chunk = keys_ref.shape[0] // steps

    @pl.when(step == 0)
    def _():
        m_ref[...] = m_in[...]
        acc_ref[...] = acc_in[...]
        for place, piece in enumerate(pieces):
            rows = pl.ds(place * piece.shape[0], piece.shape[0])
            keys_ref[rows, :] = piece[:, :size]
            values_ref[rows, :size] = piece[:, size:]
        values_ref[:, size:] = jnp.ones((values_ref.shape[0], size), jnp.bfloat16)

    rows = pl.ds(pl.multiple_of(step * chunk, chunk), chunk)
    fold_keys(q_ref, m_ref, acc_ref, keys_ref[rows, :], values_ref[rows, :], factor)
    if last:

        @pl.when(step == steps - 1)
        def _():
            finish(acc_ref, out_ref)


def pack_kernel(target_ref, block_ref, count_ref, pool_ref, out_ref, sems):
    entries = target_ref.shape[1]

    def block(entry):
        return pltpu.make_async_copy(
            pool_ref.at[block_ref[0, entry]], out_ref.at[target_ref[0, entry]], sems.at[entry]
        )

    @pl.loop(0, entries)
    def _(entry):
        live = entry < count_ref[0]

        @pl.when(live)
        def _():
            block(entry).start()

        @pl.when(jnp.logical_not(live))
        def _():
            out_ref[target_ref[0, entry]] = jnp.full(out_ref.shape[1:], DEAD_MARK, out_ref.dtype)

    @pl.loop(0, entries)
    def _(entry):
        @pl.when(entry < count_ref[0])
        def _():
            block(entry).wait()


def stage_kernel(owner_ref, place_ref, kept_ref, swapped_ref, *refs):
    pieces, sems = refs[:-1], refs[-1]
    core, chip, is_last = place_ref[0], place_ref[1], place_ref[2]
    sought = owner_ref.shape[0]
    chips = len(pieces) // 2

    def copy(source, step, prefix):
        target = pieces[step].at[prefix] if prefix < sought else pieces[chips + step]
        return pltpu.make_async_copy(
            source.at[core, chip ^ step], target, sems.at[step, prefix]
        )

    def each(do):
        for step in range(chips):
            for prefix in range(sought):
                do(step, prefix, owner_ref[prefix] % 2 == core)

        @pl.when(is_last == 1)
        def _():
            for step in range(chips):
                do(step, sought, core == 1)

    def start(step, prefix, here):
        @pl.when(here)
        def _():
            copy(kept_ref, step, prefix).start()

        @pl.when(jnp.logical_not(here))
        def _():
            copy(swapped_ref, step, prefix).start()

    each(start)
    each(lambda step, prefix, here: copy(kept_ref, step, prefix).wait())


def multicast(prefix_cache, owners, readers, outgoing):
    replicas = lax.axis_size("replica")
    me = lax.axis_index("replica")
    half = replicas // 2
    chips = half // 2
    bits = chips.bit_length() - 1
    chip = me // 2 % chips
    side = me // half
    width = prefix_cache.shape[1]
    ids = jnp.arange(owners.shape[0], dtype=jnp.int32)
    known = jnp.sum(jnp.where(owners == replicas - 1, ids, 0))
    sought = jnp.where(ids[:-1] >= known, owners[1:], owners[:-1])

    def swap_cores(rows):
        return lax.ppermute(rows, "replica", [(i, i ^ 1) for i in range(replicas)])

    def to_peer(rows, step):
        return lax.ppermute(rows, "replica", [(i, i ^ (2 * step)) for i in range(replicas)])

    def from_last(rows, step):
        pair = (replicas - 2, replicas - 1)
        return lax.ppermute(rows, "replica", [(i, i ^ (2 * step)) for i in pair])

    split = prefix_cache.reshape(2, chips, -1, width)
    swapped, outgoing = lax.optimization_barrier((swap_cores(prefix_cache), outgoing))
    swapped = swapped.reshape(split.shape)
    piece = jax.ShapeDtypeStruct(split.shape[2:], split.dtype)
    pieces = jax.ShapeDtypeStruct((owners.shape[0] - 1, *piece.shape), split.dtype)
    anywhere = pl.BlockSpec(memory_space=pl.ANY)
    staged = pl.pallas_call(
        stage_kernel,
        out_shape=(pieces,) * chips + (piece,) * chips,
        in_specs=[pl.BlockSpec(memory_space=pltpu.SMEM)] * 2 + [anywhere] * 2,
        out_specs=(whole(pieces.shape),) * chips + (whole(piece.shape),) * chips,
        grid=(1,),
        scratch_shapes=[pltpu.SemaphoreType.DMA((chips, owners.shape[0]))],
        compiler_params=COPY_PARAMS,
        name="stage_prefix",
    )(
        sought,
        jnp.stack([me % 2, chip, (me // 2 == replicas // 2 - 1).astype(jnp.int32)]),
        split,
        swapped,
    )
    staged, staged_known = staged[:chips], staged[chips:]

    away = chip ^ (chips - 1)
    found = staged_known[0]
    for step in range(1, chips):
        found = jnp.where(away == step, from_last(staged_known[step], step), found)
    passed = lax.ppermute(found, "replica", [(i + half, i) for i in range(half)])
    held_known = jnp.where(side == 1, found, passed)

    away = chip ^ (sought // 2 % chips)
    found = staged[0]
    for step in range(chips - 1, 0, -1):
        rows = to_peer(staged[step], step)
        found = jnp.where((away == step)[:, None, None], rows, found)
    passed = lax.ppermute(found, "replica", [(i, (i + half) % replicas) for i in range(replicas)])
    held = jnp.where((sought // half == side)[:, None, None], found, passed)
    held = jnp.concatenate([held_known[None], held])

    gathered = {0: held}
    for step in sorted(range(1, chips), key=lambda step: (step.bit_count(), step)):
        members = [bit for bit in range(bits) if step >> bit & 1]
        linked = [bit for bit in members if step >> ((bit - 1) % bits) & 1]
        last = 1 << min(linked or members)
        gathered[step] = to_peer(gathered[step ^ last], last)
    parts = [[], []]
    for step, rows in gathered.items():
        parts[step.bit_count() > 1].extend((rows, swap_cores(rows)))
    wanted = readers[me]
    place = jnp.where(wanted == known, 0, wanted + (wanted < known))
    return parts, place[None], outgoing


def whole(shape):
    return pl.BlockSpec(shape, lambda *args: (0,) * len(shape))


def cost(rows, keys, size):
    return pl.CostEstimate(
        flops=6 * rows * keys * size, bytes_accessed=4 * keys * size, transcendentals=rows * keys
    )


def on_device(
    queries,
    suffix_kv,
    own_cache,
    ctx_len,
    prefix_cache,
    owners,
    readers,
    kv_pool,
    mig_target,
    mig_block,
    mig_count,
):
    replicas = lax.axis_size("replica")
    size = suffix_kv.shape[1] // 2
    tokens = queries.shape[0]
    heads = queries.shape[1] // size
    factor = size ** (-0.5) * LOG2E
    row_count = tokens * heads
    state = (
        jax.ShapeDtypeStruct((heads, tokens, size), jnp.float32),
        jax.ShapeDtypeStruct((heads, tokens, 2 * size), jnp.float32),
    )
    state_specs = (whole(state[0].shape), whole(state[1].shape))
    in_smem = pl.BlockSpec(memory_space=pltpu.SMEM)
    anywhere = pl.BlockSpec(memory_space=pl.ANY)

    def scratch(keys):
        return [
            pltpu.VMEM((keys, size), jnp.bfloat16),
            pltpu.VMEM((keys, 2 * size), jnp.bfloat16),
        ]

    outgoing = pl.pallas_call(
        pack_kernel,
        out_shape=jax.ShapeDtypeStruct((replicas, *kv_pool.shape[1:]), kv_pool.dtype),
        in_specs=[in_smem] * 3 + [anywhere],
        out_specs=whole((replicas, *kv_pool.shape[1:])),
        grid=(1,),
        scratch_shapes=[pltpu.SemaphoreType.DMA((mig_target.shape[1],))],
        compiler_params=COPY_PARAMS,
        name="pack_moved",
    )(mig_target, mig_block, mig_count, kv_pool)
    shared, place, outgoing = multicast(prefix_cache, owners, readers, outgoing)
    arrived = lax.all_to_all(outgoing, "replica", split_axis=0, concat_axis=0, tiled=True)

    state_now = pl.pallas_call(
        functools.partial(local_kernel, factor),
        out_shape=state,
        grid=(1,),
        in_specs=[
            in_smem,
            whole(queries.shape),
            whole(suffix_kv.shape),
            whole(own_cache.shape),
        ],
        out_specs=state_specs,
        scratch_shapes=scratch(max(own_cache.shape[0], tokens)),
        compiler_params=PARAMS,
        cost_estimate=cost(row_count, tokens + own_cache.shape[0], size),
        name="local_keys",
    )(ctx_len, queries, suffix_kv, own_cache)

    rows = arrived.shape[1]
    group = max(1, CHUNK // rows)
    steps = replicas // group
    for begin, end in ((0, steps // 2), (steps // 2, steps)):
        state_now = pl.pallas_call(
            functools.partial(moved_kernel, factor),
            out_shape=state,
            grid=(end - begin,),
            in_specs=[
                whole(queries.shape),
                whole(suffix_kv.shape),
                pl.BlockSpec((group, rows, 2 * size), lambda i, begin=begin: (i + begin, 0, 0)),
                *state_specs,
            ],
            out_specs=state_specs,
            scratch_shapes=scratch(group * rows),
            compiler_params=PARAMS,
            cost_estimate=cost(row_count, (end - begin) * group * rows, size),
            name="moved_keys",
        )(queries, suffix_kv, arrived, *state_now)

    for last, pieces in enumerate(shared):
        rows = pieces[0].shape[1]
        keys = len(pieces) * rows
        steps = max(1, keys // CHUNK)
        while keys % (steps * size):
            steps -= 1
        state_now = pl.pallas_call(
            functools.partial(prefix_kernel, factor, last, len(pieces), steps),
            out_shape=jax.ShapeDtypeStruct(queries.shape, queries.dtype) if last else state,
            grid_spec=pltpu.PrefetchScalarGridSpec(
                num_scalar_prefetch=1,
                grid=(steps,),
                in_specs=[
                    whole(queries.shape),
                    *[pl.BlockSpec((None, rows, 2 * size), lambda i, which: (which[0], 0, 0))]
                    * len(pieces),
                    *state_specs,
                ],
                out_specs=whole(queries.shape) if last else state_specs,
                scratch_shapes=[pltpu.VMEM(part.shape, part.dtype) for part in state] * last
                + scratch(keys),
            ),
            compiler_params=PARAMS,
            cost_estimate=cost(row_count, keys, size),
            name="prefix_keys",
        )(place, queries, *pieces, *state_now)
    return state_now


def solution(mesh):
    in_specs = (
        P(("groups", "replica"), None),
        P(("groups", "replica"), None),
        P(("groups", "replica"), None),
        P(("groups", "replica")),
        P(("groups", "replica"), None),
        P("groups"),
        P("groups"),
        P(("groups", "replica"), None, None),
        P(("groups", "replica"), None),
        P(("groups", "replica"), None),
        P(("groups", "replica")),
    )
    out_specs = P(("groups", "replica"), None)
    return jax.shard_map(
        on_device, mesh=mesh, in_specs=in_specs, out_specs=out_specs, check_vma=False
    )
```

```python
import functools

import jax
import jax.numpy as jnp
from jax import lax
from jax.experimental import pallas as pl
from jax.experimental.pallas import tpu as pltpu
from jax.sharding import PartitionSpec as P

LOG2E = 1.4426950408889634
DEAD_MARK = 1024.0
DEAD_ABOVE = 512.0
NEG = -1e30
CHUNK = 1024
PARAMS = pltpu.CompilerParams(vmem_limit_bytes=40 * 1024 * 1024)
COPY_PARAMS = pltpu.CompilerParams(vmem_limit_bytes=56 * 1024 * 1024)

IN_SMEM = pl.BlockSpec(memory_space=pltpu.SMEM)
IN_HBM = pl.BlockSpec(memory_space=pltpu.HBM)
MOVED_PARTS = 2


def fold_keys(q_ref, m_ref, acc_ref, keys, values, factor, mask=None):
    heads, tokens, width = acc_ref.shape
    size = keys.shape[1]
    for head in range(heads):
        rows = q_ref[:, head * size:(head + 1) * size]
        scores = lax.dot_general(
            rows, keys, (((1,), (1,)), ((), ())), preferred_element_type=jnp.float32
        )
        if mask is not None:
            scores = jnp.where(mask, scores, NEG)
        old_max = m_ref[head]
        new_max = jnp.maximum(old_max, jnp.max(scores, axis=1, keepdims=True))
        shrink = jnp.exp2((old_max - new_max) * factor)
        weights = jnp.exp2((scores - jnp.tile(new_max, (1, keys.shape[0] // size))) * factor)
        m_ref[head] = new_max
        acc_ref[head] = acc_ref[head] * jnp.tile(shrink, (1, width // size)) + jnp.dot(
            weights.astype(jnp.bfloat16), values, preferred_element_type=jnp.float32
        )


def finish(acc_ref, out_ref):
    heads, tokens, width = acc_ref.shape
    size = width // 2
    for head in range(heads):
        out_ref[:, head * size:(head + 1) * size] = (
            acc_ref[head, :, :size] / acc_ref[head, :, size:]
        ).astype(out_ref.dtype)


def stage_live(rows, live, suffix_ref, keys_ref, values_ref):
    size = suffix_ref.shape[1] // 2
    zeros = jnp.zeros((rows.shape[0], size), jnp.float32)
    spare = jnp.broadcast_to(suffix_ref[:1, :size].astype(jnp.float32), zeros.shape)
    keys_ref[:rows.shape[0], :] = jnp.where(live, rows[:, :size], spare).astype(jnp.bfloat16)
    values_ref[:rows.shape[0], :size] = jnp.where(live, rows[:, size:], zeros).astype(jnp.bfloat16)
    values_ref[:rows.shape[0], size:] = jnp.where(live, 1.0, zeros).astype(jnp.bfloat16)


def state_copies(state_here, state_there, sems):
    return [
        pltpu.make_async_copy(source, target, sems.at[place])
        for place, (source, target) in enumerate(zip(state_here, state_there))
    ]


def start_all(copies):
    for copy in copies:
        copy.start()


def wait_all(copies):
    for copy in copies:
        copy.wait()


def fold_local(factor, len_ref, q_ref, suffix_ref, own_ref, m_ref, acc_ref, keys_ref, values_ref):
    size = suffix_ref.shape[1] // 2
    suffix = suffix_ref.shape[0]
    own = own_ref.shape[0]
    m_ref[...] = jnp.full(m_ref.shape, NEG, jnp.float32)
    acc_ref[...] = jnp.zeros(acc_ref.shape, jnp.float32)
    values_ref[:suffix, :size] = suffix_ref[:, size:]
    values_ref[:suffix, size:] = jnp.ones((suffix, size), jnp.bfloat16)
    causal = lax.broadcasted_iota(jnp.int32, (suffix, suffix), 1) <= lax.broadcasted_iota(
        jnp.int32, (suffix, suffix), 0
    )
    fold_keys(
        q_ref, m_ref, acc_ref, suffix_ref[:, :size], values_ref[:suffix, :], factor, causal
    )
    live = lax.broadcasted_iota(jnp.int32, (own, size), 0) < len_ref[0]
    stage_live(own_ref[...].astype(jnp.float32), live, suffix_ref, keys_ref, values_ref)
    fold_keys(q_ref, m_ref, acc_ref, keys_ref[:own, :], values_ref[:own, :], factor)


def moved_kernel(factor, local, steps, *refs):
    q_ref, suffix_ref, kv_ref = refs[:3]
    state_out = refs[-7:-5]
    m_ref, acc_ref, keys_ref, values_ref, sems = refs[-5:]
    step = pl.program_id(0)

    if local:

        @pl.when(step == 0)
        def _():
            fold_local(factor, refs[3], q_ref, suffix_ref, refs[4], *refs[-5:-1])

    else:
        loads = state_copies(refs[3:5], (m_ref, acc_ref), sems)
        pl.when(step == 0)(lambda: start_all(loads))

    rows = kv_ref[...].reshape(-1, kv_ref.shape[-1]).astype(jnp.float32)
    size = suffix_ref.shape[1] // 2
    live = jnp.broadcast_to(rows[:, size:size + 1] < DEAD_ABOVE, (rows.shape[0], size))
    stage_live(rows, live, suffix_ref, keys_ref, values_ref)
    if not local:
        pl.when(step == 0)(lambda: wait_all(loads))
    count = rows.shape[0]
    fold_keys(q_ref, m_ref, acc_ref, keys_ref[:count, :], values_ref[:count, :], factor)

    @pl.when(step == steps - 1)
    def _():
        saves = state_copies((m_ref, acc_ref), state_out, sems)
        start_all(saves)
        wait_all(saves)


def prefix_kernel(factor, last, count, steps, which_ref, q_ref, *refs):
    pieces, refs = refs[:count], refs[count:]
    m_ref, acc_ref, keys_ref, values_ref, sems = refs[-5:]
    size = keys_ref.shape[1]
    step = pl.program_id(0)
    chunk = keys_ref.shape[0] // steps

    @pl.when(step == 0)
    def _():
        loads = state_copies(refs[:2], (m_ref, acc_ref), sems)
        start_all(loads)
        for place, piece in enumerate(pieces):
            rows = pl.ds(place * piece.shape[0], piece.shape[0])
            keys_ref[rows, :] = piece[:, :size]
            values_ref[rows, :size] = piece[:, size:]
        values_ref[:, size:] = jnp.ones((values_ref.shape[0], size), jnp.bfloat16)
        wait_all(loads)

    rows = pl.ds(pl.multiple_of(step * chunk, chunk), chunk)
    fold_keys(q_ref, m_ref, acc_ref, keys_ref[rows, :], values_ref[rows, :], factor)

    @pl.when(step == steps - 1)
    def _():
        if last:
            finish(acc_ref, refs[2])
        else:
            saves = state_copies((m_ref, acc_ref), refs[2:4], sems)
            start_all(saves)
            wait_all(saves)


def pack_kernel(target_ref, block_ref, count_ref, pool_ref, *refs):
    parts = refs[:-4]
    held_ref, mark_ref, in_sems, out_sems = refs[-4:]
    entries = target_ref.shape[1]
    mark_ref[...] = jnp.full(mark_ref.shape, DEAD_MARK, mark_ref.dtype)

    def load(entry):
        return pltpu.make_async_copy(
            pool_ref.at[block_ref[0, entry]], held_ref.at[entry], in_sems.at[entry]
        )

    def stores(entry, source):
        rows = parts[0].shape[1]
        return [
            pltpu.make_async_copy(
                source.at[pl.ds(place * rows, rows)],
                part.at[target_ref[0, entry]],
                out_sems.at[place, entry],
            )
            for place, part in enumerate(parts)
        ]

    @pl.loop(0, entries)
    def _(entry):
        live = entry < count_ref[0]
        pl.when(live)(lambda: load(entry).start())
        pl.when(jnp.logical_not(live))(lambda: start_all(stores(entry, mark_ref)))

    @pl.loop(0, entries)
    def _(entry):
        @pl.when(entry < count_ref[0])
        def _():
            load(entry).wait()
            start_all(stores(entry, held_ref.at[entry]))

    @pl.loop(0, entries)
    def _(entry):
        wait_all(stores(entry, mark_ref))


def stage_kernel(owner_ref, place_ref, kept_ref, swapped_ref, *refs):
    outs, (sought_ref, known_ref, in_sems, out_sems) = refs[:-4], refs[-4:]
    core, chip, is_last = place_ref[0], place_ref[1], place_ref[2]
    chips, sought = sought_ref.shape[:2]
    bits = chips.bit_length() - 1

    def load(source, step, prefix):
        if prefix < sought:
            place, target = chip ^ step, sought_ref.at[step, prefix]
        else:
            mirrored = sum((step >> bit & 1) << (bits - 1 - bit) for bit in range(bits))
            place, target = step, known_ref.at[mirrored]
        return pltpu.make_async_copy(source.at[core, place], target, in_sems.at[step, prefix])

    def start(step, prefix, here):
        pl.when(here)(lambda: load(kept_ref, step, prefix).start())
        pl.when(jnp.logical_not(here))(lambda: load(swapped_ref, step, prefix).start())

    def store(place):
        half = chips // 2
        if place < chips:
            source = sought_ref.at[place]
        else:
            source = known_ref.at[pl.ds((place - chips) * half, half)]
        return pltpu.make_async_copy(source, outs[place], out_sems.at[place])

    for step in range(chips):
        for prefix in range(sought):
            start(step, prefix, owner_ref[prefix] % 2 == core)

    @pl.when(is_last == 1)
    def _():
        for step in range(chips):
            start(step, sought, core == 1)

    for step in range(chips):
        for prefix in range(sought):
            load(kept_ref, step, prefix).wait()
        store(step).start()

    @pl.when(is_last == 1)
    def _():
        for step in range(chips):
            load(kept_ref, step, sought).wait()

    for place in range(chips, chips + 2):
        store(place).start()
    for place in range(chips + 2):
        store(place).wait()


def multicast(prefix_cache, owners, readers, outgoing):
    replicas = lax.axis_size("replica")
    me = lax.axis_index("replica")
    half = replicas // 2
    chips = half // 2
    bits = chips.bit_length() - 1
    chip = me // 2 % chips
    side = me // half
    width = prefix_cache.shape[1]
    ids = jnp.arange(owners.shape[0], dtype=jnp.int32)
    known = jnp.sum(jnp.where(owners == replicas - 1, ids, 0))
    sought = jnp.where(ids[:-1] >= known, owners[1:], owners[:-1])

    def swap_cores(rows):
        return lax.ppermute(rows, "replica", [(i, i ^ 1) for i in range(replicas)])

    def to_peer(rows, step):
        return lax.ppermute(rows, "replica", [(i, i ^ (2 * step)) for i in range(replicas)])

    split = prefix_cache.reshape(2, chips, -1, width)
    swapped, *outgoing = lax.optimization_barrier((swap_cores(prefix_cache), *outgoing))
    swapped = swapped.reshape(split.shape)
    rows = split.shape[2]
    pieces = jax.ShapeDtypeStruct((owners.shape[0] - 1, rows, width), split.dtype)
    known_pieces = jax.ShapeDtypeStruct((chips // 2, rows, width), split.dtype)
    staged = pl.pallas_call(
        stage_kernel,
        out_shape=(pieces,) * chips + (known_pieces,) * 2,
        in_specs=[IN_SMEM] * 2 + [IN_HBM] * 2,
        out_specs=(IN_HBM,) * (chips + 2),
        scratch_shapes=[
            pltpu.VMEM((chips, *pieces.shape), split.dtype),
            pltpu.VMEM((chips, rows, width), split.dtype),
            pltpu.SemaphoreType.DMA((chips, owners.shape[0])),
            pltpu.SemaphoreType.DMA((chips + 2,)),
        ],
        compiler_params=COPY_PARAMS,
        name="stage_prefix",
    )(
        sought,
        jnp.stack([me % 2, chip, (me // 2 == replicas // 2 - 1).astype(jnp.int32)]),
        split,
        swapped,
    )

    away = chip ^ (sought // 2 % chips)
    found = staged[0]
    for step in range(chips - 1, 0, -1):
        rows = to_peer(staged[step], step)
        found = jnp.where((away == step)[:, None, None], rows, found)
    passed = lax.ppermute(found, "replica", [(i, (i + half) % replicas) for i in range(replicas)])
    passed, *later = lax.optimization_barrier((passed, *outgoing[1:]))
    held = jnp.where((sought // half == side)[:, None, None], found, passed)

    sent, known_held = staged[chips], staged[chips + 1]
    for bit in range(bits):
        senders = [
            i for i in range(half, replicas) if (i // 2 % chips) >> bit == (chips - 1) >> bit
        ]
        passed = lax.ppermute(sent, "replica", [(i, i ^ (2 << bit)) for i in senders])
        known_held = jnp.where(chip >> bit & 1 == 1, known_held, passed)
        left = known_held.shape[0] // 2
        sent, known_held = known_held[:left], known_held[left:] if left else known_held
    passed = lax.ppermute(known_held, "replica", [(i + half, i) for i in range(half)])
    held = jnp.concatenate([jnp.where(side == 1, known_held, passed), held])

    gathered = {0: held}
    for step in sorted(range(1, chips), key=lambda step: (step.bit_count(), step)):
        members = [bit for bit in range(bits) if step >> bit & 1]
        linked = [bit for bit in members if step >> ((bit - 1) % bits) & 1]
        last = 1 << min(linked or members)
        gathered[step] = to_peer(gathered[step ^ last], last)
    parts = [[], []]
    for step, rows in gathered.items():
        parts[step.bit_count() > 1].extend((rows, swap_cores(rows)))
    wanted = readers[me]
    place = jnp.where(wanted == known, 0, wanted + (wanted < known))
    return parts, place[None], (outgoing[0], *later)


def whole(shape):
    return pl.BlockSpec(shape, lambda *args: (0,) * len(shape))


def cost(rows, keys, size):
    return pl.CostEstimate(
        flops=12 * rows * keys * size, bytes_accessed=4 * keys * size, transcendentals=rows * keys
    )


def on_device(
    queries,
    suffix_kv,
    own_cache,
    ctx_len,
    prefix_cache,
    owners,
    readers,
    kv_pool,
    mig_target,
    mig_block,
    mig_count,
):
    replicas = lax.axis_size("replica")
    size = suffix_kv.shape[1] // 2
    tokens = queries.shape[0]
    heads = queries.shape[1] // size
    factor = size ** (-0.5) * LOG2E
    row_count = tokens * heads
    state = (
        jax.ShapeDtypeStruct((heads, tokens, size), jnp.float32),
        jax.ShapeDtypeStruct((heads, tokens, 2 * size), jnp.float32),
    )
    def scratch(keys):
        return [
            *[pltpu.VMEM(part.shape, part.dtype) for part in state],
            pltpu.VMEM((keys, size), jnp.bfloat16),
            pltpu.VMEM((keys, 2 * size), jnp.bfloat16),
            pltpu.SemaphoreType.DMA((2,)),
        ]

    entries = mig_target.shape[1]
    rows = kv_pool.shape[1] // MOVED_PARTS
    part = jax.ShapeDtypeStruct((replicas, rows, kv_pool.shape[2]), kv_pool.dtype)
    outgoing = pl.pallas_call(
        pack_kernel,
        out_shape=(part,) * MOVED_PARTS,
        in_specs=[IN_SMEM] * 3 + [IN_HBM],
        out_specs=(IN_HBM,) * MOVED_PARTS,
        scratch_shapes=[
            pltpu.VMEM((entries, *kv_pool.shape[1:]), kv_pool.dtype),
            pltpu.VMEM(kv_pool.shape[1:], kv_pool.dtype),
            pltpu.SemaphoreType.DMA((entries,)),
            pltpu.SemaphoreType.DMA((MOVED_PARTS, entries)),
        ],
        compiler_params=COPY_PARAMS,
        name="pack_moved",
    )(mig_target, mig_block, mig_count, kv_pool)
    shared, place, outgoing = multicast(prefix_cache, owners, readers, outgoing)

    state_now = ()
    for count, part in enumerate(outgoing):
        arrived = lax.all_to_all(part, "replica", split_axis=0, concat_axis=0, tiled=True)
        local = count == 0
        group = min(replicas, max(1, CHUNK // rows))
        steps = replicas // group
        most = max(group * rows, own_cache.shape[0], tokens) if local else group * rows
        keys = replicas * rows + (tokens + own_cache.shape[0]) * local
        state_now = pl.pallas_call(
            functools.partial(moved_kernel, factor, local, steps),
            out_shape=state,
            grid=(steps,),
            in_specs=[
                whole(queries.shape),
                whole(suffix_kv.shape),
                pl.BlockSpec((group, rows, 2 * size), lambda i: (i, 0, 0)),
                *([IN_SMEM, whole(own_cache.shape)] if local else [IN_HBM, IN_HBM]),
            ],
            out_specs=(IN_HBM, IN_HBM),
            scratch_shapes=scratch(most),
            compiler_params=PARAMS,
            cost_estimate=cost(row_count, keys, size),
            name="moved_keys",
        )(queries, suffix_kv, arrived, *((ctx_len, own_cache) if local else state_now))

    for last, pieces in enumerate(shared):
        rows = pieces[0].shape[1]
        keys = len(pieces) * rows
        steps = max(1, keys // CHUNK)
        while keys % (steps * size):
            steps -= 1
        state_now = pl.pallas_call(
            functools.partial(prefix_kernel, factor, last, len(pieces), steps),
            out_shape=jax.ShapeDtypeStruct(queries.shape, queries.dtype) if last else state,
            grid_spec=pltpu.PrefetchScalarGridSpec(
                num_scalar_prefetch=1,
                grid=(steps,),
                in_specs=[
                    whole(queries.shape),
                    *[pl.BlockSpec((None, rows, 2 * size), lambda i, which: (which[0], 0, 0))]
                    * len(pieces),
                    IN_HBM,
                    IN_HBM,
                ],
                out_specs=whole(queries.shape) if last else (IN_HBM, IN_HBM),
                scratch_shapes=scratch(keys),
            ),
            compiler_params=PARAMS,
            cost_estimate=cost(row_count, keys, size),
            name="prefix_keys",
        )(place, queries, *pieces, *state_now)
    return state_now


def solution(mesh):
    in_specs = (
        P(("groups", "replica"), None),
        P(("groups", "replica"), None),
        P(("groups", "replica"), None),
        P(("groups", "replica")),
        P(("groups", "replica"), None),
        P("groups"),
        P("groups"),
        P(("groups", "replica"), None, None),
        P(("groups", "replica"), None),
        P(("groups", "replica"), None),
        P(("groups", "replica")),
    )
    out_specs = P(("groups", "replica"), None)
    return jax.shard_map(
        on_device, mesh=mesh, in_specs=in_specs, out_specs=out_specs, check_vma=False
    )
```

```python
import functools

import jax
import jax.numpy as jnp
from jax import lax
from jax.experimental import pallas as pl
from jax.experimental.pallas import tpu as pltpu
from jax.sharding import PartitionSpec as P

LOG2E = 1.4426950408889634
DEAD_MARK = 1024.0
DEAD_ABOVE = 512.0
NEG = -1e30
CHUNK = 1024
PARAMS = pltpu.CompilerParams(vmem_limit_bytes=40 * 1024 * 1024)
COPY_PARAMS = pltpu.CompilerParams(vmem_limit_bytes=56 * 1024 * 1024)

IN_SMEM = pl.BlockSpec(memory_space=pltpu.SMEM)
IN_HBM = pl.BlockSpec(memory_space=pltpu.HBM)
MOVED_PARTS = 2
ONE_ROWS = 16
MAX_ROWS = 8


def fold_keys(qt_ref, state_ref, tokens, keys, values, factor, mask=None):
    high = values.shape[0]
    heads = qt_ref.shape[1] // tokens

    def score(head):
        columns = slice(head * tokens, (head + 1) * tokens)
        scores = jnp.dot(keys, qt_ref[:, columns], preferred_element_type=jnp.float32)
        return scores if mask is None else jnp.where(mask, scores, NEG)

    following = score(0)
    for head in range(heads):
        scores, following = following, score(head + 1) if head + 1 < heads else None
        columns = slice(head * tokens, (head + 1) * tokens)
        old_max = state_ref[high:high + 1, columns]
        new_max = jnp.maximum(old_max, jnp.max(scores, axis=0, keepdims=True))
        shrink = jnp.exp2((old_max - new_max) * factor)
        weights = jnp.exp2((scores - new_max) * factor).astype(jnp.bfloat16)
        state_ref[high:, columns] = jnp.broadcast_to(new_max, (MAX_ROWS, tokens))
        state_ref[:high, columns] = state_ref[:high, columns] * shrink + jnp.dot(
            values, weights, preferred_element_type=jnp.float32
        )


def finish(state_ref, out_ref):
    tokens, width = out_ref.shape
    size = state_ref.shape[0] - ONE_ROWS - MAX_ROWS
    for head in range(width // size):
        columns = slice(head * tokens, (head + 1) * tokens)
        attended = state_ref[:size, columns] / state_ref[size:size + 1, columns]
        out_ref[:, head * size:(head + 1) * size] = attended.T.astype(out_ref.dtype)


def stage_rows(rows, place, keys_ref, values_ref):
    size = keys_ref.shape[1]
    count = rows.shape[0]
    columns = pl.ds(place, count)
    keys_ref[columns, :] = rows[:, :size]
    values_ref[:size, columns] = rows[:, size:].astype(jnp.float32).T.astype(jnp.bfloat16)
    values_ref[size:, columns] = jnp.ones((ONE_ROWS, count), jnp.bfloat16)


def stage_live(rows, live, suffix_ref, keys_ref, values_ref):
    size = suffix_ref.shape[1] // 2
    count = rows.shape[0]
    zeros = jnp.zeros((count, size), jnp.float32)
    spare = jnp.broadcast_to(suffix_ref[:1, :size].astype(jnp.float32), zeros.shape)
    keys_ref[:count, :] = jnp.where(live, rows[:, :size], spare).astype(jnp.bfloat16)
    values_ref[:size, :count] = jnp.where(live, rows[:, size:], zeros).T.astype(jnp.bfloat16)
    ones = jnp.where(live, 1.0, zeros).T
    values_ref[size:, :count] = ones[:ONE_ROWS].astype(jnp.bfloat16)


def start_all(copies):
    for copy in copies:
        copy.start()


def wait_all(copies):
    for copy in copies:
        copy.wait()


def fold_local(factor, len_ref, qt_ref, suffix_ref, own_ref, state_ref, keys_ref, values_ref):
    size = suffix_ref.shape[1] // 2
    suffix = suffix_ref.shape[0]
    own = own_ref.shape[0]
    high = values_ref.shape[0]
    state_ref[:high] = jnp.zeros((high, state_ref.shape[1]), jnp.float32)
    state_ref[high:] = jnp.full((MAX_ROWS, state_ref.shape[1]), NEG, jnp.float32)
    stage_rows(suffix_ref[...], 0, keys_ref, values_ref)
    causal = lax.broadcasted_iota(jnp.int32, (suffix, suffix), 0) <= lax.broadcasted_iota(
        jnp.int32, (suffix, suffix), 1
    )
    fold_keys(
        qt_ref, state_ref, suffix, keys_ref[:suffix, :], values_ref[:, :suffix], factor, causal
    )
    live = lax.broadcasted_iota(jnp.int32, (own, size), 0) < len_ref[0]
    stage_live(own_ref[...].astype(jnp.float32), live, suffix_ref, keys_ref, values_ref)
    fold_keys(qt_ref, state_ref, suffix, keys_ref[:own, :], values_ref[:, :own], factor)


def moved_kernel(factor, local, steps, *refs):
    qt_ref, suffix_ref, kv_ref = refs[:3]
    state_out, state_ref, keys_ref, values_ref, sem = refs[-5:]
    step = pl.program_id(0)

    if local:

        @pl.when(step == 0)
        def _():
            fold_local(
                factor, refs[3], qt_ref, suffix_ref, refs[4], state_ref, keys_ref, values_ref
            )

    else:
        load = pltpu.make_async_copy(refs[3], state_ref, sem)
        pl.when(step == 0)(lambda: load.start())

    rows = kv_ref[...].reshape(-1, kv_ref.shape[-1]).astype(jnp.float32)
    count, size = rows.shape[0], rows.shape[1] // 2
    live = jnp.broadcast_to(rows[:, size:size + 1] < DEAD_ABOVE, (count, size))
    stage_live(rows, live, suffix_ref, keys_ref, values_ref)
    if not local:
        pl.when(step == 0)(lambda: load.wait())
    fold_keys(
        qt_ref, state_ref, suffix_ref.shape[0], keys_ref[:count, :], values_ref[:, :count], factor
    )

    @pl.when(step == steps - 1)
    def _():
        save = pltpu.make_async_copy(state_ref, state_out, sem)
        save.start()
        save.wait()


def prefix_kernel(factor, last, count, steps, tokens, which_ref, qt_ref, *refs):
    pieces, refs = refs[:count], refs[count:]
    state_in, out_ref, state_ref, keys_ref, values_ref, sem = refs
    step = pl.program_id(0)
    chunk = keys_ref.shape[0] // steps

    @pl.when(step == 0)
    def _():
        load = pltpu.make_async_copy(state_in, state_ref, sem)
        load.start()
        place = 0
        for piece in pieces:
            stage_rows(piece[...], place, keys_ref, values_ref)
            place += piece.shape[0]
        load.wait()

    rows = pl.ds(pl.multiple_of(step * chunk, keys_ref.shape[1]), chunk)
    fold_keys(qt_ref, state_ref, tokens, keys_ref[rows, :], values_ref[:, rows], factor)

    @pl.when(step == steps - 1)
    def _():
        if last:
            finish(state_ref, out_ref)
        else:
            save = pltpu.make_async_copy(state_ref, out_ref, sem)
            save.start()
            save.wait()


def pick_kernel(which_ref, *refs):
    pieces, out_ref = refs[:-1], refs[-1]
    for place, piece in enumerate(pieces):
        out_ref[pl.ds(place * piece.shape[0], piece.shape[0]), :] = piece[...]


def pack_kernel(target_ref, block_ref, count_ref, pool_ref, *refs):
    parts = refs[:-4]
    held_ref, mark_ref, in_sems, out_sems = refs[-4:]
    entries = target_ref.shape[1]
    mark_ref[...] = jnp.full(mark_ref.shape, DEAD_MARK, mark_ref.dtype)

    def load(entry):
        return pltpu.make_async_copy(
            pool_ref.at[block_ref[0, entry]], held_ref.at[entry], in_sems.at[entry]
        )

    def stores(entry, source):
        rows = parts[0].shape[1]
        return [
            pltpu.make_async_copy(
                source.at[pl.ds(place * rows, rows)],
                part.at[target_ref[0, entry]],
                out_sems.at[place, entry],
            )
            for place, part in enumerate(parts)
        ]

    @pl.loop(0, entries)
    def _(entry):
        live = entry < count_ref[0]
        pl.when(live)(lambda: load(entry).start())
        pl.when(jnp.logical_not(live))(lambda: start_all(stores(entry, mark_ref)))

    @pl.loop(0, entries)
    def _(entry):
        @pl.when(entry < count_ref[0])
        def _():
            load(entry).wait()
            start_all(stores(entry, held_ref.at[entry]))

    @pl.loop(0, entries)
    def _(entry):
        wait_all(stores(entry, mark_ref))


def placed(step, order):
    return sum((step >> bit & 1) << (len(order) - 1 - rank) for rank, bit in enumerate(order))


def stage_kernel(orders, owner_ref, place_ref, kept_ref, swapped_ref, *refs):
    outs, (sought_ref, known_ref, in_sems, out_sems) = refs[:-4], refs[-4:]
    core, chip, is_last = place_ref[0], place_ref[1], place_ref[2]
    chips, sought = sought_ref.shape[:2]

    def load(source, step, prefix):
        if prefix < sought:
            target = sought_ref.at[placed(step, orders[0]), prefix]
        else:
            target = known_ref.at[placed(step, orders[1]), 0]
        return pltpu.make_async_copy(source.at[core, chip ^ step], target, in_sems.at[step, prefix])

    def start(step, prefix, here):
        pl.when(here)(lambda: load(kept_ref, step, prefix).start())
        pl.when(jnp.logical_not(here))(lambda: load(swapped_ref, step, prefix).start())

    def stores(held_ref, first):
        half = chips // 2
        return [
            pltpu.make_async_copy(
                held_ref.at[pl.ds((1 - place) * half, half)],
                outs[first + place],
                out_sems.at[first + place],
            )
            for place in range(2)
        ]

    for step in range(chips):
        for prefix in range(sought):
            start(step, prefix, owner_ref[prefix] % 2 == core)

    @pl.when(is_last == 1)
    def _():
        for step in range(chips):
            start(step, sought, core == 1)

    for step in range(chips):
        for prefix in range(sought):
            load(kept_ref, step, prefix).wait()
    start_all(stores(sought_ref, 0))

    @pl.when(is_last == 1)
    def _():
        for step in range(chips):
            load(kept_ref, step, sought).wait()

    start_all(stores(known_ref, 2))
    wait_all(stores(sought_ref, 0) + stores(known_ref, 2))


def multicast(prefix_cache, owners, readers, outgoing):
    replicas = lax.axis_size("replica")
    me = lax.axis_index("replica")
    half = replicas // 2
    chips = half // 2
    bits = chips.bit_length() - 1
    chip = me // 2 % chips
    side = me // half
    width = prefix_cache.shape[1]
    ids = jnp.arange(owners.shape[0], dtype=jnp.int32)
    known = jnp.sum(jnp.where(owners == replicas - 1, ids, 0))
    sought = jnp.where(ids[:-1] >= known, owners[1:], owners[:-1])
    orders = ([*range(1, bits), 0], [*range(bits)])

    split = prefix_cache.reshape(2, chips, -1, width)
    swapped, *outgoing = lax.optimization_barrier((swap_cores(prefix_cache), *outgoing))
    swapped = swapped.reshape(split.shape)
    rows = split.shape[2]
    shares = [
        jax.ShapeDtypeStruct((chips // 2, count, rows, width), split.dtype)
        for count in (owners.shape[0] - 1, 1)
    ]
    staged = pl.pallas_call(
        functools.partial(stage_kernel, orders),
        out_shape=(shares[0],) * 2 + (shares[1],) * 2,
        in_specs=[IN_SMEM] * 2 + [IN_HBM] * 2,
        out_specs=(IN_HBM,) * 4,
        scratch_shapes=[
            *[pltpu.VMEM((chips, *share.shape[1:]), split.dtype) for share in shares],
            pltpu.SemaphoreType.DMA((chips, owners.shape[0])),
            pltpu.SemaphoreType.DMA((4,)),
        ],
        compiler_params=COPY_PARAMS,
        name="stage_prefix",
    )(
        sought,
        jnp.stack([me % 2, chip, (me // 2 == replicas // 2 - 1).astype(jnp.int32)]),
        split,
        swapped,
    )

    def scatter(sent, kept, source, order, senders):
        for rank, bit in enumerate(order):
            pairs = [(i, i ^ (2 << bit)) for i in range(replicas) if senders(i, order[rank:])]
            passed = lax.ppermute(sent, "replica", pairs)
            away = (source >> bit ^ chip >> bit) & 1 == 1
            kept = jnp.where(away[None, :, None, None], passed, kept)
            left = kept.shape[0] // 2
            if left:
                kept, sent = kept[:left], kept[left:]
        return kept[0]

    def holds(i, ahead):
        return i >= half and all(i // 2 >> bit & 1 for bit in ahead)

    found = scatter(*staged[:2], sought // 2 % chips, orders[0], lambda i, ahead: True)
    passed = lax.ppermute(found, "replica", [(i, (i + half) % replicas) for i in range(replicas)])
    held = jnp.where((sought // half == side)[:, None, None], found, passed)
    last_chip = jnp.full((1,), chips - 1, jnp.int32)
    found = scatter(*staged[2:], last_chip, orders[1], holds)
    passed = lax.ppermute(found, "replica", [(i + half, i) for i in range(half)])
    held = jnp.concatenate([jnp.where(side == 1, found, passed), held])
    wanted = jnp.stack([readers[me], readers[me ^ 1]])
    return held, jnp.where(wanted == known, 0, wanted + (wanted < known)), outgoing


def swap_cores(rows):
    return lax.ppermute(rows, "replica", [(i, i ^ 1) for i in range(lax.axis_size("replica"))])


def gather(held, place):
    replicas = lax.axis_size("replica")
    chips = replicas // 4
    bits = chips.bit_length() - 1
    gathered = {0: held}
    for step in sorted(range(1, chips), key=lambda step: (step.bit_count(), step)):
        members = [bit for bit in range(bits) if step >> bit & 1]
        linked = [bit for bit in members if step >> ((bit - 1) % bits) & 1]
        last = min(linked or members)
        gathered[step] = lax.ppermute(
            gathered[step ^ 1 << last], "replica", [(i, i ^ (2 << last)) for i in range(replicas)]
        )
    parts = []
    for late in (False, True):
        pieces = [gathered[step] for step in gathered if (step.bit_count() > 1) == late]
        rows, width = pieces[0].shape[1:]
        spec = pl.BlockSpec((None, rows, width), lambda i, which: (which[1], 0, 0))
        picked = pl.pallas_call(
            pick_kernel,
            out_shape=jax.ShapeDtypeStruct((len(pieces) * rows, width), held.dtype),
            grid_spec=pltpu.PrefetchScalarGridSpec(
                num_scalar_prefetch=1,
                grid=(1,),
                in_specs=[spec] * len(pieces),
                out_specs=pl.BlockSpec((len(pieces) * rows, width), lambda i, which: (0, 0)),
            ),
            compiler_params=PARAMS,
            name="pick_other",
        )(place, *pieces)
        parts.append((pieces, swap_cores(picked)))
    return parts


def whole(shape):
    return pl.BlockSpec(shape, lambda *args: (0,) * len(shape))


def cost(rows, keys, size):
    return pl.CostEstimate(
        flops=12 * rows * keys * size, bytes_accessed=4 * keys * size, transcendentals=rows * keys
    )


def on_device(
    queries,
    suffix_kv,
    own_cache,
    ctx_len,
    prefix_cache,
    owners,
    readers,
    kv_pool,
    mig_target,
    mig_block,
    mig_count,
):
    replicas = lax.axis_size("replica")
    size = suffix_kv.shape[1] // 2
    tokens = queries.shape[0]
    heads = queries.shape[1] // size
    factor = size ** (-0.5) * LOG2E
    row_count = tokens * heads
    state = jax.ShapeDtypeStruct((size + ONE_ROWS + MAX_ROWS, row_count), jnp.float32)
    columns = queries.reshape(tokens, heads, size).transpose(2, 1, 0).reshape(size, row_count)

    def scratch(keys):
        return [
            pltpu.VMEM(state.shape, state.dtype),
            pltpu.VMEM((keys, size), jnp.bfloat16),
            pltpu.VMEM((size + ONE_ROWS, keys), jnp.bfloat16),
            pltpu.SemaphoreType.DMA,
        ]

    entries = mig_target.shape[1]
    rows = kv_pool.shape[1] // MOVED_PARTS
    part = jax.ShapeDtypeStruct((replicas, rows, kv_pool.shape[2]), kv_pool.dtype)
    outgoing = pl.pallas_call(
        pack_kernel,
        out_shape=(part,) * MOVED_PARTS,
        in_specs=[IN_SMEM] * 3 + [IN_HBM],
        out_specs=(IN_HBM,) * MOVED_PARTS,
        scratch_shapes=[
            pltpu.VMEM((entries, *kv_pool.shape[1:]), kv_pool.dtype),
            pltpu.VMEM(kv_pool.shape[1:], kv_pool.dtype),
            pltpu.SemaphoreType.DMA((entries,)),
            pltpu.SemaphoreType.DMA((MOVED_PARTS, entries)),
        ],
        compiler_params=COPY_PARAMS,
        name="pack_moved",
    )(mig_target, mig_block, mig_count, kv_pool)
    held, place, outgoing = multicast(prefix_cache, owners, readers, outgoing)

    def fold_moved(part, state_now):
        arrived = lax.all_to_all(part, "replica", split_axis=0, concat_axis=0, tiled=True)
        local = state_now is None
        group = min(replicas, max(1, CHUNK // rows))
        steps = replicas // group
        most = max(group * rows, own_cache.shape[0], tokens) if local else group * rows
        keys = replicas * rows + (tokens + own_cache.shape[0]) * local
        return pl.pallas_call(
            functools.partial(moved_kernel, factor, local, steps),
            out_shape=state,
            grid=(steps,),
            in_specs=[
                whole(columns.shape),
                whole(suffix_kv.shape),
                pl.BlockSpec((group, rows, 2 * size), lambda i: (i, 0, 0)),
                *([IN_SMEM, whole(own_cache.shape)] if local else [IN_HBM]),
            ],
            out_specs=IN_HBM,
            scratch_shapes=scratch(most),
            compiler_params=PARAMS,
            cost_estimate=cost(row_count, keys, size),
            name="moved_keys",
        )(columns, suffix_kv, arrived, *((ctx_len, own_cache) if local else (state_now,)))

    state_now = fold_moved(outgoing[0], None)
    held, state_now, *later = lax.optimization_barrier((held, state_now, *outgoing[1:]))
    for part in later:
        state_now = fold_moved(part, state_now)

    for last, (pieces, others) in enumerate(gather(held, place)):
        piece_rows = pieces[0].shape[1]
        keys = 2 * len(pieces) * piece_rows
        steps = max(1, keys // CHUNK)
        while keys % (steps * size):
            steps -= 1
        state_now = pl.pallas_call(
            functools.partial(prefix_kernel, factor, last, len(pieces) + 1, steps, tokens),
            out_shape=jax.ShapeDtypeStruct(queries.shape, queries.dtype) if last else state,
            grid_spec=pltpu.PrefetchScalarGridSpec(
                num_scalar_prefetch=1,
                grid=(steps,),
                in_specs=[
                    whole(columns.shape),
                    *[pl.BlockSpec((None, piece_rows, 2 * size), lambda i, which: (which[0], 0, 0))]
                    * len(pieces),
                    whole(others.shape),
                    IN_HBM,
                ],
                out_specs=whole(queries.shape) if last else IN_HBM,
                scratch_shapes=scratch(keys),
            ),
            compiler_params=PARAMS,
            cost_estimate=cost(row_count, keys, size),
            name="prefix_keys",
        )(place, columns, *pieces, others, state_now)
    return state_now


def solution(mesh):
    in_specs = (
        P(("groups", "replica"), None),
        P(("groups", "replica"), None),
        P(("groups", "replica"), None),
        P(("groups", "replica")),
        P(("groups", "replica"), None),
        P("groups"),
        P("groups"),
        P(("groups", "replica"), None, None),
        P(("groups", "replica"), None),
        P(("groups", "replica"), None),
        P(("groups", "replica")),
    )
    out_specs = P(("groups", "replica"), None)
    return jax.shard_map(
        on_device, mesh=mesh, in_specs=in_specs, out_specs=out_specs, check_vma=False
    )
```

```python
import functools

import jax
import jax.numpy as jnp
from jax import lax
from jax.experimental import pallas as pl
from jax.experimental.pallas import tpu as pltpu
from jax.sharding import PartitionSpec as P

LOG2E = 1.4426950408889634
DEAD_MARK = 1024.0
DEAD_ABOVE = 512.0
NEG = -1e30
CHUNK = 2048
PARAMS = pltpu.CompilerParams(vmem_limit_bytes=62 * 1024 * 1024)

IN_SMEM = pl.BlockSpec(memory_space=pltpu.SMEM)
IN_HBM = pl.BlockSpec(memory_space=pltpu.HBM)


def fold_keys(q_ref, max_ref, sums_ref, keys, values, factor, mask=None):
    heads, tokens, width = sums_ref.shape
    size = keys.shape[1]

    def score(head):
        scores = lax.dot_general(
            q_ref[:, head * size:(head + 1) * size],
            keys,
            (((1,), (1,)), ((), ())),
            preferred_element_type=jnp.float32,
        )
        return scores if mask is None else jnp.where(mask, scores, NEG)

    following = score(0)
    for head in range(heads):
        scores, following = following, score(head + 1) if head + 1 < heads else None
        old_max = max_ref[head]
        new_max = jnp.maximum(old_max, jnp.max(scores, axis=1, keepdims=True))
        shrink = jnp.exp2((old_max - new_max) * factor)
        weights = jnp.exp2((scores - jnp.tile(new_max, (1, keys.shape[0] // size))) * factor)
        max_ref[head] = new_max
        sums_ref[head] = sums_ref[head] * jnp.tile(shrink, (1, width // size)) + jnp.dot(
            weights.astype(jnp.bfloat16), values, preferred_element_type=jnp.float32
        )


def finish(sums_ref, out_ref):
    heads, tokens, width = sums_ref.shape
    size = width // 2
    for head in range(heads):
        out_ref[:, head * size:(head + 1) * size] = (
            sums_ref[head, :, :size] / sums_ref[head, :, size:]
        ).astype(out_ref.dtype)


def stage_rows(rows, place, keys_ref, values_ref):
    size = keys_ref.shape[1]
    here = pl.ds(place, rows.shape[0])
    keys_ref[here, :] = rows[:, :size]
    values_ref[here, :size] = rows[:, size:]
    values_ref[here, size:] = jnp.ones((rows.shape[0], size), jnp.bfloat16)


def stage_live(rows, live, suffix_ref, keys_ref, values_ref):
    size = suffix_ref.shape[1] // 2
    count = rows.shape[0]
    zeros = jnp.zeros((count, size), jnp.float32)
    spare = jnp.broadcast_to(suffix_ref[:1, :size].astype(jnp.float32), zeros.shape)
    keys_ref[:count, :] = jnp.where(live, rows[:, :size], spare).astype(jnp.bfloat16)
    values_ref[:count, :size] = jnp.where(live, rows[:, size:], zeros).astype(jnp.bfloat16)
    values_ref[:count, size:] = jnp.where(live, 1.0, zeros).astype(jnp.bfloat16)


def start_all(copies):
    for copy in copies:
        copy.start()


def wait_all(copies):
    for copy in copies:
        copy.wait()


def state_copies(state_here, state_there, sems):
    return [
        pltpu.make_async_copy(source, target, sems.at[place])
        for place, (source, target) in enumerate(zip(state_here, state_there))
    ]


def fold_local(
    factor, len_ref, q_ref, suffix_ref, own_ref, max_ref, sums_ref, keys_ref, values_ref
):
    size = suffix_ref.shape[1] // 2
    suffix = suffix_ref.shape[0]
    own = own_ref.shape[0]
    max_ref[...] = jnp.full(max_ref.shape, NEG, jnp.float32)
    sums_ref[...] = jnp.zeros(sums_ref.shape, jnp.float32)
    stage_rows(suffix_ref[...], 0, keys_ref, values_ref)
    causal = lax.broadcasted_iota(jnp.int32, (suffix, suffix), 1) <= lax.broadcasted_iota(
        jnp.int32, (suffix, suffix), 0
    )
    fold_keys(
        q_ref, max_ref, sums_ref, keys_ref[:suffix, :], values_ref[:suffix, :], factor, causal
    )
    live = lax.broadcasted_iota(jnp.int32, (own, size), 0) < len_ref[0]
    stage_live(own_ref[...].astype(jnp.float32), live, suffix_ref, keys_ref, values_ref)
    fold_keys(q_ref, max_ref, sums_ref, keys_ref[:own, :], values_ref[:own, :], factor)


def moved_kernel(factor, local, steps, *refs):
    q_ref, suffix_ref, kv_ref = refs[:3]
    state_out = refs[-7:-5]
    max_ref, sums_ref, keys_ref, values_ref, sems = refs[-5:]
    step = pl.program_id(0)

    if local:

        @pl.when(step == 0)
        def _():
            fold_local(factor, refs[3], q_ref, suffix_ref, refs[4], *refs[-5:-1])

    else:
        loads = state_copies(refs[3:5], (max_ref, sums_ref), sems)
        pl.when(step == 0)(lambda: start_all(loads))

    rows = kv_ref[...].reshape(-1, kv_ref.shape[-1]).astype(jnp.float32)
    count, size = rows.shape[0], rows.shape[1] // 2
    live = jnp.broadcast_to(rows[:, size:size + 1] < DEAD_ABOVE, (count, size))
    stage_live(rows, live, suffix_ref, keys_ref, values_ref)
    if not local:
        pl.when(step == 0)(lambda: wait_all(loads))
    fold_keys(q_ref, max_ref, sums_ref, keys_ref[:count, :], values_ref[:count, :], factor)

    @pl.when(step == steps - 1)
    def _():
        saves = state_copies((max_ref, sums_ref), state_out, sems)
        start_all(saves)
        wait_all(saves)


def prefix_kernel(factor, last, count, steps, which_ref, q_ref, *refs):
    pieces, refs = refs[:count], refs[count:]
    max_ref, sums_ref, keys_ref, values_ref, sems = refs[-5:]
    step = pl.program_id(0)
    chunk = keys_ref.shape[0] // steps

    @pl.when(step == 0)
    def _():
        loads = state_copies(refs[:2], (max_ref, sums_ref), sems)
        start_all(loads)
        place = 0
        for piece in pieces:
            stage_rows(piece[...], place, keys_ref, values_ref)
            place += piece.shape[0]
        wait_all(loads)

    rows = pl.ds(pl.multiple_of(step * chunk, keys_ref.shape[1]), chunk)
    fold_keys(q_ref, max_ref, sums_ref, keys_ref[rows, :], values_ref[rows, :], factor)

    @pl.when(step == steps - 1)
    def _():
        if last:
            finish(sums_ref, refs[2])
        else:
            saves = state_copies((max_ref, sums_ref), refs[2:4], sems)
            start_all(saves)
            wait_all(saves)


def pick_kernel(which_ref, *refs):
    pieces, out_ref = refs[:-1], refs[-1]
    for place, piece in enumerate(pieces):
        out_ref[pl.ds(place * piece.shape[0], piece.shape[0]), :] = piece[...]


def pack_kernel(target_ref, block_ref, count_ref, pool_ref, *refs):
    parts = refs[:-4]
    held_ref, mark_ref, in_sems, out_sems = refs[-4:]
    entries = target_ref.shape[1]
    mark_ref[...] = jnp.full(mark_ref.shape, DEAD_MARK, mark_ref.dtype)

    def load(entry):
        return pltpu.make_async_copy(
            pool_ref.at[block_ref[0, entry]], held_ref.at[entry], in_sems.at[entry]
        )

    def stores(entry, source):
        copies = []
        first = 0
        for place, part in enumerate(parts):
            rows = part.shape[1]
            copies.append(
                pltpu.make_async_copy(
                    source.at[pl.ds(first, rows)],
                    part.at[target_ref[0, entry]],
                    out_sems.at[place, entry],
                )
            )
            first += rows
        return copies

    @pl.loop(0, entries)
    def _(entry):
        live = entry < count_ref[0]
        pl.when(live)(lambda: load(entry).start())
        pl.when(jnp.logical_not(live))(lambda: start_all(stores(entry, mark_ref)))

    @pl.loop(0, entries)
    def _(entry):
        @pl.when(entry < count_ref[0])
        def _():
            load(entry).wait()
            start_all(stores(entry, held_ref.at[entry]))

    @pl.loop(0, entries)
    def _(entry):
        wait_all(stores(entry, mark_ref))


def placed(step, order):
    return sum((step >> bit & 1) << (len(order) - 1 - rank) for rank, bit in enumerate(order))


def stage_kernel(order, owner_ref, place_ref, kept_ref, swapped_ref, *refs):
    outs, (sought_ref, known_ref, in_sems, out_sems) = refs[:-4], refs[-4:]
    core, chip, is_last = place_ref[0], place_ref[1], place_ref[2]
    chips, sought = sought_ref.shape[:2]

    def load(source, step, prefix):
        if prefix < sought:
            target = sought_ref.at[step, prefix]
        else:
            target = known_ref.at[placed(step, order), 0]
        return pltpu.make_async_copy(source.at[core, chip ^ step], target, in_sems.at[step, prefix])

    def start(step, prefix, here):
        pl.when(here)(lambda: load(kept_ref, step, prefix).start())
        pl.when(jnp.logical_not(here))(lambda: load(swapped_ref, step, prefix).start())

    def store(place):
        half = chips // 2
        if place < chips:
            source = sought_ref.at[place]
        else:
            source = known_ref.at[pl.ds((chips + 1 - place) * half, half)]
        return pltpu.make_async_copy(source, outs[place], out_sems.at[place])

    for step in range(chips):
        for prefix in range(sought):
            start(step, prefix, owner_ref[prefix] % 2 == core)

    @pl.when(is_last == 1)
    def _():
        for step in range(chips):
            start(step, sought, core == 1)

    for step in range(chips):
        for prefix in range(sought):
            load(kept_ref, step, prefix).wait()
        store(step).start()

    @pl.when(is_last == 1)
    def _():
        for step in range(chips):
            load(kept_ref, step, sought).wait()

    store(chips).start()
    store(chips + 1).start()
    wait_all([store(place) for place in range(chips + 2)])


def multicast(prefix_cache, owners, readers, outgoing):
    replicas = lax.axis_size("replica")
    me = lax.axis_index("replica")
    half = replicas // 2
    chips = half // 2
    bits = chips.bit_length() - 1
    chip = me // 2 % chips
    side = me // half
    width = prefix_cache.shape[1]
    ids = jnp.arange(owners.shape[0], dtype=jnp.int32)
    known = jnp.sum(jnp.where(owners == replicas - 1, ids, 0))
    sought = jnp.where(ids[:-1] >= known, owners[1:], owners[:-1])
    order = [*range(bits)]

    split = prefix_cache.reshape(2, chips, -1, width)
    swapped, *outgoing = lax.optimization_barrier((swap_cores(prefix_cache), *outgoing))
    swapped = swapped.reshape(split.shape)
    rows = split.shape[2]
    pieces = jax.ShapeDtypeStruct((owners.shape[0] - 1, rows, width), split.dtype)
    share = jax.ShapeDtypeStruct((chips // 2, 1, rows, width), split.dtype)
    staged = pl.pallas_call(
        functools.partial(stage_kernel, order),
        out_shape=(pieces,) * chips + (share,) * 2,
        in_specs=[IN_SMEM] * 2 + [IN_HBM] * 2,
        out_specs=(IN_HBM,) * (chips + 2),
        scratch_shapes=[
            pltpu.VMEM((chips, *pieces.shape), split.dtype),
            pltpu.VMEM((chips, *share.shape[1:]), split.dtype),
            pltpu.SemaphoreType.DMA((chips, owners.shape[0])),
            pltpu.SemaphoreType.DMA((chips + 2,)),
        ],
        compiler_params=PARAMS,
        name="stage_prefix",
    )(
        sought,
        jnp.stack([me % 2, chip, (me // 2 == replicas // 2 - 1).astype(jnp.int32)]),
        split,
        swapped,
    )

    away = chip ^ (sought // 2 % chips)
    found = staged[0]
    for step in range(chips - 1, 0, -1):
        passed = lax.ppermute(
            staged[step], "replica", [(i, i ^ (2 * step)) for i in range(replicas)]
        )
        found = jnp.where((away == step)[:, None, None], passed, found)
    passed = lax.ppermute(found, "replica", [(i, (i + half) % replicas) for i in range(replicas)])
    held = jnp.where((sought // half == side)[:, None, None], found, passed)

    sent, kept = staged[chips:]
    for rank, bit in enumerate(order):
        senders = [
            i for i in range(half, replicas) if all(i // 2 >> ahead & 1 for ahead in order[rank:])
        ]
        passed = lax.ppermute(sent, "replica", [(i, i ^ (2 << bit)) for i in senders])
        kept = jnp.where(chip >> bit & 1 == 1, kept, passed)
        left = kept.shape[0] // 2
        if left:
            kept, sent = kept[:left], kept[left:]
    passed = lax.ppermute(kept[0], "replica", [(i + half, i) for i in range(half)])
    held = jnp.concatenate([jnp.where(side == 1, kept[0], passed), held])
    wanted = jnp.stack([readers[me], readers[me ^ 1]])
    return held, jnp.where(wanted == known, 0, wanted + (wanted < known)), outgoing


def swap_cores(rows):
    return lax.ppermute(rows, "replica", [(i, i ^ 1) for i in range(lax.axis_size("replica"))])


def gather_step(gathered, step):
    replicas = lax.axis_size("replica")
    bits = (replicas // 4).bit_length() - 1
    members = [bit for bit in range(bits) if step >> bit & 1]
    linked = [bit for bit in members if step >> ((bit - 1) % bits) & 1]
    last = min(linked or members)
    pairs = [(i, i ^ (2 << last)) for i in range(replicas)]
    return lax.ppermute(gathered[step ^ 1 << last], "replica", pairs)


def from_other(pieces, place):
    rows, width = pieces[0].shape[1:]
    spec = pl.BlockSpec((None, rows, width), lambda i, which: (which[1], 0, 0))
    picked = pl.pallas_call(
        pick_kernel,
        out_shape=jax.ShapeDtypeStruct((len(pieces) * rows, width), pieces[0].dtype),
        grid_spec=pltpu.PrefetchScalarGridSpec(
            num_scalar_prefetch=1,
            grid=(1,),
            in_specs=[spec] * len(pieces),
            out_specs=pl.BlockSpec((len(pieces) * rows, width), lambda i, which: (0, 0)),
        ),
        compiler_params=PARAMS,
        name="pick_other",
    )(place, *pieces)
    return swap_cores(picked)


def whole(shape):
    return pl.BlockSpec(shape, lambda *args: (0,) * len(shape))


def cost(rows, keys, size):
    return pl.CostEstimate(
        flops=12 * rows * keys * size, bytes_accessed=4 * keys * size, transcendentals=rows * keys
    )


def on_device(
    queries,
    suffix_kv,
    own_cache,
    ctx_len,
    prefix_cache,
    owners,
    readers,
    kv_pool,
    mig_target,
    mig_block,
    mig_count,
):
    replicas = lax.axis_size("replica")
    size = suffix_kv.shape[1] // 2
    tokens = queries.shape[0]
    heads = queries.shape[1] // size
    factor = size ** (-0.5) * LOG2E
    row_count = tokens * heads
    state = (
        jax.ShapeDtypeStruct((heads, tokens, size), jnp.float32),
        jax.ShapeDtypeStruct((heads, tokens, 2 * size), jnp.float32),
    )

    def scratch(keys):
        return [
            *[pltpu.VMEM(part.shape, part.dtype) for part in state],
            pltpu.VMEM((keys, size), jnp.bfloat16),
            pltpu.VMEM((keys, 2 * size), jnp.bfloat16),
            pltpu.SemaphoreType.DMA((2,)),
        ]

    entries = mig_target.shape[1]
    block = kv_pool.shape[1]
    early = block * 3 // 4
    parts = tuple(
        jax.ShapeDtypeStruct((replicas, rows, kv_pool.shape[2]), kv_pool.dtype)
        for rows in (early, block - early)
    )
    outgoing = pl.pallas_call(
        pack_kernel,
        out_shape=parts,
        in_specs=[IN_SMEM] * 3 + [IN_HBM],
        out_specs=(IN_HBM,) * len(parts),
        scratch_shapes=[
            pltpu.VMEM((entries, *kv_pool.shape[1:]), kv_pool.dtype),
            pltpu.VMEM(kv_pool.shape[1:], kv_pool.dtype),
            pltpu.SemaphoreType.DMA((entries,)),
            pltpu.SemaphoreType.DMA((len(parts), entries)),
        ],
        compiler_params=PARAMS,
        name="pack_moved",
    )(mig_target, mig_block, mig_count, kv_pool)
    held, place, outgoing = multicast(prefix_cache, owners, readers, outgoing)

    def fold_moved(part, state_now):
        arrived = lax.all_to_all(part, "replica", split_axis=0, concat_axis=0, tiled=True)
        local = state_now is None
        rows = part.shape[1]
        group = max(n for n in range(1, replicas + 1) if replicas % n == 0 and n * rows <= CHUNK)
        steps = replicas // group
        most = max(group * rows, own_cache.shape[0], tokens) if local else group * rows
        keys = replicas * rows + (tokens + own_cache.shape[0]) * local
        return pl.pallas_call(
            functools.partial(moved_kernel, factor, local, steps),
            out_shape=state,
            grid=(steps,),
            in_specs=[
                whole(queries.shape),
                whole(suffix_kv.shape),
                pl.BlockSpec((group, rows, 2 * size), lambda i: (i, 0, 0)),
                *([IN_SMEM, whole(own_cache.shape)] if local else [IN_HBM] * 2),
            ],
            out_specs=(IN_HBM,) * 2,
            scratch_shapes=scratch(most),
            compiler_params=PARAMS,
            cost_estimate=cost(row_count, keys, size),
            name="moved_keys",
        )(queries, suffix_kv, arrived, *((ctx_len, own_cache) if local else state_now))

    def fold_prefix(pieces, state_now, last):
        others = from_other(pieces, place)
        rows = pieces[0].shape[1]
        keys = 2 * len(pieces) * rows
        steps = max(1, keys // CHUNK)
        while keys % (steps * size):
            steps -= 1
        return pl.pallas_call(
            functools.partial(prefix_kernel, factor, last, len(pieces) + 1, steps),
            out_shape=jax.ShapeDtypeStruct(queries.shape, queries.dtype) if last else state,
            grid_spec=pltpu.PrefetchScalarGridSpec(
                num_scalar_prefetch=1,
                grid=(steps,),
                in_specs=[
                    whole(queries.shape),
                    *[pl.BlockSpec((None, rows, 2 * size), lambda i, which: (which[0], 0, 0))]
                    * len(pieces),
                    whole(others.shape),
                    IN_HBM,
                    IN_HBM,
                ],
                out_specs=whole(queries.shape) if last else (IN_HBM, IN_HBM),
                scratch_shapes=scratch(keys),
            ),
            compiler_params=PARAMS,
            cost_estimate=cost(row_count, keys, size),
            name="prefix_keys",
        )(place, queries, *pieces, others, *state_now)

    state_now = fold_moved(outgoing[0], None)
    held, *later = lax.optimization_barrier((held, *outgoing[1:]))
    chips = replicas // 4
    gathered = {0: held}
    for step in (step for step in range(1, chips) if step.bit_count() == 1):
        gathered[step] = gather_step(gathered, step)
    state_now = fold_prefix(list(gathered.values()), state_now, False)
    late = sorted(
        (step for step in range(1, chips) if step.bit_count() > 1),
        key=lambda step: (step.bit_count(), step),
    )
    for step in late:
        if step == late[-1]:
            source, *state_now = lax.optimization_barrier((gathered, *state_now))
        else:
            source = gathered
        gathered[step] = gather_step(source, step)
    for part in later:
        state_now = fold_moved(part, state_now)
    return fold_prefix([gathered[step] for step in late], state_now, True)


def solution(mesh):
    in_specs = (
        P(("groups", "replica"), None),
        P(("groups", "replica"), None),
        P(("groups", "replica"), None),
        P(("groups", "replica")),
        P(("groups", "replica"), None),
        P("groups"),
        P("groups"),
        P(("groups", "replica"), None, None),
        P(("groups", "replica"), None),
        P(("groups", "replica"), None),
        P(("groups", "replica")),
    )
    out_specs = P(("groups", "replica"), None)
    return jax.shard_map(
        on_device, mesh=mesh, in_specs=in_specs, out_specs=out_specs, check_vma=False
    )
```

```python
import functools

import jax
import jax.numpy as jnp
from jax import lax
from jax.experimental import pallas as pl
from jax.experimental.pallas import tpu as pltpu
from jax.sharding import PartitionSpec as P

LOG2E = 1.4426950408889634
DEAD_MARK = 1024.0
DEAD_ABOVE = 512.0
NEG = -1e30
CHUNK = 1024
ROWS = 512
PARAMS = pltpu.CompilerParams(vmem_limit_bytes=44 * 1024 * 1024)
COPY_PARAMS = pltpu.CompilerParams(vmem_limit_bytes=60 * 1024 * 1024)

IN_SMEM = pl.BlockSpec(memory_space=pltpu.SMEM)
IN_HBM = pl.BlockSpec(memory_space=pltpu.HBM)


def fold_keys(work, keys, values, factor, mask=None):
    q_ref, max_ref, sums_ref = work
    count, width = sums_ref.shape
    size = keys.shape[1]
    block = min(ROWS, count)

    def score(first):
        scores = lax.dot_general(
            q_ref[first:first + block, :],
            keys,
            (((1,), (1,)), ((), ())),
            preferred_element_type=jnp.float32,
        )
        return scores if mask is None else jnp.where(mask, scores, NEG)

    following = score(0)
    for first in range(0, count, block):
        here = slice(first, first + block)
        scores, following = following, score(first + block) if first + block < count else None
        old_max = max_ref[here]
        new_max = jnp.maximum(old_max, jnp.max(scores, axis=1, keepdims=True))
        shrink = jnp.exp2((old_max - new_max) * factor)
        weights = jnp.exp2((scores - jnp.tile(new_max, (1, keys.shape[0] // size))) * factor)
        max_ref[here] = new_max
        sums_ref[here] = sums_ref[here] * jnp.tile(shrink, (1, width // size)) + jnp.dot(
            weights.astype(jnp.bfloat16), values, preferred_element_type=jnp.float32
        )


def stack_queries(q_ref, stacked_ref):
    tokens, width = q_ref.shape
    size = stacked_ref.shape[1]
    for head in range(width // size):
        stacked_ref[head * tokens:(head + 1) * tokens, :] = q_ref[:, head * size:(head + 1) * size]


def load_state(loaded_ref, max_ref, sums_ref):
    count, size = max_ref.shape
    sums_ref[:, :size] = loaded_ref[0]
    sums_ref[:, size:] = jnp.broadcast_to(loaded_ref[1, :, :1], (count, size))
    max_ref[...] = jnp.broadcast_to(loaded_ref[1, :, size - 1:], (count, size))


def save_state(max_ref, sums_ref, saved_ref):
    count, size = max_ref.shape
    left = lax.broadcasted_iota(jnp.int32, (count, size), 1) < size // 2
    saved_ref[0] = sums_ref[:, :size]
    saved_ref[1] = jnp.where(left, sums_ref[:, size:], max_ref[...])


def finish(sums_ref, out_ref):
    tokens = out_ref.shape[0]
    size = sums_ref.shape[1] // 2
    for head in range(out_ref.shape[1] // size):
        here = slice(head * tokens, (head + 1) * tokens)
        out_ref[:, head * size:(head + 1) * size] = (
            sums_ref[here, :size] / sums_ref[here, size:]
        ).astype(out_ref.dtype)


def stage_rows(rows, place, keys_ref, values_ref):
    size = keys_ref.shape[1]
    here = pl.ds(place, rows.shape[0])
    keys_ref[here, :] = rows[:, :size]
    values_ref[here, :size] = rows[:, size:]
    values_ref[here, size:] = jnp.ones((rows.shape[0], size), jnp.bfloat16)


def stage_live(rows, live, suffix_ref, keys_ref, values_ref):
    size = suffix_ref.shape[1] // 2
    count = rows.shape[0]
    zeros = jnp.zeros((count, size), jnp.float32)
    spare = jnp.broadcast_to(suffix_ref[:1, :size].astype(jnp.float32), zeros.shape)
    keys_ref[:count, :] = jnp.where(live, rows[:, :size], spare).astype(jnp.bfloat16)
    values_ref[:count, :size] = jnp.where(live, rows[:, size:], zeros).astype(jnp.bfloat16)
    values_ref[:count, size:] = jnp.where(live, 1.0, zeros).astype(jnp.bfloat16)


def start_all(copies):
    for copy in copies:
        copy.start()


def wait_all(copies):
    for copy in copies:
        copy.wait()


def fold_local(factor, len_ref, suffix_ref, own_ref, work, keys_ref, values_ref):
    q_ref, max_ref, sums_ref = work
    size = suffix_ref.shape[1] // 2
    suffix = suffix_ref.shape[0]
    own = own_ref.shape[0]
    max_ref[...] = jnp.full(max_ref.shape, NEG, jnp.float32)
    sums_ref[...] = jnp.zeros(sums_ref.shape, jnp.float32)
    stage_rows(suffix_ref[...], 0, keys_ref, values_ref)
    block = min(ROWS, sums_ref.shape[0])
    token = lax.broadcasted_iota(jnp.int32, (block, suffix), 0) % suffix
    causal = lax.broadcasted_iota(jnp.int32, (block, suffix), 1) <= token
    fold_keys(work, keys_ref[:suffix, :], values_ref[:suffix, :], factor, causal)
    live = lax.broadcasted_iota(jnp.int32, (own, size), 0) < len_ref[0]
    stage_live(own_ref[...].astype(jnp.float32), live, suffix_ref, keys_ref, values_ref)
    fold_keys(work, keys_ref[:own, :], values_ref[:own, :], factor)


def moved_kernel(factor, local, steps, *refs):
    q_ref, suffix_ref, kv_ref = refs[:3]
    out_ref, *work, keys_ref, values_ref = refs[-6:]
    step = pl.program_id(0)

    @pl.when(step == 0)
    def _():
        stack_queries(q_ref, work[0])
        if local:
            fold_local(factor, refs[3], suffix_ref, refs[4], work, keys_ref, values_ref)
        else:
            load_state(refs[3], *work[1:])

    rows = kv_ref[...].reshape(-1, kv_ref.shape[-1]).astype(jnp.float32)
    count, size = rows.shape[0], rows.shape[1] // 2
    live = jnp.broadcast_to(rows[:, size:size + 1] < DEAD_ABOVE, (count, size))
    stage_live(rows, live, suffix_ref, keys_ref, values_ref)
    fold_keys(work, keys_ref[:count, :], values_ref[:count, :], factor)

    @pl.when(step == steps - 1)
    def _():
        if local:
            save_state(*work[1:], out_ref)
        else:
            finish(work[2], out_ref)


def prefix_kernel(factor, count, steps, which_ref, q_ref, *refs):
    pieces = refs[:count]
    loaded_ref, out_ref, *work, keys_ref, values_ref = refs[count:]
    step = pl.program_id(0)
    chunk = keys_ref.shape[0] // steps

    @pl.when(step == 0)
    def _():
        stack_queries(q_ref, work[0])
        place = 0
        for piece in pieces:
            stage_rows(piece[...], place, keys_ref, values_ref)
            place += piece.shape[0]
        load_state(loaded_ref, *work[1:])

    rows = pl.ds(pl.multiple_of(step * chunk, keys_ref.shape[1]), chunk)
    fold_keys(work, keys_ref[rows, :], values_ref[rows, :], factor)

    @pl.when(step == steps - 1)
    def _():
        save_state(*work[1:], out_ref)


def pick_kernel(which_ref, *refs):
    pieces, out_ref = refs[:-1], refs[-1]
    for place, piece in enumerate(pieces):
        out_ref[pl.ds(place * piece.shape[0], piece.shape[0]), :] = piece[...]


def pack_kernel(target_ref, block_ref, count_ref, pool_ref, *refs):
    parts = refs[:-4]
    held_ref, mark_ref, in_sems, out_sems = refs[-4:]
    entries = target_ref.shape[1]
    mark_ref[...] = jnp.full(mark_ref.shape, DEAD_MARK, mark_ref.dtype)

    def load(entry):
        return pltpu.make_async_copy(
            pool_ref.at[block_ref[0, entry]], held_ref.at[entry], in_sems.at[entry]
        )

    def stores(entry, source):
        copies = []
        first = 0
        for place, part in enumerate(parts):
            rows = part.shape[1]
            copies.append(
                pltpu.make_async_copy(
                    source.at[pl.ds(first, rows)],
                    part.at[target_ref[0, entry]],
                    out_sems.at[place, entry],
                )
            )
            first += rows
        return copies

    @pl.loop(0, entries)
    def _(entry):
        live = entry < count_ref[0]
        pl.when(live)(lambda: load(entry).start())
        pl.when(jnp.logical_not(live))(lambda: start_all(stores(entry, mark_ref)))

    @pl.loop(0, entries)
    def _(entry):
        @pl.when(entry < count_ref[0])
        def _():
            load(entry).wait()
            start_all(stores(entry, held_ref.at[entry]))

    @pl.loop(0, entries)
    def _(entry):
        wait_all(stores(entry, mark_ref))


def placed(step, order):
    return sum((step >> bit & 1) << (len(order) - 1 - rank) for rank, bit in enumerate(order))


def stage_kernel(order, owner_ref, place_ref, kept_ref, swapped_ref, *refs):
    outs, (sought_ref, known_ref, in_sems, out_sems) = refs[:-4], refs[-4:]
    core, chip, is_last = place_ref[0], place_ref[1], place_ref[2]
    chips, sought = sought_ref.shape[:2]

    def load(source, step, prefix):
        if prefix < sought:
            target = sought_ref.at[step, prefix]
        else:
            target = known_ref.at[placed(step, order), 0]
        return pltpu.make_async_copy(source.at[core, chip ^ step], target, in_sems.at[step, prefix])

    def start(step, prefix, here):
        pl.when(here)(lambda: load(kept_ref, step, prefix).start())
        pl.when(jnp.logical_not(here))(lambda: load(swapped_ref, step, prefix).start())

    def store(place):
        half = chips // 2
        if place < chips:
            source = sought_ref.at[place]
        else:
            source = known_ref.at[pl.ds((chips + 1 - place) * half, half)]
        return pltpu.make_async_copy(source, outs[place], out_sems.at[place])

    for step in range(chips):
        for prefix in range(sought):
            start(step, prefix, owner_ref[prefix] % 2 == core)

    @pl.when(is_last == 1)
    def _():
        for step in range(chips):
            start(step, sought, core == 1)

    for step in range(chips):
        for prefix in range(sought):
            load(kept_ref, step, prefix).wait()
        store(step).start()

    @pl.when(is_last == 1)
    def _():
        for step in range(chips):
            load(kept_ref, step, sought).wait()

    store(chips).start()
    store(chips + 1).start()
    wait_all([store(place) for place in range(chips + 2)])


def multicast(prefix_cache, owners, readers, outgoing):
    replicas = lax.axis_size("replica")
    me = lax.axis_index("replica")
    half = replicas // 2
    chips = half // 2
    bits = chips.bit_length() - 1
    chip = me // 2 % chips
    side = me // half
    width = prefix_cache.shape[1]
    ids = jnp.arange(owners.shape[0], dtype=jnp.int32)
    known = jnp.sum(jnp.where(owners == replicas - 1, ids, 0))
    sought = jnp.where(ids[:-1] >= known, owners[1:], owners[:-1])
    order = [*range(bits)]

    split = prefix_cache.reshape(2, chips, -1, width)
    swapped, *outgoing = lax.optimization_barrier((swap_cores(prefix_cache), *outgoing))
    swapped = swapped.reshape(split.shape)
    rows = split.shape[2]
    pieces = jax.ShapeDtypeStruct((owners.shape[0] - 1, rows, width), split.dtype)
    share = jax.ShapeDtypeStruct((chips // 2, 1, rows, width), split.dtype)
    staged = pl.pallas_call(
        functools.partial(stage_kernel, order),
        out_shape=(pieces,) * chips + (share,) * 2,
        in_specs=[IN_SMEM] * 2 + [IN_HBM] * 2,
        out_specs=(IN_HBM,) * (chips + 2),
        scratch_shapes=[
            pltpu.VMEM((chips, *pieces.shape), split.dtype),
            pltpu.VMEM((chips, *share.shape[1:]), split.dtype),
            pltpu.SemaphoreType.DMA((chips, owners.shape[0])),
            pltpu.SemaphoreType.DMA((chips + 2,)),
        ],
        compiler_params=COPY_PARAMS,
        name="stage_prefix",
    )(
        sought,
        jnp.stack([me % 2, chip, (me // 2 == replicas // 2 - 1).astype(jnp.int32)]),
        split,
        swapped,
    )

    away = chip ^ (sought // 2 % chips)
    found = staged[0]
    for step in range(chips - 1, 0, -1):
        passed = lax.ppermute(
            staged[step], "replica", [(i, i ^ (2 * step)) for i in range(replicas)]
        )
        found = jnp.where((away == step)[:, None, None], passed, found)
    passed = lax.ppermute(found, "replica", [(i, (i + half) % replicas) for i in range(replicas)])
    held = jnp.where((sought // half == side)[:, None, None], found, passed)

    sent, kept = staged[chips:]
    for rank, bit in enumerate(order):
        senders = [
            i for i in range(half, replicas) if all(i // 2 >> ahead & 1 for ahead in order[rank:])
        ]
        passed = lax.ppermute(sent, "replica", [(i, i ^ (2 << bit)) for i in senders])
        kept = jnp.where(chip >> bit & 1 == 1, kept, passed)
        left = kept.shape[0] // 2
        if left:
            kept, sent = kept[:left], kept[left:]
    passed = lax.ppermute(kept[0], "replica", [(i + half, i) for i in range(half)])
    held = jnp.concatenate([jnp.where(side == 1, kept[0], passed), held])
    wanted = jnp.stack([readers[me], readers[me ^ 1]])
    return held, jnp.where(wanted == known, 0, wanted + (wanted < known)), outgoing


def swap_cores(rows):
    return lax.ppermute(rows, "replica", [(i, i ^ 1) for i in range(lax.axis_size("replica"))])


def gather_step(gathered, step):
    replicas = lax.axis_size("replica")
    bits = (replicas // 4).bit_length() - 1
    members = [bit for bit in range(bits) if step >> bit & 1]
    linked = [bit for bit in members if step >> ((bit - 1) % bits) & 1]
    last = min(linked or members)
    pairs = [(i, i ^ (2 << last)) for i in range(replicas)]
    return lax.ppermute(gathered[step ^ 1 << last], "replica", pairs)


def from_other(pieces, place):
    rows, width = pieces[0].shape[1:]
    spec = pl.BlockSpec((None, rows, width), lambda i, which: (which[1], 0, 0))
    picked = pl.pallas_call(
        pick_kernel,
        out_shape=jax.ShapeDtypeStruct((len(pieces) * rows, width), pieces[0].dtype),
        grid_spec=pltpu.PrefetchScalarGridSpec(
            num_scalar_prefetch=1,
            grid=(1,),
            in_specs=[spec] * len(pieces),
            out_specs=pl.BlockSpec((len(pieces) * rows, width), lambda i, which: (0, 0)),
        ),
        compiler_params=PARAMS,
        name="pick_other",
    )(place, *pieces)
    return swap_cores(picked)


def whole(shape):
    return pl.BlockSpec(shape, lambda *args: (0,) * len(shape))


def cost(rows, keys, size):
    return pl.CostEstimate(
        flops=12 * rows * keys * size, bytes_accessed=4 * keys * size, transcendentals=rows * keys
    )


def on_device(
    queries,
    suffix_kv,
    own_cache,
    ctx_len,
    prefix_cache,
    owners,
    readers,
    kv_pool,
    mig_target,
    mig_block,
    mig_count,
):
    replicas = lax.axis_size("replica")
    size = suffix_kv.shape[1] // 2
    tokens = queries.shape[0]
    heads = queries.shape[1] // size
    factor = size ** (-0.5) * LOG2E
    row_count = tokens * heads
    state = jax.ShapeDtypeStruct((2, row_count, size), jnp.float32)
    result = jax.ShapeDtypeStruct(queries.shape, queries.dtype)

    def scratch(keys):
        return [
            pltpu.VMEM((row_count, size), queries.dtype),
            pltpu.VMEM((row_count, size), jnp.float32),
            pltpu.VMEM((row_count, 2 * size), jnp.float32),
            pltpu.VMEM((keys, size), jnp.bfloat16),
            pltpu.VMEM((keys, 2 * size), jnp.bfloat16),
        ]

    entries = mig_target.shape[1]
    block = kv_pool.shape[1]
    early = block // 2
    parts = tuple(
        jax.ShapeDtypeStruct((replicas, rows, kv_pool.shape[2]), kv_pool.dtype)
        for rows in (early, block - early)
    )
    outgoing = pl.pallas_call(
        pack_kernel,
        out_shape=parts,
        in_specs=[IN_SMEM] * 3 + [IN_HBM],
        out_specs=(IN_HBM,) * len(parts),
        scratch_shapes=[
            pltpu.VMEM((entries, *kv_pool.shape[1:]), kv_pool.dtype),
            pltpu.VMEM(kv_pool.shape[1:], kv_pool.dtype),
            pltpu.SemaphoreType.DMA((entries,)),
            pltpu.SemaphoreType.DMA((len(parts), entries)),
        ],
        compiler_params=COPY_PARAMS,
        name="pack_moved",
    )(mig_target, mig_block, mig_count, kv_pool)
    held, place, outgoing = multicast(prefix_cache, owners, readers, outgoing)

    def fold_moved(part, state_now):
        arrived = lax.all_to_all(part, "replica", split_axis=0, concat_axis=0, tiled=True)
        local = state_now is None
        rows = part.shape[1]
        group = max(n for n in range(1, replicas + 1) if replicas % n == 0 and n * rows <= CHUNK)
        steps = replicas // group
        most = max(group * rows, own_cache.shape[0], tokens) if local else group * rows
        keys = replicas * rows + (tokens + own_cache.shape[0]) * local
        return pl.pallas_call(
            functools.partial(moved_kernel, factor, local, steps),
            out_shape=state if local else result,
            grid=(steps,),
            in_specs=[
                whole(queries.shape),
                whole(suffix_kv.shape),
                pl.BlockSpec((group, rows, 2 * size), lambda i: (i, 0, 0)),
                *([IN_SMEM, whole(own_cache.shape)] if local else [whole(state.shape)]),
            ],
            out_specs=whole(state.shape if local else queries.shape),
            scratch_shapes=scratch(most),
            compiler_params=PARAMS,
            cost_estimate=cost(row_count, keys, size),
            name="moved_keys",
        )(queries, suffix_kv, arrived, *((ctx_len, own_cache) if local else (state_now,)))

    def fold_prefix(gathered, state_now):
        near = [gathered[step] for step in gathered if step.bit_count() < 2]
        far = [gathered[step] for step in gathered if step.bit_count() > 1]
        others = [from_other(near, place), from_other(far, place)]
        rows = near[0].shape[1]
        keys = 2 * len(gathered) * rows
        steps = max(1, keys // CHUNK)
        while keys % (steps * size):
            steps -= 1
        return pl.pallas_call(
            functools.partial(prefix_kernel, factor, len(gathered) + 2, steps),
            out_shape=state,
            grid_spec=pltpu.PrefetchScalarGridSpec(
                num_scalar_prefetch=1,
                grid=(steps,),
                in_specs=[
                    whole(queries.shape),
                    *[pl.BlockSpec((None, rows, 2 * size), lambda i, which: (which[0], 0, 0))]
                    * len(gathered),
                    *[whole(part.shape) for part in others],
                    whole(state.shape),
                ],
                out_specs=whole(state.shape),
                scratch_shapes=scratch(keys),
            ),
            compiler_params=PARAMS,
            cost_estimate=cost(row_count, keys, size),
            name="prefix_keys",
        )(place, queries, *near, *far, *others, state_now)

    state_now = fold_moved(outgoing[0], None)
    gathered = {0: held}
    for step in sorted(range(1, replicas // 4), key=lambda step: (step.bit_count(), step)):
        gathered[step] = gather_step(gathered, step)
    gathered[1], last_part = lax.optimization_barrier((gathered[1], outgoing[1]))
    return fold_moved(last_part, fold_prefix(gathered, state_now))


def solution(mesh):
    in_specs = (
        P(("groups", "replica"), None),
        P(("groups", "replica"), None),
        P(("groups", "replica"), None),
        P(("groups", "replica")),
        P(("groups", "replica"), None),
        P("groups"),
        P("groups"),
        P(("groups", "replica"), None, None),
        P(("groups", "replica"), None),
        P(("groups", "replica"), None),
        P(("groups", "replica")),
    )
    out_specs = P(("groups", "replica"), None)
    return jax.shard_map(
        on_device, mesh=mesh, in_specs=in_specs, out_specs=out_specs, check_vma=False
    )
```

```python
import functools

import jax
import jax.numpy as jnp
from jax import lax
from jax.experimental import pallas as pl
from jax.experimental.pallas import tpu as pltpu
from jax.sharding import PartitionSpec as P

LOG2E = 1.4426950408889634
DEAD_MARK = 1024.0
DEAD_ABOVE = 512.0
NEG = -1e30
CHUNK = 1024
ROWS = 512
PARAMS = pltpu.CompilerParams(vmem_limit_bytes=44 * 1024 * 1024)
COPY_PARAMS = pltpu.CompilerParams(vmem_limit_bytes=60 * 1024 * 1024)

IN_SMEM = pl.BlockSpec(memory_space=pltpu.SMEM)
IN_HBM = pl.BlockSpec(memory_space=pltpu.HBM)


def fold_keys(work, keys, values, factor, mask=None):
    q_ref, max_ref, sums_ref = work
    count, width = sums_ref.shape
    size = keys.shape[1]
    block = min(ROWS, count)

    def score(first):
        scores = lax.dot_general(
            q_ref[first:first + block, :],
            keys,
            (((1,), (1,)), ((), ())),
            preferred_element_type=jnp.float32,
        )
        return scores if mask is None else jnp.where(mask, scores, NEG)

    following = score(0)
    for first in range(0, count, block):
        here = slice(first, first + block)
        scores, following = following, score(first + block) if first + block < count else None
        old_max = max_ref[here]
        new_max = jnp.maximum(old_max, jnp.max(scores, axis=1, keepdims=True))
        shrink = jnp.exp2((old_max - new_max) * factor)
        weights = jnp.exp2((scores - jnp.tile(new_max, (1, keys.shape[0] // size))) * factor)
        max_ref[here] = new_max
        sums_ref[here] = sums_ref[here] * jnp.tile(shrink, (1, width // size)) + jnp.dot(
            weights.astype(jnp.bfloat16), values, preferred_element_type=jnp.float32
        )


def stack_queries(q_ref, stacked_ref):
    tokens, width = q_ref.shape
    size = stacked_ref.shape[1]
    for head in range(width // size):
        stacked_ref[head * tokens:(head + 1) * tokens, :] = q_ref[:, head * size:(head + 1) * size]


def load_state(loaded_ref, max_ref, sums_ref):
    count, size = max_ref.shape
    sums_ref[:, :size] = loaded_ref[0]
    sums_ref[:, size:] = jnp.broadcast_to(loaded_ref[1, :, :1], (count, size))
    max_ref[...] = jnp.broadcast_to(loaded_ref[1, :, size - 1:], (count, size))


def save_state(max_ref, sums_ref, saved_ref):
    count, size = max_ref.shape
    left = lax.broadcasted_iota(jnp.int32, (count, size), 1) < size // 2
    saved_ref[0] = sums_ref[:, :size]
    saved_ref[1] = jnp.where(left, sums_ref[:, size:], max_ref[...])


def finish(sums_ref, out_ref):
    tokens = out_ref.shape[0]
    size = sums_ref.shape[1] // 2
    for head in range(out_ref.shape[1] // size):
        here = slice(head * tokens, (head + 1) * tokens)
        out_ref[:, head * size:(head + 1) * size] = (
            sums_ref[here, :size] / sums_ref[here, size:]
        ).astype(out_ref.dtype)


def stage_rows(rows, place, keys_ref, values_ref):
    size = keys_ref.shape[1]
    here = pl.ds(place, rows.shape[0])
    keys_ref[here, :] = rows[:, :size]
    values_ref[here, :size] = rows[:, size:]
    values_ref[here, size:] = jnp.ones((rows.shape[0], size), jnp.bfloat16)


def stage_live(rows, live, suffix_ref, keys_ref, values_ref):
    size = suffix_ref.shape[1] // 2
    count = rows.shape[0]
    zeros = jnp.zeros((count, size), jnp.float32)
    spare = jnp.broadcast_to(suffix_ref[:1, :size].astype(jnp.float32), zeros.shape)
    keys_ref[:count, :] = jnp.where(live, rows[:, :size], spare).astype(jnp.bfloat16)
    values_ref[:count, :size] = jnp.where(live, rows[:, size:], zeros).astype(jnp.bfloat16)
    values_ref[:count, size:] = jnp.where(live, 1.0, zeros).astype(jnp.bfloat16)


def start_all(copies):
    for copy in copies:
        copy.start()


def wait_all(copies):
    for copy in copies:
        copy.wait()


def fold_local(factor, len_ref, suffix_ref, own_ref, work, keys_ref, values_ref):
    q_ref, max_ref, sums_ref = work
    size = suffix_ref.shape[1] // 2
    suffix = suffix_ref.shape[0]
    own = own_ref.shape[0]
    max_ref[...] = jnp.full(max_ref.shape, NEG, jnp.float32)
    sums_ref[...] = jnp.zeros(sums_ref.shape, jnp.float32)
    stage_rows(suffix_ref[...], 0, keys_ref, values_ref)
    block = min(ROWS, sums_ref.shape[0])
    token = lax.broadcasted_iota(jnp.int32, (block, suffix), 0) % suffix
    causal = lax.broadcasted_iota(jnp.int32, (block, suffix), 1) <= token
    fold_keys(work, keys_ref[:suffix, :], values_ref[:suffix, :], factor, causal)
    live = lax.broadcasted_iota(jnp.int32, (own, size), 0) < len_ref[0]
    stage_live(own_ref[...].astype(jnp.float32), live, suffix_ref, keys_ref, values_ref)
    fold_keys(work, keys_ref[:own, :], values_ref[:own, :], factor)


def moved_kernel(factor, local, steps, *refs):
    q_ref, suffix_ref, kv_ref = refs[:3]
    out_ref, *work, keys_ref, values_ref = refs[-6:]
    step = pl.program_id(0)

    @pl.when(step == 0)
    def _():
        stack_queries(q_ref, work[0])
        if local:
            fold_local(factor, refs[3], suffix_ref, refs[4], work, keys_ref, values_ref)
        else:
            load_state(refs[3], *work[1:])

    rows = kv_ref[...].reshape(-1, kv_ref.shape[-1]).astype(jnp.float32)
    count, size = rows.shape[0], rows.shape[1] // 2
    live = jnp.broadcast_to(rows[:, size:size + 1] < DEAD_ABOVE, (count, size))
    stage_live(rows, live, suffix_ref, keys_ref, values_ref)
    fold_keys(work, keys_ref[:count, :], values_ref[:count, :], factor)

    @pl.when(step == steps - 1)
    def _():
        save_state(*work[1:], out_ref)


def prefix_kernel(factor, count, steps, which_ref, q_ref, *refs):
    pieces = refs[:count]
    loaded_ref, out_ref, *work, keys_ref, values_ref = refs[count:]
    step = pl.program_id(0)
    chunk = keys_ref.shape[0] // steps

    @pl.when(step == 0)
    def _():
        stack_queries(q_ref, work[0])
        place = 0
        for piece in pieces:
            stage_rows(piece[...], place, keys_ref, values_ref)
            place += piece.shape[0]
        load_state(loaded_ref, *work[1:])

    rows = pl.ds(pl.multiple_of(step * chunk, keys_ref.shape[1]), chunk)
    fold_keys(work, keys_ref[rows, :], values_ref[rows, :], factor)

    @pl.when(step == steps - 1)
    def _():
        finish(work[2], out_ref)


def pick_kernel(which_ref, *refs):
    pieces, out_ref = refs[:-1], refs[-1]
    for place, piece in enumerate(pieces):
        out_ref[pl.ds(place * piece.shape[0], piece.shape[0]), :] = piece[...]


def pack_kernel(target_ref, block_ref, count_ref, pool_ref, *refs):
    parts = refs[:-4]
    held_ref, mark_ref, in_sems, out_sems = refs[-4:]
    entries = target_ref.shape[1]
    mark_ref[...] = jnp.full(mark_ref.shape, DEAD_MARK, mark_ref.dtype)

    def load(entry):
        return pltpu.make_async_copy(
            pool_ref.at[block_ref[0, entry]], held_ref.at[entry], in_sems.at[entry]
        )

    def stores(entry, source):
        copies = []
        first = 0
        for place, part in enumerate(parts):
            rows = part.shape[1]
            copies.append(
                pltpu.make_async_copy(
                    source.at[pl.ds(first, rows)],
                    part.at[target_ref[0, entry]],
                    out_sems.at[place, entry],
                )
            )
            first += rows
        return copies

    @pl.loop(0, entries)
    def _(entry):
        live = entry < count_ref[0]
        pl.when(live)(lambda: load(entry).start())
        pl.when(jnp.logical_not(live))(lambda: start_all(stores(entry, mark_ref)))

    @pl.loop(0, entries)
    def _(entry):
        @pl.when(entry < count_ref[0])
        def _():
            load(entry).wait()
            start_all(stores(entry, held_ref.at[entry]))

    @pl.loop(0, entries)
    def _(entry):
        wait_all(stores(entry, mark_ref))


def placed(step, order):
    return sum((step >> bit & 1) << (len(order) - 1 - rank) for rank, bit in enumerate(order))


def stage_kernel(order, owner_ref, place_ref, kept_ref, swapped_ref, *refs):
    outs, (sought_ref, known_ref, in_sems, out_sems) = refs[:-4], refs[-4:]
    core, chip, is_last = place_ref[0], place_ref[1], place_ref[2]
    chips, sought = sought_ref.shape[:2]

    def load(source, step, prefix):
        if prefix < sought:
            target = sought_ref.at[step, prefix]
        else:
            target = known_ref.at[placed(step, order), 0]
        return pltpu.make_async_copy(source.at[core, chip ^ step], target, in_sems.at[step, prefix])

    def start(step, prefix, here):
        pl.when(here)(lambda: load(kept_ref, step, prefix).start())
        pl.when(jnp.logical_not(here))(lambda: load(swapped_ref, step, prefix).start())

    def store(place):
        half = chips // 2
        if place < chips:
            source = sought_ref.at[place]
        else:
            source = known_ref.at[pl.ds((chips + 1 - place) * half, half)]
        return pltpu.make_async_copy(source, outs[place], out_sems.at[place])

    for step in range(chips):
        for prefix in range(sought):
            start(step, prefix, owner_ref[prefix] % 2 == core)

    @pl.when(is_last == 1)
    def _():
        for step in range(chips):
            start(step, sought, core == 1)

    for step in range(chips):
        for prefix in range(sought):
            load(kept_ref, step, prefix).wait()
        store(step).start()

    @pl.when(is_last == 1)
    def _():
        for step in range(chips):
            load(kept_ref, step, sought).wait()

    store(chips).start()
    store(chips + 1).start()
    wait_all([store(place) for place in range(chips + 2)])


def multicast(prefix_cache, owners, readers, outgoing, fold_first):
    replicas = lax.axis_size("replica")
    me = lax.axis_index("replica")
    half = replicas // 2
    chips = half // 2
    bits = chips.bit_length() - 1
    chip = me // 2 % chips
    side = me // half
    width = prefix_cache.shape[1]
    ids = jnp.arange(owners.shape[0], dtype=jnp.int32)
    known = jnp.sum(jnp.where(owners == replicas - 1, ids, 0))
    sought = jnp.where(ids[:-1] >= known, owners[1:], owners[:-1])
    order = [*range(bits)]

    split = prefix_cache.reshape(2, chips, -1, width)
    swapped, *outgoing = lax.optimization_barrier((swap_cores(prefix_cache), *outgoing))
    swapped = swapped.reshape(split.shape)
    rows = split.shape[2]
    pieces = jax.ShapeDtypeStruct((owners.shape[0] - 1, rows, width), split.dtype)
    share = jax.ShapeDtypeStruct((chips // 2, 1, rows, width), split.dtype)
    staged = pl.pallas_call(
        functools.partial(stage_kernel, order),
        out_shape=(pieces,) * chips + (share,) * 2,
        in_specs=[IN_SMEM] * 2 + [IN_HBM] * 2,
        out_specs=(IN_HBM,) * (chips + 2),
        scratch_shapes=[
            pltpu.VMEM((chips, *pieces.shape), split.dtype),
            pltpu.VMEM((chips, *share.shape[1:]), split.dtype),
            pltpu.SemaphoreType.DMA((chips, owners.shape[0])),
            pltpu.SemaphoreType.DMA((chips + 2,)),
        ],
        compiler_params=COPY_PARAMS,
        name="stage_prefix",
    )(
        sought,
        jnp.stack([me % 2, chip, (me // 2 == replicas // 2 - 1).astype(jnp.int32)]),
        split,
        swapped,
    )

    away = chip ^ (sought // 2 % chips)
    found = staged[0]
    for step in range(chips - 1, 0, -1):
        passed = lax.ppermute(
            staged[step], "replica", [(i, i ^ (2 * step)) for i in range(replicas)]
        )
        found = jnp.where((away == step)[:, None, None], passed, found)
    found, state_now = lax.optimization_barrier((found, fold_first(outgoing[0])))
    passed = lax.ppermute(found, "replica", [(i, (i + half) % replicas) for i in range(replicas)])
    held = jnp.where((sought // half == side)[:, None, None], found, passed)

    sent, kept = staged[chips:]
    for rank, bit in enumerate(order):
        senders = [
            i for i in range(half, replicas) if all(i // 2 >> ahead & 1 for ahead in order[rank:])
        ]
        passed = lax.ppermute(sent, "replica", [(i, i ^ (2 << bit)) for i in senders])
        kept = jnp.where(chip >> bit & 1 == 1, kept, passed)
        left = kept.shape[0] // 2
        if left:
            kept, sent = kept[:left], kept[left:]
    passed = lax.ppermute(kept[0], "replica", [(i + half, i) for i in range(half)])
    held = jnp.concatenate([jnp.where(side == 1, kept[0], passed), held])
    wanted = jnp.stack([readers[me], readers[me ^ 1]])
    place = jnp.where(wanted == known, 0, wanted + (wanted < known))
    held, last_part = lax.optimization_barrier((held, outgoing[1]))
    return held, place, state_now, last_part


def swap_cores(rows):
    return lax.ppermute(rows, "replica", [(i, i ^ 1) for i in range(lax.axis_size("replica"))])


def gather_step(gathered, step):
    replicas = lax.axis_size("replica")
    bits = (replicas // 4).bit_length() - 1
    members = [bit for bit in range(bits) if step >> bit & 1]
    linked = [bit for bit in members if step >> ((bit - 1) % bits) & 1]
    last = min(linked or members)
    pairs = [(i, i ^ (2 << last)) for i in range(replicas)]
    return lax.ppermute(gathered[step ^ 1 << last], "replica", pairs)


def from_other(pieces, place):
    rows, width = pieces[0].shape[1:]
    spec = pl.BlockSpec((None, rows, width), lambda i, which: (which[1], 0, 0))
    picked = pl.pallas_call(
        pick_kernel,
        out_shape=jax.ShapeDtypeStruct((len(pieces) * rows, width), pieces[0].dtype),
        grid_spec=pltpu.PrefetchScalarGridSpec(
            num_scalar_prefetch=1,
            grid=(1,),
            in_specs=[spec] * len(pieces),
            out_specs=pl.BlockSpec((len(pieces) * rows, width), lambda i, which: (0, 0)),
        ),
        compiler_params=PARAMS,
        name="pick_other",
    )(place, *pieces)
    return swap_cores(picked)


def whole(shape):
    return pl.BlockSpec(shape, lambda *args: (0,) * len(shape))


def cost(rows, keys, size):
    return pl.CostEstimate(
        flops=12 * rows * keys * size, bytes_accessed=4 * keys * size, transcendentals=rows * keys
    )


def on_device(
    queries,
    suffix_kv,
    own_cache,
    ctx_len,
    prefix_cache,
    owners,
    readers,
    kv_pool,
    mig_target,
    mig_block,
    mig_count,
):
    replicas = lax.axis_size("replica")
    size = suffix_kv.shape[1] // 2
    tokens = queries.shape[0]
    heads = queries.shape[1] // size
    factor = size ** (-0.5) * LOG2E
    row_count = tokens * heads
    state = jax.ShapeDtypeStruct((2, row_count, size), jnp.float32)
    result = jax.ShapeDtypeStruct(queries.shape, queries.dtype)

    def scratch(keys):
        return [
            pltpu.VMEM((row_count, size), queries.dtype),
            pltpu.VMEM((row_count, size), jnp.float32),
            pltpu.VMEM((row_count, 2 * size), jnp.float32),
            pltpu.VMEM((keys, size), jnp.bfloat16),
            pltpu.VMEM((keys, 2 * size), jnp.bfloat16),
        ]

    entries = mig_target.shape[1]
    block = kv_pool.shape[1]
    early = block // 2
    parts = tuple(
        jax.ShapeDtypeStruct((replicas, rows, kv_pool.shape[2]), kv_pool.dtype)
        for rows in (early, block - early)
    )
    outgoing = pl.pallas_call(
        pack_kernel,
        out_shape=parts,
        in_specs=[IN_SMEM] * 3 + [IN_HBM],
        out_specs=(IN_HBM,) * len(parts),
        scratch_shapes=[
            pltpu.VMEM((entries, *kv_pool.shape[1:]), kv_pool.dtype),
            pltpu.VMEM(kv_pool.shape[1:], kv_pool.dtype),
            pltpu.SemaphoreType.DMA((entries,)),
            pltpu.SemaphoreType.DMA((len(parts), entries)),
        ],
        compiler_params=COPY_PARAMS,
        name="pack_moved",
    )(mig_target, mig_block, mig_count, kv_pool)
    def fold_moved(part, state_now=None):
        arrived = lax.all_to_all(part, "replica", split_axis=0, concat_axis=0, tiled=True)
        local = state_now is None
        rows = part.shape[1]
        group = max(n for n in range(1, replicas + 1) if replicas % n == 0 and n * rows <= CHUNK)
        steps = replicas // group
        most = max(group * rows, own_cache.shape[0], tokens) if local else group * rows
        keys = replicas * rows + (tokens + own_cache.shape[0]) * local
        return pl.pallas_call(
            functools.partial(moved_kernel, factor, local, steps),
            out_shape=state,
            grid=(steps,),
            in_specs=[
                whole(queries.shape),
                whole(suffix_kv.shape),
                pl.BlockSpec((group, rows, 2 * size), lambda i: (i, 0, 0)),
                *([IN_SMEM, whole(own_cache.shape)] if local else [whole(state.shape)]),
            ],
            out_specs=whole(state.shape),
            scratch_shapes=scratch(most),
            compiler_params=PARAMS,
            cost_estimate=cost(row_count, keys, size),
            name="moved_keys",
        )(queries, suffix_kv, arrived, *((ctx_len, own_cache) if local else (state_now,)))

    def fold_prefix(gathered, place, state_now):
        near = [gathered[step] for step in gathered if step.bit_count() < 2]
        far = [gathered[step] for step in gathered if step.bit_count() > 1]
        others = [from_other(near, place), from_other(far, place)]
        rows = near[0].shape[1]
        keys = 2 * len(gathered) * rows
        steps = max(1, keys // CHUNK)
        while keys % (steps * size):
            steps -= 1
        return pl.pallas_call(
            functools.partial(prefix_kernel, factor, len(gathered) + 2, steps),
            out_shape=result,
            grid_spec=pltpu.PrefetchScalarGridSpec(
                num_scalar_prefetch=1,
                grid=(steps,),
                in_specs=[
                    whole(queries.shape),
                    *[pl.BlockSpec((None, rows, 2 * size), lambda i, which: (which[0], 0, 0))]
                    * len(gathered),
                    *[whole(part.shape) for part in others],
                    whole(state.shape),
                ],
                out_specs=whole(queries.shape),
                scratch_shapes=scratch(keys),
            ),
            compiler_params=PARAMS,
            cost_estimate=cost(row_count, keys, size),
            name="prefix_keys",
        )(place, queries, *near, *far, *others, state_now)

    held, place, state_now, last_part = multicast(
        prefix_cache, owners, readers, outgoing, fold_moved
    )
    gathered = {0: held}
    for step in sorted(range(1, replicas // 4), key=lambda step: (step.bit_count(), step)):
        gathered[step] = gather_step(gathered, step)
    return fold_prefix(gathered, place, fold_moved(last_part, state_now))


def solution(mesh):
    in_specs = (
        P(("groups", "replica"), None),
        P(("groups", "replica"), None),
        P(("groups", "replica"), None),
        P(("groups", "replica")),
        P(("groups", "replica"), None),
        P("groups"),
        P("groups"),
        P(("groups", "replica"), None, None),
        P(("groups", "replica"), None),
        P(("groups", "replica"), None),
        P(("groups", "replica")),
    )
    out_specs = P(("groups", "replica"), None)
    return jax.shard_map(
        on_device, mesh=mesh, in_specs=in_specs, out_specs=out_specs, check_vma=False
    )
```

```python
import functools

import jax
import jax.numpy as jnp
from jax import lax
from jax.experimental import pallas as pl
from jax.experimental.pallas import tpu as pltpu
from jax.sharding import PartitionSpec as P

LOG2E = 1.4426950408889634
DEAD_MARK = 1024.0
DEAD_ABOVE = 512.0
NEG = -1e30
CHUNK = 1024
ROWS = 512
PARAMS = pltpu.CompilerParams(vmem_limit_bytes=44 * 1024 * 1024)
COPY_PARAMS = pltpu.CompilerParams(vmem_limit_bytes=60 * 1024 * 1024)

IN_SMEM = pl.BlockSpec(memory_space=pltpu.SMEM)
IN_HBM = pl.BlockSpec(memory_space=pltpu.HBM)


def fold_keys(work, keys, values, factor, bias=None):
    q_ref, max_ref, lanes_ref, sums_ref = work
    count, size = sums_ref.shape
    block = min(ROWS, count)
    groups = keys.shape[0] // size

    def score(first):
        scores = lax.dot_general(
            q_ref[first:first + block, :],
            keys,
            (((1,), (1,)), ((), ())),
            preferred_element_type=jnp.float32,
        )
        return scores if bias is None else scores + bias

    following = score(0)
    for first in range(0, count, block):
        here = slice(first, first + block)
        scores, following = following, score(first + block) if first + block < count else None
        old_max = max_ref[here]
        new_max = jnp.maximum(old_max, jnp.max(scores, axis=1, keepdims=True))
        shrink = jnp.exp2((old_max - new_max) * factor)
        weights = jnp.exp2((scores - jnp.tile(new_max, (1, groups))) * factor)
        lanes = weights[:, :size]
        for group in range(1, groups):
            lanes += weights[:, group * size:(group + 1) * size]
        max_ref[here] = new_max
        lanes_ref[here] = lanes_ref[here] * shrink + lanes
        sums_ref[here] = sums_ref[here] * shrink + jnp.dot(
            weights.astype(jnp.bfloat16), values, preferred_element_type=jnp.float32
        )


def stack_queries(q_ref, stacked_ref):
    tokens, width = q_ref.shape
    size = stacked_ref.shape[1]
    for head in range(width // size):
        stacked_ref[head * tokens:(head + 1) * tokens, :] = q_ref[:, head * size:(head + 1) * size]


def load_state(loaded_ref, max_ref, lanes_ref, sums_ref):
    count, size = max_ref.shape
    lane = lax.broadcasted_iota(jnp.int32, (count, size), 1)
    sums_ref[...] = loaded_ref[0]
    lanes_ref[...] = jnp.where(lane == 0, loaded_ref[1], 0.0)
    max_ref[...] = jnp.broadcast_to(loaded_ref[1, :, size - 1:], (count, size))


def save_state(max_ref, lanes_ref, sums_ref, saved_ref):
    count, size = max_ref.shape
    left = lax.broadcasted_iota(jnp.int32, (count, size), 1) < size // 2
    saved_ref[0] = sums_ref[...]
    saved_ref[1] = jnp.where(left, jnp.sum(lanes_ref[...], axis=1, keepdims=True), max_ref[...])


def finish(lanes_ref, sums_ref, out_ref):
    tokens = out_ref.shape[0]
    size = sums_ref.shape[1]
    for head in range(out_ref.shape[1] // size):
        here = slice(head * tokens, (head + 1) * tokens)
        out_ref[:, head * size:(head + 1) * size] = (
            sums_ref[here] / jnp.sum(lanes_ref[here], axis=1, keepdims=True)
        ).astype(out_ref.dtype)


def local_kernel(factor, len_ref, q_ref, suffix_ref, own_ref, out_ref, *work):
    q_stacked, max_ref, lanes_ref, sums_ref = work
    size = sums_ref.shape[1]
    suffix, own = suffix_ref.shape[0], own_ref.shape[0]
    stack_queries(q_ref, q_stacked)
    max_ref[...] = jnp.full(max_ref.shape, NEG, jnp.float32)
    lanes_ref[...] = jnp.zeros(lanes_ref.shape, jnp.float32)
    sums_ref[...] = jnp.zeros(sums_ref.shape, jnp.float32)
    block = min(ROWS, sums_ref.shape[0])
    token = lax.broadcasted_iota(jnp.int32, (block, suffix), 0) % suffix
    key = lax.broadcasted_iota(jnp.int32, (block, suffix), 1)
    causal = jnp.where(key <= token, 0.0, NEG)
    fold_keys(work, suffix_ref[:, :size], suffix_ref[:, size:], factor, causal)
    dead = jnp.where(lax.broadcasted_iota(jnp.int32, (1, own), 1) < len_ref[0], 0.0, NEG)
    fold_keys(work, own_ref[:, :size], own_ref[:, size:], factor, dead)
    save_state(max_ref, lanes_ref, sums_ref, out_ref)


def moved_kernel(factor, steps, q_ref, kv_ref, loaded_ref, out_ref, *work):
    step = pl.program_id(0)
    size = work[3].shape[1]

    @pl.when(step == 0)
    def _():
        stack_queries(q_ref, work[0])
        load_state(loaded_ref, *work[1:])

    rows = kv_ref[...].reshape(-1, kv_ref.shape[-1])
    dead = jnp.where(rows[:, size:].astype(jnp.float32) > DEAD_ABOVE, NEG, 0.0).T[:1]
    fold_keys(work, rows[:, :size], rows[:, size:], factor, dead)

    @pl.when(step == steps - 1)
    def _():
        save_state(*work[1:], out_ref)


def prefix_kernel(factor, count, steps, which_ref, q_ref, *refs):
    pieces = refs[:count]
    loaded_ref, out_ref, *work, rows_ref = refs[count:]
    step = pl.program_id(0)
    size = work[3].shape[1]
    chunk = rows_ref.shape[0] // steps

    @pl.when(step == 0)
    def _():
        stack_queries(q_ref, work[0])
        place = 0
        for piece in pieces:
            rows_ref[pl.ds(place, piece.shape[0]), :] = piece[...]
            place += piece.shape[0]
        load_state(loaded_ref, *work[1:])

    rows = pl.ds(pl.multiple_of(step * chunk, size), chunk)
    fold_keys(work, rows_ref[rows, :size], rows_ref[rows, size:], factor)

    @pl.when(step == steps - 1)
    def _():
        finish(*work[2:], out_ref)


def wait_all(copies):
    for copy in copies:
        copy.wait()


def pick_kernel(which_ref, *refs):
    pieces, out_ref = refs[:-1], refs[-1]
    for place, piece in enumerate(pieces):
        out_ref[pl.ds(place * piece.shape[0], piece.shape[0]), :] = piece[...]


def pack_kernel(target_ref, block_ref, count_ref, pool_ref, out_ref, held_ref, mark_ref, *sems):
    in_sems, out_sems = sems
    entries = target_ref.shape[1]
    mark_ref[...] = jnp.full(mark_ref.shape, DEAD_MARK, mark_ref.dtype)

    def load(entry):
        return pltpu.make_async_copy(
            pool_ref.at[block_ref[0, entry]], held_ref.at[entry], in_sems.at[entry]
        )

    def store(entry, source):
        return pltpu.make_async_copy(
            source, out_ref.at[target_ref[0, entry]], out_sems.at[entry]
        )

    @pl.loop(0, entries)
    def _(entry):
        live = entry < count_ref[0]
        pl.when(live)(lambda: load(entry).start())
        pl.when(jnp.logical_not(live))(lambda: store(entry, mark_ref).start())

    @pl.loop(0, entries)
    def _(entry):
        @pl.when(entry < count_ref[0])
        def _():
            load(entry).wait()
            store(entry, held_ref.at[entry]).start()

    @pl.loop(0, entries)
    def _(entry):
        store(entry, mark_ref).wait()


def stage_kernel(owner_ref, place_ref, kept_ref, swapped_ref, *refs):
    outs, (sought_ref, known_ref, in_sems, out_sems) = refs[:-4], refs[-4:]
    core, chip, is_last = place_ref[0], place_ref[1], place_ref[2]
    chips, sought = sought_ref.shape[:2]

    def load(source, step, prefix):
        target = sought_ref.at[step, prefix] if prefix < sought else known_ref.at[step, 0]
        return pltpu.make_async_copy(source.at[core, chip ^ step], target, in_sems.at[step, prefix])

    def start(step, prefix, here):
        pl.when(here)(lambda: load(kept_ref, step, prefix).start())
        pl.when(jnp.logical_not(here))(lambda: load(swapped_ref, step, prefix).start())

    def store(place):
        source = sought_ref.at[place] if place < chips else known_ref.at[place - chips]
        return pltpu.make_async_copy(source, outs[place], out_sems.at[place])

    for step in range(chips):
        for prefix in range(sought):
            start(step, prefix, owner_ref[prefix] % 2 == core)

    @pl.when(is_last == 1)
    def _():
        for step in range(chips):
            start(step, sought, core == 1)

    for step in range(chips):
        for prefix in range(sought):
            load(kept_ref, step, prefix).wait()
        store(step).start()

    @pl.when(is_last == 1)
    def _():
        for step in range(chips):
            load(kept_ref, step, sought).wait()
            store(chips + step).start()
        wait_all([store(chips + step) for step in range(chips)])

    wait_all([store(step) for step in range(chips)])


def multicast(prefix_cache, owners, readers, outgoing, local):
    replicas = lax.axis_size("replica")
    me = lax.axis_index("replica")
    half = replicas // 2
    chips = half // 2
    chip = me // 2 % chips
    width = prefix_cache.shape[1]
    ids = jnp.arange(owners.shape[0], dtype=jnp.int32)
    known = jnp.sum(jnp.where(owners == replicas - 1, ids, 0))
    sought = jnp.where(ids[:-1] >= known, owners[1:], owners[:-1])

    split = prefix_cache.reshape(2, chips, -1, width)
    swapped, outgoing = lax.optimization_barrier((swap_cores(prefix_cache), outgoing))
    arrived = lax.all_to_all(outgoing, "replica", split_axis=0, concat_axis=0, tiled=True)
    swapped = swapped.reshape(split.shape)
    pieces = jax.ShapeDtypeStruct((owners.shape[0] - 1, *split.shape[2:]), split.dtype)
    piece = jax.ShapeDtypeStruct((1, *split.shape[2:]), split.dtype)
    staged = pl.pallas_call(
        stage_kernel,
        out_shape=(pieces,) * chips + (piece,) * chips,
        in_specs=[IN_SMEM] * 2 + [IN_HBM] * 2,
        out_specs=(IN_HBM,) * (2 * chips),
        scratch_shapes=[
            pltpu.VMEM((chips, *pieces.shape), split.dtype),
            pltpu.VMEM((chips, *piece.shape), split.dtype),
            pltpu.SemaphoreType.DMA((chips, owners.shape[0])),
            pltpu.SemaphoreType.DMA((2 * chips,)),
        ],
        compiler_params=COPY_PARAMS,
        name="stage_prefix",
    )(
        sought,
        jnp.stack([me % 2, chip, (me // 2 == replicas // 2 - 1).astype(jnp.int32)]),
        split,
        swapped,
    )

    def to_peers(staged, senders):
        return [
            lax.ppermute(rows, "replica", [(i, i ^ (2 * step)) for i in senders])
            for step, rows in enumerate(staged)
            if step
        ]

    def choose(own, passed, source):
        away = chip ^ source
        for step, rows in enumerate(passed, 1):
            own = jnp.where((away == step)[:, None, None], rows, own)
        return own

    passed = to_peers(staged[:chips], range(replicas))
    passed[0], local, *known_staged = lax.optimization_barrier((passed[0], local, *staged[chips:]))
    passed_known = to_peers(known_staged, (replicas - 2, replicas - 1))
    last_chip = jnp.full((1,), chips - 1, jnp.int32)
    found = jnp.concatenate(
        [
            choose(known_staged[0], passed_known, last_chip),
            choose(staged[0], passed, sought // 2 % chips),
        ]
    )
    source = jnp.concatenate([jnp.full((1,), replicas - 1, jnp.int32), sought])
    passed = lax.ppermute(found, "replica", [(i, (i + half) % replicas) for i in range(replicas)])
    held = jnp.where((source // half == me // half)[:, None, None], found, passed)
    wanted = jnp.stack([readers[me], readers[me ^ 1]])
    place = jnp.where(wanted == known, 0, wanted + (wanted < known))
    return held, place, local, arrived


def swap_cores(rows):
    return lax.ppermute(rows, "replica", [(i, i ^ 1) for i in range(lax.axis_size("replica"))])


def gather_step(gathered, step):
    replicas = lax.axis_size("replica")
    bits = (replicas // 4).bit_length() - 1
    members = [bit for bit in range(bits) if step >> bit & 1]
    linked = [bit for bit in members if step >> ((bit - 1) % bits) & 1]
    last = min(linked or members)
    pairs = [(i, i ^ (2 << last)) for i in range(replicas)]
    return lax.ppermute(gathered[step ^ 1 << last], "replica", pairs)


def from_other(pieces, place):
    rows, width = pieces[0].shape[1:]
    spec = pl.BlockSpec((None, rows, width), lambda i, which: (which[1], 0, 0))
    picked = pl.pallas_call(
        pick_kernel,
        out_shape=jax.ShapeDtypeStruct((len(pieces) * rows, width), pieces[0].dtype),
        grid_spec=pltpu.PrefetchScalarGridSpec(
            num_scalar_prefetch=1,
            grid=(1,),
            in_specs=[spec] * len(pieces),
            out_specs=pl.BlockSpec((len(pieces) * rows, width), lambda i, which: (0, 0)),
        ),
        compiler_params=PARAMS,
        name="pick_other",
    )(place, *pieces)
    return swap_cores(picked)


def whole(shape):
    return pl.BlockSpec(shape, lambda *args: (0,) * len(shape))


def cost(rows, keys, size):
    return pl.CostEstimate(
        flops=12 * rows * keys * size, bytes_accessed=4 * keys * size, transcendentals=rows * keys
    )


def on_device(
    queries,
    suffix_kv,
    own_cache,
    ctx_len,
    prefix_cache,
    owners,
    readers,
    kv_pool,
    mig_target,
    mig_block,
    mig_count,
):
    replicas = lax.axis_size("replica")
    size = suffix_kv.shape[1] // 2
    tokens = queries.shape[0]
    heads = queries.shape[1] // size
    factor = size ** (-0.5) * LOG2E
    row_count = tokens * heads
    state = jax.ShapeDtypeStruct((2, row_count, size), jnp.float32)
    result = jax.ShapeDtypeStruct(queries.shape, queries.dtype)

    work = [
        pltpu.VMEM((row_count, size), queries.dtype),
        *[pltpu.VMEM((row_count, size), jnp.float32)] * 3,
    ]

    entries = mig_target.shape[1]
    slots = jax.ShapeDtypeStruct((replicas, *kv_pool.shape[1:]), kv_pool.dtype)
    outgoing = pl.pallas_call(
        pack_kernel,
        out_shape=slots,
        in_specs=[IN_SMEM] * 3 + [IN_HBM],
        out_specs=IN_HBM,
        scratch_shapes=[
            pltpu.VMEM((entries, *kv_pool.shape[1:]), kv_pool.dtype),
            pltpu.VMEM(kv_pool.shape[1:], kv_pool.dtype),
            pltpu.SemaphoreType.DMA((entries,)),
            pltpu.SemaphoreType.DMA((entries,)),
        ],
        compiler_params=COPY_PARAMS,
        name="pack_moved",
    )(mig_target, mig_block, mig_count, kv_pool)
    local = pl.pallas_call(
        functools.partial(local_kernel, factor),
        out_shape=state,
        grid=(1,),
        in_specs=[IN_SMEM, whole(queries.shape), whole(suffix_kv.shape), whole(own_cache.shape)],
        out_specs=whole(state.shape),
        scratch_shapes=work,
        compiler_params=PARAMS,
        cost_estimate=cost(row_count, tokens + own_cache.shape[0], size),
        name="local_keys",
    )(ctx_len, queries, suffix_kv, own_cache)
    held, place, state_now, arrived = multicast(prefix_cache, owners, readers, outgoing, local)

    rows = arrived.shape[1]
    group = max(n for n in range(1, replicas + 1) if replicas % n == 0 and n * rows <= CHUNK)
    steps = max(1, replicas // group // 2)
    for first in range(0, replicas // group, steps):
        state_now = pl.pallas_call(
            functools.partial(moved_kernel, factor, steps),
            out_shape=state,
            grid=(steps,),
            in_specs=[
                whole(queries.shape),
                pl.BlockSpec((group, rows, 2 * size), lambda i, first=first: (first + i, 0, 0)),
                whole(state.shape),
            ],
            out_specs=whole(state.shape),
            scratch_shapes=work,
            compiler_params=PARAMS,
            cost_estimate=cost(row_count, steps * group * rows, size),
            name="moved_keys",
        )(queries, arrived, state_now)

    gathered = {0: held}
    for step in sorted(range(1, replicas // 4), key=lambda step: (step.bit_count(), step)):
        gathered[step] = gather_step(gathered, step)
    pieces = list(gathered.values())
    others = from_other(pieces, place)
    rows = held.shape[1]
    keys = 2 * len(pieces) * rows
    steps = max(1, keys // CHUNK)
    while keys % (steps * size):
        steps -= 1
    return pl.pallas_call(
        functools.partial(prefix_kernel, factor, len(pieces) + 1, steps),
        out_shape=result,
        grid_spec=pltpu.PrefetchScalarGridSpec(
            num_scalar_prefetch=1,
            grid=(steps,),
            in_specs=[
                whole(queries.shape),
                *[pl.BlockSpec((None, rows, 2 * size), lambda i, which: (which[0], 0, 0))]
                * len(pieces),
                whole(others.shape),
                whole(state.shape),
            ],
            out_specs=whole(queries.shape),
            scratch_shapes=[*work, pltpu.VMEM((keys, 2 * size), jnp.bfloat16)],
        ),
        compiler_params=PARAMS,
        cost_estimate=cost(row_count, keys, size),
        name="prefix_keys",
    )(place, queries, *pieces, others, state_now)


def solution(mesh):
    in_specs = (
        P(("groups", "replica"), None),
        P(("groups", "replica"), None),
        P(("groups", "replica"), None),
        P(("groups", "replica")),
        P(("groups", "replica"), None),
        P("groups"),
        P("groups"),
        P(("groups", "replica"), None, None),
        P(("groups", "replica"), None),
        P(("groups", "replica"), None),
        P(("groups", "replica")),
    )
    out_specs = P(("groups", "replica"), None)
    return jax.shard_map(
        on_device, mesh=mesh, in_specs=in_specs, out_specs=out_specs, check_vma=False
    )
```

```python
import functools

import jax
import jax.numpy as jnp
from jax import lax
from jax.experimental import pallas as pl
from jax.experimental.pallas import tpu as pltpu
from jax.sharding import PartitionSpec as P

LOG2E = 1.4426950408889634
DEAD_MARK = 1024.0
DEAD_ABOVE = 512.0
NEG = -1e30
CHUNK = 1024
ROWS = 512
PARAMS = pltpu.CompilerParams(vmem_limit_bytes=44 * 1024 * 1024)
COPY_PARAMS = pltpu.CompilerParams(vmem_limit_bytes=60 * 1024 * 1024)

IN_SMEM = pl.BlockSpec(memory_space=pltpu.SMEM)
IN_HBM = pl.BlockSpec(memory_space=pltpu.HBM)


def fold_keys(work, keys, values, factor, bias=None):
    q_ref, max_ref, lanes_ref, sums_ref = work
    count, size = sums_ref.shape
    block = min(ROWS, count)
    groups = keys.shape[0] // size

    def score(first):
        scores = lax.dot_general(
            q_ref[first:first + block, :],
            keys,
            (((1,), (1,)), ((), ())),
            preferred_element_type=jnp.float32,
        )
        return scores if bias is None else scores + bias

    following = score(0)
    for first in range(0, count, block):
        here = slice(first, first + block)
        scores, following = following, score(first + block) if first + block < count else None
        old_max = max_ref[here]
        new_max = jnp.maximum(old_max, jnp.max(scores, axis=1, keepdims=True))
        shrink = jnp.exp2((old_max - new_max) * factor)
        weights = jnp.exp2((scores - jnp.tile(new_max, (1, groups))) * factor)
        lanes = weights[:, :size]
        for group in range(1, groups):
            lanes += weights[:, group * size:(group + 1) * size]
        max_ref[here] = new_max
        lanes_ref[here] = lanes_ref[here] * shrink + lanes
        sums_ref[here] = sums_ref[here] * shrink + jnp.dot(
            weights.astype(jnp.bfloat16), values, preferred_element_type=jnp.float32
        )


def stack_queries(q_ref, stacked_ref):
    tokens, width = q_ref.shape
    size = stacked_ref.shape[1]
    for head in range(width // size):
        stacked_ref[head * tokens:(head + 1) * tokens, :] = q_ref[:, head * size:(head + 1) * size]


def load_state(loaded_ref, max_ref, lanes_ref, sums_ref):
    count, size = max_ref.shape
    lane = lax.broadcasted_iota(jnp.int32, (count, size), 1)
    sums_ref[...] = loaded_ref[0]
    lanes_ref[...] = jnp.where(lane == 0, loaded_ref[1], 0.0)
    max_ref[...] = jnp.broadcast_to(loaded_ref[1, :, size - 1:], (count, size))


def save_state(max_ref, lanes_ref, sums_ref, saved_ref):
    count, size = max_ref.shape
    left = lax.broadcasted_iota(jnp.int32, (count, size), 1) < size // 2
    saved_ref[0] = sums_ref[...]
    saved_ref[1] = jnp.where(left, jnp.sum(lanes_ref[...], axis=1, keepdims=True), max_ref[...])


def finish(lanes_ref, sums_ref, out_ref):
    tokens = out_ref.shape[0]
    size = sums_ref.shape[1]
    for head in range(out_ref.shape[1] // size):
        here = slice(head * tokens, (head + 1) * tokens)
        out_ref[:, head * size:(head + 1) * size] = (
            sums_ref[here] / jnp.sum(lanes_ref[here], axis=1, keepdims=True)
        ).astype(out_ref.dtype)


def local_kernel(factor, len_ref, q_ref, suffix_ref, own_ref, out_ref, *work):
    q_stacked, max_ref, lanes_ref, sums_ref = work
    size = sums_ref.shape[1]
    suffix, own = suffix_ref.shape[0], own_ref.shape[0]
    stack_queries(q_ref, q_stacked)
    max_ref[...] = jnp.full(max_ref.shape, NEG, jnp.float32)
    lanes_ref[...] = jnp.zeros(lanes_ref.shape, jnp.float32)
    sums_ref[...] = jnp.zeros(sums_ref.shape, jnp.float32)
    block = min(ROWS, sums_ref.shape[0])
    token = lax.broadcasted_iota(jnp.int32, (block, suffix), 0) % suffix
    key = lax.broadcasted_iota(jnp.int32, (block, suffix), 1)
    causal = jnp.where(key <= token, 0.0, NEG)
    fold_keys(work, suffix_ref[:, :size], suffix_ref[:, size:], factor, causal)
    dead = jnp.where(lax.broadcasted_iota(jnp.int32, (1, own), 1) < len_ref[0], 0.0, NEG)
    fold_keys(work, own_ref[:, :size], own_ref[:, size:], factor, dead)
    save_state(max_ref, lanes_ref, sums_ref, out_ref)


def moved_kernel(factor, steps, q_ref, kv_ref, loaded_ref, out_ref, *work):
    step = pl.program_id(0)
    size = work[3].shape[1]

    @pl.when(step == 0)
    def _():
        stack_queries(q_ref, work[0])
        load_state(loaded_ref, *work[1:])

    rows = kv_ref[...].reshape(-1, kv_ref.shape[-1])
    dead = jnp.where(rows[:, size:].astype(jnp.float32) > DEAD_ABOVE, NEG, 0.0).T[:1]
    fold_keys(work, rows[:, :size], rows[:, size:], factor, dead)

    @pl.when(step == steps - 1)
    def _():
        save_state(*work[1:], out_ref)


def prefix_kernel(factor, last, count, steps, which_ref, q_ref, *refs):
    pieces = refs[:count]
    loaded_ref, out_ref, *work, rows_ref = refs[count:]
    step = pl.program_id(0)
    size = work[3].shape[1]
    chunk = rows_ref.shape[0] // steps

    @pl.when(step == 0)
    def _():
        stack_queries(q_ref, work[0])
        place = 0
        for piece in pieces:
            rows_ref[pl.ds(place, piece.shape[0]), :] = piece[...]
            place += piece.shape[0]
        load_state(loaded_ref, *work[1:])

    rows = pl.ds(pl.multiple_of(step * chunk, size), chunk)
    fold_keys(work, rows_ref[rows, :size], rows_ref[rows, size:], factor)

    @pl.when(step == steps - 1)
    def _():
        if last:
            finish(*work[2:], out_ref)
        else:
            save_state(*work[1:], out_ref)


def wait_all(copies):
    for copy in copies:
        copy.wait()


def pick_kernel(which_ref, *refs):
    pieces, out_ref = refs[:-1], refs[-1]
    for place, piece in enumerate(pieces):
        out_ref[pl.ds(place * piece.shape[0], piece.shape[0]), :] = piece[...]


def pack_kernel(target_ref, block_ref, count_ref, pool_ref, out_ref, held_ref, mark_ref, *sems):
    in_sems, out_sems = sems
    entries = target_ref.shape[1]
    mark_ref[...] = jnp.full(mark_ref.shape, DEAD_MARK, mark_ref.dtype)

    def load(entry):
        return pltpu.make_async_copy(
            pool_ref.at[block_ref[0, entry]], held_ref.at[entry], in_sems.at[entry]
        )

    def store(entry, source):
        return pltpu.make_async_copy(
            source, out_ref.at[target_ref[0, entry]], out_sems.at[entry]
        )

    @pl.loop(0, entries)
    def _(entry):
        live = entry < count_ref[0]
        pl.when(live)(lambda: load(entry).start())
        pl.when(jnp.logical_not(live))(lambda: store(entry, mark_ref).start())

    @pl.loop(0, entries)
    def _(entry):
        @pl.when(entry < count_ref[0])
        def _():
            load(entry).wait()
            store(entry, held_ref.at[entry]).start()

    @pl.loop(0, entries)
    def _(entry):
        store(entry, mark_ref).wait()


def stage_kernel(owner_ref, kept_ref, swapped_ref, *refs):
    outs, (sought_ref, known_ref, in_sems, out_sems) = refs[:-4], refs[-4:]
    chips, sought = sought_ref.shape[:2]
    replicas = 4 * chips
    me = lax.axis_index("replica")
    core, chip, is_last = me % 2, me // 2 % chips, me // 2 == replicas // 2 - 1
    owners = [owner_ref[prefix] for prefix in range(sought + 1)]
    after = False
    for prefix in range(sought):
        after |= owners[prefix] == replicas - 1
        owners[prefix] = jnp.where(after, owners[prefix + 1], owners[prefix])

    def load(source, step, prefix):
        target = sought_ref.at[step, prefix] if prefix < sought else known_ref.at[step, 0]
        return pltpu.make_async_copy(source.at[core, chip ^ step], target, in_sems.at[step, prefix])

    def start(step, prefix, here):
        pl.when(here)(lambda: load(kept_ref, step, prefix).start())
        pl.when(jnp.logical_not(here))(lambda: load(swapped_ref, step, prefix).start())

    def store(place):
        source = sought_ref.at[place] if place < chips else known_ref.at[place - chips]
        return pltpu.make_async_copy(source, outs[place], out_sems.at[place])

    for step in range(chips):
        for prefix in range(sought):
            start(step, prefix, owners[prefix] % 2 == core)

    @pl.when(is_last)
    def _():
        for step in range(chips):
            start(step, sought, core == 1)

    for step in range(chips):
        for prefix in range(sought):
            load(kept_ref, step, prefix).wait()
        store(step).start()

    @pl.when(is_last)
    def _():
        for step in range(chips):
            load(kept_ref, step, sought).wait()
            store(chips + step).start()
        wait_all([store(chips + step) for step in range(chips)])

    wait_all([store(step) for step in range(chips)])


def multicast(prefix_cache, owners, readers, outgoing, local, fold_moved):
    replicas = lax.axis_size("replica")
    me = lax.axis_index("replica")
    half = replicas // 2
    chips = half // 2
    chip = me // 2 % chips
    width = prefix_cache.shape[1]
    ids = jnp.arange(owners.shape[0], dtype=jnp.int32)
    known = jnp.sum(jnp.where(owners == replicas - 1, ids, 0))
    sought = jnp.where(ids[:-1] >= known, owners[1:], owners[:-1])

    split = prefix_cache.reshape(2, chips, -1, width)
    swapped, outgoing = lax.optimization_barrier((swap_cores(prefix_cache), outgoing))
    arrived = lax.all_to_all(outgoing, "replica", split_axis=0, concat_axis=0, tiled=True)
    swapped = swapped.reshape(split.shape)
    pieces = jax.ShapeDtypeStruct((owners.shape[0] - 1, *split.shape[2:]), split.dtype)
    piece = jax.ShapeDtypeStruct((1, *split.shape[2:]), split.dtype)
    staged = pl.pallas_call(
        stage_kernel,
        out_shape=(pieces,) * chips + (piece,) * chips,
        in_specs=[IN_SMEM] + [IN_HBM] * 2,
        out_specs=(IN_HBM,) * (2 * chips),
        scratch_shapes=[
            pltpu.VMEM((chips, *pieces.shape), split.dtype),
            pltpu.VMEM((chips, *piece.shape), split.dtype),
            pltpu.SemaphoreType.DMA((chips, owners.shape[0])),
            pltpu.SemaphoreType.DMA((2 * chips,)),
        ],
        compiler_params=COPY_PARAMS,
        name="stage_prefix",
    )(owners, split, swapped)

    def to_peers(staged, senders):
        return [
            lax.ppermute(rows, "replica", [(i, i ^ (2 * step)) for i in senders])
            for step, rows in enumerate(staged)
            if step
        ]

    def choose(own, passed, source):
        away = chip ^ source
        for step, rows in enumerate(passed, 1):
            own = jnp.where((away == step)[:, None, None], rows, own)
        return own

    passed = to_peers(staged[:chips], range(replicas))
    wanted = jnp.stack([readers[me], readers[me ^ 1]])
    place = jnp.where(wanted == known, 0, wanted + (wanted < known))
    passed[0], local, place, *known_staged = lax.optimization_barrier(
        (passed[0], local, place, *staged[chips:])
    )
    passed_known = to_peers(known_staged, (replicas - 2, replicas - 1))
    last_chip = jnp.full((1,), chips - 1, jnp.int32)
    found = jnp.concatenate(
        [
            choose(known_staged[0], passed_known, last_chip),
            choose(staged[0], passed, sought // 2 % chips),
        ]
    )
    source = jnp.concatenate([jnp.full((1,), replicas - 1, jnp.int32), sought])
    passed = lax.ppermute(found, "replica", [(i, (i + half) % replicas) for i in range(replicas)])
    passed, state_now = lax.optimization_barrier((passed, fold_moved(arrived, local)))
    held = jnp.where((source // half == me // half)[:, None, None], found, passed)
    return held, place, state_now


def swap_cores(rows):
    return lax.ppermute(rows, "replica", [(i, i ^ 1) for i in range(lax.axis_size("replica"))])


def gather_step(gathered, step):
    replicas = lax.axis_size("replica")
    bits = (replicas // 4).bit_length() - 1
    members = [bit for bit in range(bits) if step >> bit & 1]
    linked = [bit for bit in members if step >> ((bit - 1) % bits) & 1]
    last = min(linked or members)
    pairs = [(i, i ^ (2 << last)) for i in range(replicas)]
    return lax.ppermute(gathered[step ^ 1 << last], "replica", pairs)


def from_other(pieces, place):
    rows, width = pieces[0].shape[1:]
    spec = pl.BlockSpec((None, rows, width), lambda i, which: (which[1], 0, 0))
    picked = pl.pallas_call(
        pick_kernel,
        out_shape=jax.ShapeDtypeStruct((len(pieces) * rows, width), pieces[0].dtype),
        grid_spec=pltpu.PrefetchScalarGridSpec(
            num_scalar_prefetch=1,
            grid=(1,),
            in_specs=[spec] * len(pieces),
            out_specs=pl.BlockSpec((len(pieces) * rows, width), lambda i, which: (0, 0)),
        ),
        compiler_params=PARAMS,
        name="pick_other",
    )(place, *pieces)
    return swap_cores(picked)


def whole(shape):
    return pl.BlockSpec(shape, lambda *args: (0,) * len(shape))


def cost(rows, keys, size):
    return pl.CostEstimate(
        flops=12 * rows * keys * size, bytes_accessed=4 * keys * size, transcendentals=rows * keys
    )


def on_device(
    queries,
    suffix_kv,
    own_cache,
    ctx_len,
    prefix_cache,
    owners,
    readers,
    kv_pool,
    mig_target,
    mig_block,
    mig_count,
):
    replicas = lax.axis_size("replica")
    size = suffix_kv.shape[1] // 2
    tokens = queries.shape[0]
    heads = queries.shape[1] // size
    factor = size ** (-0.5) * LOG2E
    row_count = tokens * heads
    state = jax.ShapeDtypeStruct((2, row_count, size), jnp.float32)
    result = jax.ShapeDtypeStruct(queries.shape, queries.dtype)

    work = [
        pltpu.VMEM((row_count, size), queries.dtype),
        *[pltpu.VMEM((row_count, size), jnp.float32)] * 3,
    ]

    entries = mig_target.shape[1]
    slots = jax.ShapeDtypeStruct((replicas, *kv_pool.shape[1:]), kv_pool.dtype)
    outgoing = pl.pallas_call(
        pack_kernel,
        out_shape=slots,
        in_specs=[IN_SMEM] * 3 + [IN_HBM],
        out_specs=IN_HBM,
        scratch_shapes=[
            pltpu.VMEM((entries, *kv_pool.shape[1:]), kv_pool.dtype),
            pltpu.VMEM(kv_pool.shape[1:], kv_pool.dtype),
            pltpu.SemaphoreType.DMA((entries,)),
            pltpu.SemaphoreType.DMA((entries,)),
        ],
        compiler_params=COPY_PARAMS,
        name="pack_moved",
    )(mig_target, mig_block, mig_count, kv_pool)
    local = pl.pallas_call(
        functools.partial(local_kernel, factor),
        out_shape=state,
        grid=(1,),
        in_specs=[IN_SMEM, whole(queries.shape), whole(suffix_kv.shape), whole(own_cache.shape)],
        out_specs=whole(state.shape),
        scratch_shapes=work,
        compiler_params=PARAMS,
        cost_estimate=cost(row_count, tokens + own_cache.shape[0], size),
        name="local_keys",
    )(ctx_len, queries, suffix_kv, own_cache)
    def fold_moved(arrived, state_now):
        rows = arrived.shape[1]
        group = max(n for n in range(1, replicas + 1) if replicas % n == 0 and n * rows <= CHUNK)
        steps = max(1, replicas // group // 2)
        for first in range(0, replicas // group, steps):
            state_now = pl.pallas_call(
                functools.partial(moved_kernel, factor, steps),
                out_shape=state,
                grid=(steps,),
                in_specs=[
                    whole(queries.shape),
                    pl.BlockSpec((group, rows, 2 * size), lambda i, first=first: (first + i, 0, 0)),
                    whole(state.shape),
                ],
                out_specs=whole(state.shape),
                scratch_shapes=work,
                compiler_params=PARAMS,
                cost_estimate=cost(row_count, steps * group * rows, size),
                name="moved_keys",
            )(queries, arrived, state_now)
        return state_now

    def fold_prefix(pieces, others, state_now, last):
        rows = pieces[0].shape[1]
        keys = 2 * len(pieces) * rows
        steps = max(1, keys // CHUNK)
        while keys % (steps * size):
            steps -= 1
        target = result if last else state
        return pl.pallas_call(
            functools.partial(prefix_kernel, factor, last, len(pieces) + 1, steps),
            out_shape=target,
            grid_spec=pltpu.PrefetchScalarGridSpec(
                num_scalar_prefetch=1,
                grid=(steps,),
                in_specs=[
                    whole(queries.shape),
                    *[pl.BlockSpec((None, rows, 2 * size), lambda i, which: (which[0], 0, 0))]
                    * len(pieces),
                    whole(others.shape),
                    whole(state.shape),
                ],
                out_specs=whole(target.shape),
                scratch_shapes=[*work, pltpu.VMEM((keys, 2 * size), jnp.bfloat16)],
            ),
            compiler_params=PARAMS,
            cost_estimate=cost(row_count, keys, size),
            name="prefix_keys",
        )(place, queries, *pieces, others, state_now)

    held, place, state_now = multicast(
        prefix_cache, owners, readers, outgoing, local, fold_moved
    )
    gathered = {0: held}
    steps = sorted(range(1, replicas // 4), key=lambda step: (step.bit_count(), step))
    for step in steps:
        gathered[step] = gather_step(gathered, step)
    near = [rows for step, rows in gathered.items() if step.bit_count() < 2]
    state_now = fold_prefix(near, from_other(near, place), state_now, False)
    gathered[steps[-1]], state_now = lax.optimization_barrier((gathered[steps[-1]], state_now))
    far = [rows for step, rows in gathered.items() if step.bit_count() > 1]
    return fold_prefix(far, from_other(far, place), state_now, True)


def solution(mesh):
    in_specs = (
        P(("groups", "replica"), None),
        P(("groups", "replica"), None),
        P(("groups", "replica"), None),
        P(("groups", "replica")),
        P(("groups", "replica"), None),
        P("groups"),
        P("groups"),
        P(("groups", "replica"), None, None),
        P(("groups", "replica"), None),
        P(("groups", "replica"), None),
        P(("groups", "replica")),
    )
    out_specs = P(("groups", "replica"), None)
    return jax.shard_map(
        on_device, mesh=mesh, in_specs=in_specs, out_specs=out_specs, check_vma=False
    )
```

```python
import functools

import jax
import jax.numpy as jnp
from jax import lax
from jax.experimental import pallas as pl
from jax.experimental.pallas import tpu as pltpu
from jax.sharding import PartitionSpec as P

LOG2E = 1.4426950408889634
DEAD_MARK = 1024.0
DEAD_ABOVE = 512.0
NEG = -1e30
CHUNK = 1024
ROWS = 512
PARAMS = pltpu.CompilerParams(vmem_limit_bytes=58 * 1024 * 1024)
COPY_PARAMS = pltpu.CompilerParams(vmem_limit_bytes=62 * 1024 * 1024)

IN_SMEM = pl.BlockSpec(memory_space=pltpu.SMEM)
IN_HBM = pl.BlockSpec(memory_space=pltpu.HBM)


def fold_keys(work, keys, values, factor, bias=None):
    q_ref, max_ref, lanes_ref, sums_ref = work
    count, size = sums_ref.shape
    block = min(ROWS, count)
    groups = keys.shape[0] // size

    def score(first):
        scores = lax.dot_general(
            q_ref[first:first + block, :],
            keys,
            (((1,), (1,)), ((), ())),
            preferred_element_type=jnp.float32,
        )
        return scores if bias is None else scores + bias

    following = score(0)
    for first in range(0, count, block):
        here = slice(first, first + block)
        scores, following = following, score(first + block) if first + block < count else None
        old_max = max_ref[here]
        new_max = jnp.maximum(old_max, jnp.max(scores, axis=1, keepdims=True))
        shrink = jnp.exp2((old_max - new_max) * factor)
        weights = jnp.exp2((scores - jnp.tile(new_max, (1, groups))) * factor)
        lanes = weights[:, :size]
        for group in range(1, groups):
            lanes += weights[:, group * size:(group + 1) * size]
        max_ref[here] = new_max
        lanes_ref[here] = lanes_ref[here] * shrink + lanes
        sums_ref[here] = sums_ref[here] * shrink + jnp.dot(
            weights.astype(jnp.bfloat16), values, preferred_element_type=jnp.float32
        )


def stack_queries(q_ref, stacked_ref):
    tokens, width = q_ref.shape
    size = stacked_ref.shape[1]
    for head in range(width // size):
        stacked_ref[head * tokens:(head + 1) * tokens, :] = q_ref[:, head * size:(head + 1) * size]


def load_state(loaded_ref, max_ref, lanes_ref, sums_ref):
    count, size = max_ref.shape
    lane = lax.broadcasted_iota(jnp.int32, (count, size), 1)
    sums_ref[...] = loaded_ref[0]
    lanes_ref[...] = jnp.where(lane == 0, loaded_ref[1], 0.0)
    max_ref[...] = jnp.broadcast_to(loaded_ref[1, :, size - 1:], (count, size))


def save_state(max_ref, lanes_ref, sums_ref, saved_ref):
    count, size = max_ref.shape
    left = lax.broadcasted_iota(jnp.int32, (count, size), 1) < size // 2
    saved_ref[0] = sums_ref[...]
    saved_ref[1] = jnp.where(left, jnp.sum(lanes_ref[...], axis=1, keepdims=True), max_ref[...])


def finish(lanes_ref, sums_ref, out_ref):
    tokens = out_ref.shape[0]
    size = sums_ref.shape[1]
    for head in range(out_ref.shape[1] // size):
        here = slice(head * tokens, (head + 1) * tokens)
        out_ref[:, head * size:(head + 1) * size] = (
            sums_ref[here] / jnp.sum(lanes_ref[here], axis=1, keepdims=True)
        ).astype(out_ref.dtype)


def local_kernel(factor, len_ref, q_ref, suffix_ref, own_ref, out_ref, *work):
    q_stacked, max_ref, lanes_ref, sums_ref = work
    size = sums_ref.shape[1]
    suffix, own = suffix_ref.shape[0], own_ref.shape[0]
    stack_queries(q_ref, q_stacked)
    max_ref[...] = jnp.full(max_ref.shape, NEG, jnp.float32)
    lanes_ref[...] = jnp.zeros(lanes_ref.shape, jnp.float32)
    sums_ref[...] = jnp.zeros(sums_ref.shape, jnp.float32)
    block = min(ROWS, sums_ref.shape[0])
    token = lax.broadcasted_iota(jnp.int32, (block, suffix), 0) % suffix
    key = lax.broadcasted_iota(jnp.int32, (block, suffix), 1)
    causal = jnp.where(key <= token, 0.0, NEG)
    fold_keys(work, suffix_ref[:, :size], suffix_ref[:, size:], factor, causal)
    dead = jnp.where(lax.broadcasted_iota(jnp.int32, (1, own), 1) < len_ref[0], 0.0, NEG)
    fold_keys(work, own_ref[:, :size], own_ref[:, size:], factor, dead)
    save_state(max_ref, lanes_ref, sums_ref, out_ref)


def moved_kernel(factor, steps, q_ref, kv_ref, loaded_ref, out_ref, *work):
    step = pl.program_id(0)
    size = work[3].shape[1]

    @pl.when(step == 0)
    def _():
        stack_queries(q_ref, work[0])
        load_state(loaded_ref, *work[1:])

    rows = kv_ref[...].reshape(-1, kv_ref.shape[-1])
    dead = jnp.where(rows[:, size:].astype(jnp.float32) > DEAD_ABOVE, NEG, 0.0).T[:1]
    fold_keys(work, rows[:, :size], rows[:, size:], factor, dead)

    @pl.when(step == steps - 1)
    def _():
        save_state(*work[1:], out_ref)


def prefix_kernel(factor, last, count, steps, which_ref, q_ref, *refs):
    pieces = refs[:count]
    loaded_ref, out_ref, *work, rows_ref = refs[count:]
    step = pl.program_id(0)
    size = work[3].shape[1]
    chunk = rows_ref.shape[0] // steps

    @pl.when(step == 0)
    def _():
        stack_queries(q_ref, work[0])
        place = 0
        for piece in pieces:
            rows_ref[pl.ds(place, piece.shape[0]), :] = piece[...]
            place += piece.shape[0]
        load_state(loaded_ref, *work[1:])

    rows = pl.ds(pl.multiple_of(step * chunk, size), chunk)
    fold_keys(work, rows_ref[rows, :size], rows_ref[rows, size:], factor)

    @pl.when(step == steps - 1)
    def _():
        if last:
            finish(*work[2:], out_ref)
        else:
            save_state(*work[1:], out_ref)


def wait_all(copies):
    for copy in copies:
        copy.wait()


def pick_kernel(which_ref, *refs):
    pieces, out_ref = refs[:-1], refs[-1]
    for place, piece in enumerate(pieces):
        out_ref[pl.ds(place * piece.shape[0], piece.shape[0]), :] = piece[...]


def pack_kernel(target_ref, block_ref, count_ref, pool_ref, out_ref, held_ref, mark_ref, *sems):
    in_sems, out_sems = sems
    entries = target_ref.shape[1]
    mark_ref[...] = jnp.full(mark_ref.shape, DEAD_MARK, mark_ref.dtype)

    def load(entry):
        return pltpu.make_async_copy(
            pool_ref.at[block_ref[0, entry]], held_ref.at[entry], in_sems.at[entry]
        )

    def store(entry, source):
        return pltpu.make_async_copy(
            source, out_ref.at[target_ref[0, entry]], out_sems.at[entry]
        )

    @pl.loop(0, entries)
    def _(entry):
        live = entry < count_ref[0]
        pl.when(live)(lambda: load(entry).start())
        pl.when(jnp.logical_not(live))(lambda: store(entry, mark_ref).start())

    @pl.loop(0, entries)
    def _(entry):
        @pl.when(entry < count_ref[0])
        def _():
            load(entry).wait()
            store(entry, held_ref.at[entry]).start()

    @pl.loop(0, entries)
    def _(entry):
        store(entry, mark_ref).wait()


def stage_kernel(owner_ref, kept_ref, swapped_ref, *refs):
    outs, (sought_ref, known_ref, in_sems, out_sems) = refs[:-4], refs[-4:]
    chips, sought = sought_ref.shape[:2]
    replicas = 4 * chips
    me = lax.axis_index("replica")
    core, chip, is_last = me % 2, me // 2 % chips, me // 2 == replicas // 2 - 1
    owners = [owner_ref[prefix] for prefix in range(sought + 1)]
    after = False
    for prefix in range(sought):
        after |= owners[prefix] == replicas - 1
        owners[prefix] = jnp.where(after, owners[prefix + 1], owners[prefix])

    def load(source, step, prefix):
        target = sought_ref.at[step, prefix] if prefix < sought else known_ref.at[step, 0]
        return pltpu.make_async_copy(source.at[core, chip ^ step], target, in_sems.at[step, prefix])

    def start(step, prefix, here):
        pl.when(here)(lambda: load(kept_ref, step, prefix).start())
        pl.when(jnp.logical_not(here))(lambda: load(swapped_ref, step, prefix).start())

    def store(place):
        source = sought_ref.at[place] if place < chips else known_ref.at[place - chips]
        return pltpu.make_async_copy(source, outs[place], out_sems.at[place])

    for step in range(chips):
        for prefix in range(sought):
            start(step, prefix, owners[prefix] % 2 == core)

    @pl.when(is_last)
    def _():
        for step in range(chips):
            start(step, sought, core == 1)

    for step in range(chips):
        for prefix in range(sought):
            load(kept_ref, step, prefix).wait()
        store(step).start()

    @pl.when(is_last)
    def _():
        for step in range(chips):
            load(kept_ref, step, sought).wait()
            store(chips + step).start()
        wait_all([store(chips + step) for step in range(chips)])

    wait_all([store(step) for step in range(chips)])


def multicast(prefix_cache, owners, readers, ctx_len, outgoing, fold_local, fold_moved):
    replicas = lax.axis_size("replica")
    me = lax.axis_index("replica")
    half = replicas // 2
    chips = half // 2
    chip = me // 2 % chips
    width = prefix_cache.shape[1]
    ids = jnp.arange(owners.shape[0], dtype=jnp.int32)
    known = jnp.sum(jnp.where(owners == replicas - 1, ids, 0))
    sought = jnp.where(ids[:-1] >= known, owners[1:], owners[:-1])

    split = prefix_cache.reshape(2, chips, -1, width)
    swapped, outgoing = lax.optimization_barrier((swap_cores(prefix_cache), outgoing))
    arrived = lax.all_to_all(outgoing, "replica", split_axis=0, concat_axis=0, tiled=True)
    swapped = swapped.reshape(split.shape)
    pieces = jax.ShapeDtypeStruct((owners.shape[0] - 1, *split.shape[2:]), split.dtype)
    piece = jax.ShapeDtypeStruct((1, *split.shape[2:]), split.dtype)
    staged = pl.pallas_call(
        stage_kernel,
        out_shape=(pieces,) * chips + (piece,) * chips,
        in_specs=[IN_SMEM] + [IN_HBM] * 2,
        out_specs=(IN_HBM,) * (2 * chips),
        scratch_shapes=[
            pltpu.VMEM((chips, *pieces.shape), split.dtype),
            pltpu.VMEM((chips, *piece.shape), split.dtype),
            pltpu.SemaphoreType.DMA((chips, owners.shape[0])),
            pltpu.SemaphoreType.DMA((2 * chips,)),
        ],
        compiler_params=COPY_PARAMS,
        name="stage_prefix",
    )(owners, split, swapped)
    staged = list(staged)

    def to_peers(staged, senders):
        return [
            lax.ppermute(rows, "replica", [(i, i ^ (2 * step)) for i in senders])
            for step, rows in enumerate(staged)
            if step
        ]

    def choose(own, passed, source):
        away = chip ^ source
        for step, rows in enumerate(passed, 1):
            own = jnp.where((away == step)[:, None, None], rows, own)
        return own

    staged[0], ctx_len = lax.optimization_barrier((staged[0], ctx_len))
    passed = to_peers(staged[:chips], range(replicas))
    wanted = jnp.stack([readers[me], readers[me ^ 1]])
    place = jnp.where(wanted == known, 0, wanted + (wanted < known))
    passed[0], local, place, *known_staged = lax.optimization_barrier(
        (passed[0], fold_local(ctx_len), place, *staged[chips:])
    )
    passed_known = to_peers(known_staged, (replicas - 2, replicas - 1))
    last_chip = jnp.full((1,), chips - 1, jnp.int32)
    found = jnp.concatenate(
        [
            choose(known_staged[0], passed_known, last_chip),
            choose(staged[0], passed, sought // 2 % chips),
        ]
    )
    source = jnp.concatenate([jnp.full((1,), replicas - 1, jnp.int32), sought])
    passed = lax.ppermute(found, "replica", [(i, (i + half) % replicas) for i in range(replicas)])
    passed, state_now = lax.optimization_barrier((passed, fold_moved(arrived, local, 0)))
    held = jnp.where((source // half == me // half)[:, None, None], found, passed)
    return held, place, state_now, arrived


def swap_cores(rows):
    return lax.ppermute(rows, "replica", [(i, i ^ 1) for i in range(lax.axis_size("replica"))])


def gather_step(gathered, step):
    replicas = lax.axis_size("replica")
    bits = (replicas // 4).bit_length() - 1
    members = [bit for bit in range(bits) if step >> bit & 1]
    linked = [bit for bit in members if step >> ((bit - 1) % bits) & 1]
    last = min(linked or members)
    pairs = [(i, i ^ (2 << last)) for i in range(replicas)]
    return lax.ppermute(gathered[step ^ 1 << last], "replica", pairs)


def from_other(pieces, place):
    rows, width = pieces[0].shape[1:]
    spec = pl.BlockSpec((None, rows, width), lambda i, which: (which[1], 0, 0))
    picked = pl.pallas_call(
        pick_kernel,
        out_shape=jax.ShapeDtypeStruct((len(pieces) * rows, width), pieces[0].dtype),
        grid_spec=pltpu.PrefetchScalarGridSpec(
            num_scalar_prefetch=1,
            grid=(1,),
            in_specs=[spec] * len(pieces),
            out_specs=pl.BlockSpec((len(pieces) * rows, width), lambda i, which: (0, 0)),
        ),
        compiler_params=PARAMS,
        name="pick_other",
    )(place, *pieces)
    return swap_cores(picked)


def whole(shape):
    return pl.BlockSpec(shape, lambda *args: (0,) * len(shape))


def cost(rows, keys, size):
    return pl.CostEstimate(
        flops=12 * rows * keys * size, bytes_accessed=4 * keys * size, transcendentals=rows * keys
    )


def on_device(
    queries,
    suffix_kv,
    own_cache,
    ctx_len,
    prefix_cache,
    owners,
    readers,
    kv_pool,
    mig_target,
    mig_block,
    mig_count,
):
    replicas = lax.axis_size("replica")
    size = suffix_kv.shape[1] // 2
    tokens = queries.shape[0]
    heads = queries.shape[1] // size
    factor = size ** (-0.5) * LOG2E
    row_count = tokens * heads
    state = jax.ShapeDtypeStruct((2, row_count, size), jnp.float32)
    result = jax.ShapeDtypeStruct(queries.shape, queries.dtype)

    work = [
        pltpu.VMEM((row_count, size), queries.dtype),
        *[pltpu.VMEM((row_count, size), jnp.float32)] * 3,
    ]

    entries = mig_target.shape[1]
    slots = jax.ShapeDtypeStruct((replicas, *kv_pool.shape[1:]), kv_pool.dtype)
    outgoing = pl.pallas_call(
        pack_kernel,
        out_shape=slots,
        in_specs=[IN_SMEM] * 3 + [IN_HBM],
        out_specs=IN_HBM,
        scratch_shapes=[
            pltpu.VMEM((entries, *kv_pool.shape[1:]), kv_pool.dtype),
            pltpu.VMEM(kv_pool.shape[1:], kv_pool.dtype),
            pltpu.SemaphoreType.DMA((entries,)),
            pltpu.SemaphoreType.DMA((entries,)),
        ],
        compiler_params=COPY_PARAMS,
        name="pack_moved",
    )(mig_target, mig_block, mig_count, kv_pool)
    def fold_local(ctx_len):
        return pl.pallas_call(
            functools.partial(local_kernel, factor),
            out_shape=state,
            grid=(1,),
            in_specs=[
                IN_SMEM,
                whole(queries.shape),
                whole(suffix_kv.shape),
                whole(own_cache.shape),
            ],
            out_specs=whole(state.shape),
            scratch_shapes=work,
            compiler_params=PARAMS,
            cost_estimate=cost(row_count, tokens + own_cache.shape[0], size),
            name="local_keys",
        )(ctx_len, queries, suffix_kv, own_cache)

    def fold_moved(arrived, state_now, part):
        rows = arrived.shape[1]
        group = max(n for n in range(1, replicas + 1) if replicas % n == 0 and n * rows <= CHUNK)
        steps = replicas // group // 2
        return pl.pallas_call(
            functools.partial(moved_kernel, factor, steps),
            out_shape=state,
            grid=(steps,),
            in_specs=[
                whole(queries.shape),
                pl.BlockSpec((group, rows, 2 * size), lambda i: (part * steps + i, 0, 0)),
                whole(state.shape),
            ],
            out_specs=whole(state.shape),
            scratch_shapes=work,
            compiler_params=PARAMS,
            cost_estimate=cost(row_count, steps * group * rows, size),
            name="moved_keys",
        )(queries, arrived, state_now)

    def fold_prefix(pieces, state_now, last=False):
        others = from_other(pieces, place)
        rows = pieces[0].shape[1]
        keys = 2 * len(pieces) * rows
        steps = max(1, keys // CHUNK)
        while keys % (steps * size):
            steps -= 1
        target = result if last else state
        return pl.pallas_call(
            functools.partial(prefix_kernel, factor, last, len(pieces) + 1, steps),
            out_shape=target,
            grid_spec=pltpu.PrefetchScalarGridSpec(
                num_scalar_prefetch=1,
                grid=(steps,),
                in_specs=[
                    whole(queries.shape),
                    *[pl.BlockSpec((None, rows, 2 * size), lambda i, which: (which[0], 0, 0))]
                    * len(pieces),
                    whole(others.shape),
                    whole(state.shape),
                ],
                out_specs=whole(target.shape),
                scratch_shapes=[*work, pltpu.VMEM((keys, 2 * size), jnp.bfloat16)],
            ),
            compiler_params=PARAMS,
            cost_estimate=cost(row_count, keys, size),
            name="prefix_keys",
        )(place, queries, *pieces, others, state_now)

    held, place, state_now, arrived = multicast(
        prefix_cache, owners, readers, ctx_len, outgoing, fold_local, fold_moved
    )
    gathered = {0: held}
    ready = [held]
    rounds = (replicas // 4).bit_length() - 1
    for near in range(1, rounds + 1):
        steps = [step for step in range(1, replicas // 4) if step.bit_count() == near]
        coming = [gather_step(gathered, step) for step in steps]
        if near == 1:
            state_now = fold_moved(arrived, state_now, 1)
        else:
            state_now = fold_prefix(ready, state_now)
            ready = []
        *coming, state_now = lax.optimization_barrier((*coming, state_now))
        gathered.update(zip(steps, coming))
        ready += coming
    return fold_prefix(ready, state_now, True)


def solution(mesh):
    in_specs = (
        P(("groups", "replica"), None),
        P(("groups", "replica"), None),
        P(("groups", "replica"), None),
        P(("groups", "replica")),
        P(("groups", "replica"), None),
        P("groups"),
        P("groups"),
        P(("groups", "replica"), None, None),
        P(("groups", "replica"), None),
        P(("groups", "replica"), None),
        P(("groups", "replica")),
    )
    out_specs = P(("groups", "replica"), None)
    return jax.shard_map(
        on_device, mesh=mesh, in_specs=in_specs, out_specs=out_specs, check_vma=False
    )
```

```python
import functools

import jax
import jax.numpy as jnp
from jax import lax
from jax.experimental import pallas as pl
from jax.experimental.pallas import tpu as pltpu
from jax.sharding import PartitionSpec as P

LOG2E = 1.4426950408889634
DEAD_MARK = 1024.0
DEAD_ABOVE = 512.0
NEG = -1e30
CHUNK = 1024
ROWS = 512
PARAMS = pltpu.CompilerParams(vmem_limit_bytes=44 * 1024 * 1024)
COPY_PARAMS = pltpu.CompilerParams(vmem_limit_bytes=62 * 1024 * 1024)

IN_SMEM = pl.BlockSpec(memory_space=pltpu.SMEM)
IN_HBM = pl.BlockSpec(memory_space=pltpu.HBM)


def fold_keys(work, keys, values, factor, bias=None):
    q_ref, max_ref, lanes_ref, sums_ref = work
    count, size = sums_ref.shape
    block = min(ROWS, count)
    groups = keys.shape[0] // size

    def score(first):
        scores = lax.dot_general(
            q_ref[first:first + block, :],
            keys,
            (((1,), (1,)), ((), ())),
            preferred_element_type=jnp.float32,
        )
        return scores if bias is None else scores + bias

    following = score(0)
    for first in range(0, count, block):
        here = slice(first, first + block)
        scores, following = following, score(first + block) if first + block < count else None
        old_max = max_ref[here]
        new_max = jnp.maximum(old_max, jnp.max(scores, axis=1, keepdims=True))
        shrink = jnp.exp2((old_max - new_max) * factor)
        weights = jnp.exp2((scores - jnp.tile(new_max, (1, groups))) * factor)
        lanes = weights[:, :size]
        for group in range(1, groups):
            lanes += weights[:, group * size:(group + 1) * size]
        max_ref[here] = new_max
        lanes_ref[here] = lanes_ref[here] * shrink + lanes
        sums_ref[here] = sums_ref[here] * shrink + jnp.dot(
            weights.astype(jnp.bfloat16), values, preferred_element_type=jnp.float32
        )


def stack_queries(q_ref, stacked_ref):
    tokens, width = q_ref.shape
    size = stacked_ref.shape[1]
    for head in range(width // size):
        stacked_ref[head * tokens:(head + 1) * tokens, :] = q_ref[:, head * size:(head + 1) * size]


def load_state(loaded_ref, max_ref, lanes_ref, sums_ref):
    count, size = max_ref.shape
    lane = lax.broadcasted_iota(jnp.int32, (count, size), 1)
    sums_ref[...] = loaded_ref[0]
    lanes_ref[...] = jnp.where(lane == 0, loaded_ref[1], 0.0)
    max_ref[...] = jnp.broadcast_to(loaded_ref[1, :, size - 1:], (count, size))


def save_state(max_ref, lanes_ref, sums_ref, saved_ref):
    count, size = max_ref.shape
    left = lax.broadcasted_iota(jnp.int32, (count, size), 1) < size // 2
    saved_ref[0] = sums_ref[...]
    saved_ref[1] = jnp.where(left, jnp.sum(lanes_ref[...], axis=1, keepdims=True), max_ref[...])


def finish(lanes_ref, sums_ref, out_ref):
    tokens = out_ref.shape[0]
    size = sums_ref.shape[1]
    for head in range(out_ref.shape[1] // size):
        here = slice(head * tokens, (head + 1) * tokens)
        out_ref[:, head * size:(head + 1) * size] = (
            sums_ref[here] / jnp.sum(lanes_ref[here], axis=1, keepdims=True)
        ).astype(out_ref.dtype)


def local_kernel(factor, len_ref, q_ref, suffix_ref, own_ref, after_ref, out_ref, *work):
    q_stacked, max_ref, lanes_ref, sums_ref = work
    size = sums_ref.shape[1]
    suffix, own = suffix_ref.shape[0], own_ref.shape[0]
    stack_queries(q_ref, q_stacked)
    max_ref[...] = jnp.full(max_ref.shape, NEG, jnp.float32)
    lanes_ref[...] = jnp.zeros(lanes_ref.shape, jnp.float32)
    sums_ref[...] = jnp.zeros(sums_ref.shape, jnp.float32)
    block = min(ROWS, sums_ref.shape[0])
    token = lax.broadcasted_iota(jnp.int32, (block, suffix), 0) % suffix
    key = lax.broadcasted_iota(jnp.int32, (block, suffix), 1)
    causal = jnp.where(key <= token, 0.0, NEG)
    fold_keys(work, suffix_ref[:, :size], suffix_ref[:, size:], factor, causal)
    dead = jnp.where(lax.broadcasted_iota(jnp.int32, (1, own), 1) < len_ref[0], 0.0, NEG)
    fold_keys(work, own_ref[:, :size], own_ref[:, size:], factor, dead)
    save_state(max_ref, lanes_ref, sums_ref, out_ref)


def moved_kernel(factor, steps, q_ref, kv_ref, loaded_ref, out_ref, *work):
    step = pl.program_id(0)
    size = work[3].shape[1]

    @pl.when(step == 0)
    def _():
        stack_queries(q_ref, work[0])
        load_state(loaded_ref, *work[1:])

    rows = kv_ref[...].reshape(-1, kv_ref.shape[-1])
    dead = jnp.where(rows[:, size:].astype(jnp.float32) > DEAD_ABOVE, NEG, 0.0).T[:1]
    fold_keys(work, rows[:, :size], rows[:, size:], factor, dead)

    @pl.when(step == steps - 1)
    def _():
        save_state(*work[1:], out_ref)


def prefix_kernel(factor, last, count, steps, which_ref, q_ref, *refs):
    pieces = refs[:count]
    loaded_ref, out_ref, *work, rows_ref = refs[count:]
    step = pl.program_id(0)
    size = work[3].shape[1]
    chunk = rows_ref.shape[0] // steps

    @pl.when(step == 0)
    def _():
        stack_queries(q_ref, work[0])
        place = 0
        for piece in pieces:
            rows_ref[pl.ds(place, piece.shape[0]), :] = piece[...]
            place += piece.shape[0]
        load_state(loaded_ref, *work[1:])

    rows = pl.ds(pl.multiple_of(step * chunk, size), chunk)
    fold_keys(work, rows_ref[rows, :size], rows_ref[rows, size:], factor)

    @pl.when(step == steps - 1)
    def _():
        if last:
            finish(*work[2:], out_ref)
        else:
            save_state(*work[1:], out_ref)


def wait_all(copies):
    for copy in copies:
        copy.wait()


def pick_kernel(which_ref, *refs):
    pieces, out_ref = refs[:-1], refs[-1]
    for place, piece in enumerate(pieces):
        out_ref[pl.ds(place * piece.shape[0], piece.shape[0]), :] = piece[...]


def pack_kernel(target_ref, block_ref, count_ref, pool_ref, out_ref, held_ref, mark_ref, *sems):
    in_sems, out_sems = sems
    entries = target_ref.shape[1]
    mark_ref[...] = jnp.full(mark_ref.shape, DEAD_MARK, mark_ref.dtype)

    def load(entry):
        return pltpu.make_async_copy(
            pool_ref.at[block_ref[0, entry]], held_ref.at[entry], in_sems.at[entry]
        )

    def store(entry, source):
        return pltpu.make_async_copy(
            source, out_ref.at[target_ref[0, entry]], out_sems.at[entry]
        )

    @pl.loop(0, entries)
    def _(entry):
        live = entry < count_ref[0]
        pl.when(live)(lambda: load(entry).start())
        pl.when(jnp.logical_not(live))(lambda: store(entry, mark_ref).start())

    @pl.loop(0, entries)
    def _(entry):
        @pl.when(entry < count_ref[0])
        def _():
            load(entry).wait()
            store(entry, held_ref.at[entry]).start()

    @pl.loop(0, entries)
    def _(entry):
        store(entry, mark_ref).wait()


def stage_kernel(owner_ref, kept_ref, swapped_ref, *refs):
    outs, (sought_ref, known_ref, in_sems, out_sems) = refs[:-4], refs[-4:]
    chips, sought = sought_ref.shape[:2]
    replicas = 4 * chips
    me = lax.axis_index("replica")
    core, chip, is_last = me % 2, me // 2 % chips, me // 2 == replicas // 2 - 1
    owners = [owner_ref[prefix] for prefix in range(sought + 1)]
    after = False
    for prefix in range(sought):
        after |= owners[prefix] == replicas - 1
        owners[prefix] = jnp.where(after, owners[prefix + 1], owners[prefix])

    def load(source, step, prefix):
        target = sought_ref.at[step, prefix] if prefix < sought else known_ref.at[step, 0]
        return pltpu.make_async_copy(source.at[core, chip ^ step], target, in_sems.at[step, prefix])

    def start(step, prefix, here):
        pl.when(here)(lambda: load(kept_ref, step, prefix).start())
        pl.when(jnp.logical_not(here))(lambda: load(swapped_ref, step, prefix).start())

    def store(place):
        source = sought_ref.at[place] if place < chips else known_ref.at[place - chips]
        return pltpu.make_async_copy(source, outs[place], out_sems.at[place])

    for step in range(chips):
        for prefix in range(sought):
            start(step, prefix, owners[prefix] % 2 == core)

    @pl.when(is_last)
    def _():
        for step in range(chips):
            start(step, sought, core == 1)

    for step in range(chips):
        for prefix in range(sought):
            load(kept_ref, step, prefix).wait()
        store(step).start()

    @pl.when(is_last)
    def _():
        for step in range(chips):
            load(kept_ref, step, sought).wait()
            store(chips + step).start()
        wait_all([store(chips + step) for step in range(chips)])

    wait_all([store(step) for step in range(chips)])


def multicast(prefix_cache, owners, readers, outgoing, fold_local, fold_moved):
    replicas = lax.axis_size("replica")
    me = lax.axis_index("replica")
    half = replicas // 2
    chips = half // 2
    chip = me // 2 % chips
    width = prefix_cache.shape[1]
    ids = jnp.arange(owners.shape[0], dtype=jnp.int32)
    known = jnp.sum(jnp.where(owners == replicas - 1, ids, 0))
    sought = jnp.where(ids[:-1] >= known, owners[1:], owners[:-1])

    split = prefix_cache.reshape(2, chips, -1, width)
    swapped, outgoing = lax.optimization_barrier((swap_cores(prefix_cache), outgoing))
    arrived = lax.all_to_all(outgoing, "replica", split_axis=0, concat_axis=0, tiled=True)
    swapped = swapped.reshape(split.shape)
    pieces = jax.ShapeDtypeStruct((owners.shape[0] - 1, *split.shape[2:]), split.dtype)
    piece = jax.ShapeDtypeStruct((1, *split.shape[2:]), split.dtype)
    staged = pl.pallas_call(
        stage_kernel,
        out_shape=(pieces,) * chips + (piece,) * chips,
        in_specs=[IN_SMEM] + [IN_HBM] * 2,
        out_specs=(IN_HBM,) * (2 * chips),
        scratch_shapes=[
            pltpu.VMEM((chips, *pieces.shape), split.dtype),
            pltpu.VMEM((chips, *piece.shape), split.dtype),
            pltpu.SemaphoreType.DMA((chips, owners.shape[0])),
            pltpu.SemaphoreType.DMA((2 * chips,)),
        ],
        compiler_params=COPY_PARAMS,
        name="stage_prefix",
    )(owners, split, swapped)
    staged = list(staged)

    def to_peers(staged, senders):
        return [
            lax.ppermute(rows, "replica", [(i, i ^ (2 * step)) for i in senders])
            for step, rows in enumerate(staged)
            if step
        ]

    def choose(own, passed, source):
        away = chip ^ source
        for step, rows in enumerate(passed, 1):
            own = jnp.where((away == step)[:, None, None], rows, own)
        return own

    passed = to_peers(staged[:chips], range(replicas))
    wanted = jnp.stack([readers[me], readers[me ^ 1]])
    place = jnp.where(wanted == known, 0, wanted + (wanted < known))
    passed[0], local, place, *known_staged = lax.optimization_barrier(
        (passed[0], fold_local(staged[0]), place, *staged[chips:])
    )
    passed_known = to_peers(known_staged, (replicas - 2, replicas - 1))
    last_chip = jnp.full((1,), chips - 1, jnp.int32)
    found = jnp.concatenate(
        [
            choose(known_staged[0], passed_known, last_chip),
            choose(staged[0], passed, sought // 2 % chips),
        ]
    )
    source = jnp.concatenate([jnp.full((1,), replicas - 1, jnp.int32), sought])
    passed = lax.ppermute(found, "replica", [(i, (i + half) % replicas) for i in range(replicas)])
    passed, state_now = lax.optimization_barrier((passed, fold_moved(arrived, local, 0)))
    held = jnp.where((source // half == me // half)[:, None, None], found, passed)
    return held, place, state_now, arrived


def swap_cores(rows):
    return lax.ppermute(rows, "replica", [(i, i ^ 1) for i in range(lax.axis_size("replica"))])


def gather_step(gathered, step):
    replicas = lax.axis_size("replica")
    bits = (replicas // 4).bit_length() - 1
    members = [bit for bit in range(bits) if step >> bit & 1]
    linked = [bit for bit in members if step >> ((bit - 1) % bits) & 1]
    last = min(linked or members)
    pairs = [(i, i ^ (2 << last)) for i in range(replicas)]
    return lax.ppermute(gathered[step ^ 1 << last], "replica", pairs)


def from_other(pieces, place):
    rows, width = pieces[0].shape[1:]
    spec = pl.BlockSpec((None, rows, width), lambda i, which: (which[1], 0, 0))
    picked = pl.pallas_call(
        pick_kernel,
        out_shape=jax.ShapeDtypeStruct((len(pieces) * rows, width), pieces[0].dtype),
        grid_spec=pltpu.PrefetchScalarGridSpec(
            num_scalar_prefetch=1,
            grid=(1,),
            in_specs=[spec] * len(pieces),
            out_specs=pl.BlockSpec((len(pieces) * rows, width), lambda i, which: (0, 0)),
        ),
        compiler_params=PARAMS,
        name="pick_other",
    )(place, *pieces)
    return swap_cores(picked)


def whole(shape):
    return pl.BlockSpec(shape, lambda *args: (0,) * len(shape))


def cost(rows, keys, size):
    return pl.CostEstimate(
        flops=12 * rows * keys * size, bytes_accessed=4 * keys * size, transcendentals=rows * keys
    )


def on_device(
    queries,
    suffix_kv,
    own_cache,
    ctx_len,
    prefix_cache,
    owners,
    readers,
    kv_pool,
    mig_target,
    mig_block,
    mig_count,
):
    replicas = lax.axis_size("replica")
    size = suffix_kv.shape[1] // 2
    tokens = queries.shape[0]
    heads = queries.shape[1] // size
    factor = size ** (-0.5) * LOG2E
    row_count = tokens * heads
    state = jax.ShapeDtypeStruct((2, row_count, size), jnp.float32)
    result = jax.ShapeDtypeStruct(queries.shape, queries.dtype)

    work = [
        pltpu.VMEM((row_count, size), queries.dtype),
        *[pltpu.VMEM((row_count, size), jnp.float32)] * 3,
    ]

    entries = mig_target.shape[1]
    slots = jax.ShapeDtypeStruct((replicas, *kv_pool.shape[1:]), kv_pool.dtype)
    outgoing = pl.pallas_call(
        pack_kernel,
        out_shape=slots,
        in_specs=[IN_SMEM] * 3 + [IN_HBM],
        out_specs=IN_HBM,
        scratch_shapes=[
            pltpu.VMEM((entries, *kv_pool.shape[1:]), kv_pool.dtype),
            pltpu.VMEM(kv_pool.shape[1:], kv_pool.dtype),
            pltpu.SemaphoreType.DMA((entries,)),
            pltpu.SemaphoreType.DMA((entries,)),
        ],
        compiler_params=COPY_PARAMS,
        name="pack_moved",
    )(mig_target, mig_block, mig_count, kv_pool)
    def fold_local(after):
        return pl.pallas_call(
            functools.partial(local_kernel, factor),
            out_shape=state,
            grid=(1,),
            in_specs=[
                IN_SMEM,
                whole(queries.shape),
                whole(suffix_kv.shape),
                whole(own_cache.shape),
                IN_HBM,
            ],
            out_specs=whole(state.shape),
            scratch_shapes=work,
            compiler_params=PARAMS,
            cost_estimate=cost(row_count, tokens + own_cache.shape[0], size),
            name="local_keys",
        )(ctx_len, queries, suffix_kv, own_cache, after)

    def fold_moved(arrived, state_now, part):
        rows = arrived.shape[1]
        group = max(n for n in range(1, replicas + 1) if replicas % n == 0 and n * rows <= CHUNK)
        steps = replicas // group // 2
        return pl.pallas_call(
            functools.partial(moved_kernel, factor, steps),
            out_shape=state,
            grid=(steps,),
            in_specs=[
                whole(queries.shape),
                pl.BlockSpec((group, rows, 2 * size), lambda i: (part * steps + i, 0, 0)),
                whole(state.shape),
            ],
            out_specs=whole(state.shape),
            scratch_shapes=work,
            compiler_params=PARAMS,
            cost_estimate=cost(row_count, steps * group * rows, size),
            name="moved_keys",
        )(queries, arrived, state_now)

    def fold_prefix(pieces, state_now, last=False):
        others = from_other(pieces, place)
        rows = pieces[0].shape[1]
        keys = 2 * len(pieces) * rows
        steps = max(1, keys // CHUNK)
        while keys % (steps * size):
            steps -= 1
        target = result if last else state
        return pl.pallas_call(
            functools.partial(prefix_kernel, factor, last, len(pieces) + 1, steps),
            out_shape=target,
            grid_spec=pltpu.PrefetchScalarGridSpec(
                num_scalar_prefetch=1,
                grid=(steps,),
                in_specs=[
                    whole(queries.shape),
                    *[pl.BlockSpec((None, rows, 2 * size), lambda i, which: (which[0], 0, 0))]
                    * len(pieces),
                    whole(others.shape),
                    whole(state.shape),
                ],
                out_specs=whole(target.shape),
                scratch_shapes=[*work, pltpu.VMEM((keys, 2 * size), jnp.bfloat16)],
            ),
            compiler_params=PARAMS,
            cost_estimate=cost(row_count, keys, size),
            name="prefix_keys",
        )(place, queries, *pieces, others, state_now)

    held, place, state_now, arrived = multicast(
        prefix_cache, owners, readers, outgoing, fold_local, fold_moved
    )
    gathered = {0: held}
    ready = [held]
    rounds = (replicas // 4).bit_length() - 1
    for near in range(1, rounds + 1):
        steps = [step for step in range(1, replicas // 4) if step.bit_count() == near]
        coming = [gather_step(gathered, step) for step in steps]
        if near == 1:
            state_now = fold_moved(arrived, state_now, 1)
        else:
            state_now = fold_prefix(ready, state_now)
            ready = []
        *coming, state_now = lax.optimization_barrier((*coming, state_now))
        gathered.update(zip(steps, coming))
        ready += coming
    return fold_prefix(ready, state_now, True)


def solution(mesh):
    in_specs = (
        P(("groups", "replica"), None),
        P(("groups", "replica"), None),
        P(("groups", "replica"), None),
        P(("groups", "replica")),
        P(("groups", "replica"), None),
        P("groups"),
        P("groups"),
        P(("groups", "replica"), None, None),
        P(("groups", "replica"), None),
        P(("groups", "replica"), None),
        P(("groups", "replica")),
    )
    out_specs = P(("groups", "replica"), None)
    return jax.shard_map(
        on_device, mesh=mesh, in_specs=in_specs, out_specs=out_specs, check_vma=False
    )
```

```python
import functools

import jax
import jax.numpy as jnp
from jax import lax
from jax.experimental import pallas as pl
from jax.experimental.pallas import tpu as pltpu
from jax.sharding import PartitionSpec as P

LOG2E = 1.4426950408889634
DEAD_MARK = 1024.0
DEAD_ABOVE = 512.0
NEG = -1e30
CHUNK = 1024
ROWS = 512
PARAMS = pltpu.CompilerParams(vmem_limit_bytes=44 * 1024 * 1024)
COPY_PARAMS = pltpu.CompilerParams(vmem_limit_bytes=62 * 1024 * 1024)

IN_SMEM = pl.BlockSpec(memory_space=pltpu.SMEM)
IN_HBM = pl.BlockSpec(memory_space=pltpu.HBM)


def fold_keys(work, keys, values, factor, bias=None):
    q_ref, max_ref, lanes_ref, sums_ref = work
    count, size = sums_ref.shape
    block = min(ROWS, count)
    groups = keys.shape[0] // size

    def score(first):
        scores = lax.dot_general(
            q_ref[first:first + block, :],
            keys,
            (((1,), (1,)), ((), ())),
            preferred_element_type=jnp.float32,
        )
        return scores if bias is None else scores + bias

    following = score(0)
    for first in range(0, count, block):
        here = slice(first, first + block)
        scores, following = following, score(first + block) if first + block < count else None
        old_max = max_ref[here]
        new_max = jnp.maximum(old_max, jnp.max(scores, axis=1, keepdims=True))
        shrink = jnp.exp2((old_max - new_max) * factor)
        weights = jnp.exp2((scores - jnp.tile(new_max, (1, groups))) * factor)
        lanes = weights[:, :size]
        for group in range(1, groups):
            lanes += weights[:, group * size:(group + 1) * size]
        max_ref[here] = new_max
        lanes_ref[here] = lanes_ref[here] * shrink + lanes
        sums_ref[here] = sums_ref[here] * shrink + jnp.dot(
            weights.astype(jnp.bfloat16), values, preferred_element_type=jnp.float32
        )


def stack_queries(q_ref, stacked_ref):
    tokens, width = q_ref.shape
    size = stacked_ref.shape[1]
    for head in range(width // size):
        stacked_ref[head * tokens:(head + 1) * tokens, :] = q_ref[:, head * size:(head + 1) * size]


def load_state(loaded_ref, max_ref, lanes_ref, sums_ref):
    count, size = max_ref.shape
    lane = lax.broadcasted_iota(jnp.int32, (count, size), 1)
    sums_ref[...] = loaded_ref[0]
    lanes_ref[...] = jnp.where(lane == 0, loaded_ref[1], 0.0)
    max_ref[...] = jnp.broadcast_to(loaded_ref[1, :, size - 1:], (count, size))


def save_state(max_ref, lanes_ref, sums_ref, saved_ref):
    count, size = max_ref.shape
    left = lax.broadcasted_iota(jnp.int32, (count, size), 1) < size // 2
    saved_ref[0] = sums_ref[...]
    saved_ref[1] = jnp.where(left, jnp.sum(lanes_ref[...], axis=1, keepdims=True), max_ref[...])


def finish(lanes_ref, sums_ref, out_ref):
    tokens = out_ref.shape[0]
    size = sums_ref.shape[1]
    for head in range(out_ref.shape[1] // size):
        here = slice(head * tokens, (head + 1) * tokens)
        out_ref[:, head * size:(head + 1) * size] = (
            sums_ref[here] / jnp.sum(lanes_ref[here], axis=1, keepdims=True)
        ).astype(out_ref.dtype)


def local_kernel(factor, len_ref, q_ref, suffix_ref, own_ref, after_ref, out_ref, *work):
    q_stacked, max_ref, lanes_ref, sums_ref = work
    size = sums_ref.shape[1]
    suffix, own = suffix_ref.shape[0], own_ref.shape[0]
    stack_queries(q_ref, q_stacked)
    max_ref[...] = jnp.full(max_ref.shape, NEG, jnp.float32)
    lanes_ref[...] = jnp.zeros(lanes_ref.shape, jnp.float32)
    sums_ref[...] = jnp.zeros(sums_ref.shape, jnp.float32)
    block = min(ROWS, sums_ref.shape[0])
    token = lax.broadcasted_iota(jnp.int32, (block, suffix), 0) % suffix
    key = lax.broadcasted_iota(jnp.int32, (block, suffix), 1)
    causal = jnp.where(key <= token, 0.0, NEG)
    fold_keys(work, suffix_ref[:, :size], suffix_ref[:, size:], factor, causal)
    dead = jnp.where(lax.broadcasted_iota(jnp.int32, (1, own), 1) < len_ref[0], 0.0, NEG)
    fold_keys(work, own_ref[:, :size], own_ref[:, size:], factor, dead)
    save_state(max_ref, lanes_ref, sums_ref, out_ref)


def moved_kernel(factor, steps, q_ref, kv_ref, loaded_ref, out_ref, *work):
    step = pl.program_id(0)
    size = work[3].shape[1]

    @pl.when(step == 0)
    def _():
        stack_queries(q_ref, work[0])
        load_state(loaded_ref, *work[1:])

    rows = kv_ref[...].reshape(-1, kv_ref.shape[-1])
    dead = jnp.where(rows[:, size:].astype(jnp.float32) > DEAD_ABOVE, NEG, 0.0).T[:1]
    fold_keys(work, rows[:, :size], rows[:, size:], factor, dead)

    @pl.when(step == steps - 1)
    def _():
        save_state(*work[1:], out_ref)


def prefix_kernel(factor, last, count, steps, which_ref, q_ref, *refs):
    pieces = refs[:count]
    loaded_ref, out_ref, *work, rows_ref = refs[count:]
    step = pl.program_id(0)
    size = work[3].shape[1]
    chunk = rows_ref.shape[0] // steps

    @pl.when(step == 0)
    def _():
        stack_queries(q_ref, work[0])
        place = 0
        for piece in pieces:
            rows_ref[pl.ds(place, piece.shape[0]), :] = piece[...]
            place += piece.shape[0]
        load_state(loaded_ref, *work[1:])

    rows = pl.ds(pl.multiple_of(step * chunk, size), chunk)
    fold_keys(work, rows_ref[rows, :size], rows_ref[rows, size:], factor)

    @pl.when(step == steps - 1)
    def _():
        if last:
            finish(*work[2:], out_ref)
        else:
            save_state(*work[1:], out_ref)


def wait_all(copies):
    for copy in copies:
        copy.wait()


def pick_kernel(which_ref, *refs):
    pieces, out_ref = refs[:-1], refs[-1]
    for place, piece in enumerate(pieces):
        out_ref[pl.ds(place * piece.shape[0], piece.shape[0]), :] = piece[...]


def pack_kernel(target_ref, block_ref, count_ref, pool_ref, out_ref, held_ref, mark_ref, *sems):
    in_sems, out_sems = sems
    entries = target_ref.shape[1]
    mark_ref[...] = jnp.full(mark_ref.shape, DEAD_MARK, mark_ref.dtype)

    def load(entry):
        return pltpu.make_async_copy(
            pool_ref.at[block_ref[0, entry]], held_ref.at[entry], in_sems.at[entry]
        )

    def store(entry, source):
        return pltpu.make_async_copy(
            source, out_ref.at[target_ref[0, entry]], out_sems.at[entry]
        )

    @pl.loop(0, entries)
    def _(entry):
        live = entry < count_ref[0]
        pl.when(live)(lambda: load(entry).start())
        pl.when(jnp.logical_not(live))(lambda: store(entry, mark_ref).start())

    @pl.loop(0, entries)
    def _(entry):
        @pl.when(entry < count_ref[0])
        def _():
            load(entry).wait()
            store(entry, held_ref.at[entry]).start()

    @pl.loop(0, entries)
    def _(entry):
        store(entry, mark_ref).wait()


def stage_kernel(owner_ref, reader_ref, kept_ref, swapped_ref, info_ref, *refs):
    outs, (sought_ref, known_ref, in_sems, out_sems) = refs[:-4], refs[-4:]
    chips, sought = sought_ref.shape[:2]
    replicas = 4 * chips
    me = lax.axis_index("replica")
    core, chip, is_last = me % 2, me // 2 % chips, me // 2 == replicas // 2 - 1
    owners = [owner_ref[prefix] for prefix in range(sought + 1)]
    known = sum(
        jnp.where(owner == replicas - 1, prefix, 0) for prefix, owner in enumerate(owners)
    )
    owners = [
        jnp.where(known <= prefix, owners[prefix + 1], owners[prefix]) for prefix in range(sought)
    ]

    def load(source, step, prefix):
        target = sought_ref.at[step, prefix] if prefix < sought else known_ref.at[step, 0]
        return pltpu.make_async_copy(source.at[core, chip ^ step], target, in_sems.at[step, prefix])

    def start(step, prefix, here):
        pl.when(here)(lambda: load(kept_ref, step, prefix).start())
        pl.when(jnp.logical_not(here))(lambda: load(swapped_ref, step, prefix).start())

    def store(place):
        source = sought_ref.at[place] if place < chips else known_ref.at[place - chips]
        return pltpu.make_async_copy(source, outs[place], out_sems.at[place])

    for step in range(chips):
        for prefix in range(sought):
            start(step, prefix, owners[prefix] % 2 == core)

    @pl.when(is_last)
    def _():
        for step in range(chips):
            start(step, sought, core == 1)

    for place, wanted in enumerate((reader_ref[me], reader_ref[me ^ 1])):
        ahead = jnp.where(wanted < known, wanted + 1, wanted)
        info_ref[place] = jnp.where(wanted == known, 0, ahead)
    for place, owner in enumerate([replicas - 1, *owners]):
        info_ref[2 + place] = chip ^ (owner // 2 % chips)
        same = owner // (replicas // 2) == me // (replicas // 2)
        info_ref[3 + sought + place] = jnp.where(same, 1, 0)

    for step in range(chips):
        for prefix in range(sought):
            load(kept_ref, step, prefix).wait()
        store(step).start()

    @pl.when(is_last)
    def _():
        for step in range(chips):
            load(kept_ref, step, sought).wait()
            store(chips + step).start()
        wait_all([store(chips + step) for step in range(chips)])

    wait_all([store(step) for step in range(chips)])


def multicast(prefix_cache, owners, readers, outgoing, fold_local, fold_moved):
    replicas = lax.axis_size("replica")
    half = replicas // 2
    chips = half // 2
    width = prefix_cache.shape[1]
    prefixes = owners.shape[0]

    split = prefix_cache.reshape(2, chips, -1, width)
    swapped, outgoing = lax.optimization_barrier((swap_cores(prefix_cache), outgoing))
    arrived = lax.all_to_all(outgoing, "replica", split_axis=0, concat_axis=0, tiled=True)
    swapped = swapped.reshape(split.shape)
    pieces = jax.ShapeDtypeStruct((owners.shape[0] - 1, *split.shape[2:]), split.dtype)
    piece = jax.ShapeDtypeStruct((1, *split.shape[2:]), split.dtype)
    info, *staged = pl.pallas_call(
        stage_kernel,
        out_shape=(jax.ShapeDtypeStruct((2 + 2 * prefixes,), jnp.int32),)
        + (pieces,) * chips
        + (piece,) * chips,
        in_specs=[IN_SMEM] * 2 + [IN_HBM] * 2,
        out_specs=(IN_SMEM,) + (IN_HBM,) * (2 * chips),
        scratch_shapes=[
            pltpu.VMEM((chips, *pieces.shape), split.dtype),
            pltpu.VMEM((chips, *piece.shape), split.dtype),
            pltpu.SemaphoreType.DMA((chips, owners.shape[0])),
            pltpu.SemaphoreType.DMA((2 * chips,)),
        ],
        compiler_params=COPY_PARAMS,
        name="stage_prefix",
    )(owners, readers, split, swapped)
    place, away, same_half = info[:2], info[2:2 + prefixes], info[2 + prefixes:] == 1

    def to_peers(staged, senders):
        return [
            lax.ppermute(rows, "replica", [(i, i ^ (2 * step)) for i in senders])
            for step, rows in enumerate(staged)
            if step
        ]

    def choose(own, passed, away):
        for step, rows in enumerate(passed, 1):
            own = jnp.where((away == step)[:, None, None], rows, own)
        return own

    passed = to_peers(staged[:chips], range(replicas))
    passed[0], local, *known_staged = lax.optimization_barrier(
        (passed[0], fold_local(staged[0]), *staged[chips:])
    )
    passed_known = to_peers(known_staged, (replicas - 2, replicas - 1))
    found = choose(staged[0], passed, away[1:])
    passed = lax.ppermute(found, "replica", [(i, (i + half) % replicas) for i in range(replicas)])
    found_known = choose(known_staged[0], passed_known, away[:1])
    passed_known = lax.ppermute(found_known, "replica", [(i + half, i) for i in range(half)])
    passed, passed_known, state_now = lax.optimization_barrier(
        (passed, passed_known, fold_moved(arrived, local, 0))
    )
    held = jnp.where(
        same_half[:, None, None],
        jnp.concatenate([found_known, found]),
        jnp.concatenate([passed_known, passed]),
    )
    return held, place, state_now, arrived


def swap_cores(rows):
    return lax.ppermute(rows, "replica", [(i, i ^ 1) for i in range(lax.axis_size("replica"))])


def gather_step(gathered, step):
    replicas = lax.axis_size("replica")
    bits = (replicas // 4).bit_length() - 1
    members = [bit for bit in range(bits) if step >> bit & 1]
    linked = [bit for bit in members if step >> ((bit - 1) % bits) & 1]
    last = min(linked or members)
    pairs = [(i, i ^ (2 << last)) for i in range(replicas)]
    return lax.ppermute(gathered[step ^ 1 << last], "replica", pairs)


def from_other(pieces, place):
    rows, width = pieces[0].shape[1:]
    spec = pl.BlockSpec((None, rows, width), lambda i, which: (which[1], 0, 0))
    picked = pl.pallas_call(
        pick_kernel,
        out_shape=jax.ShapeDtypeStruct((len(pieces) * rows, width), pieces[0].dtype),
        grid_spec=pltpu.PrefetchScalarGridSpec(
            num_scalar_prefetch=1,
            grid=(1,),
            in_specs=[spec] * len(pieces),
            out_specs=pl.BlockSpec((len(pieces) * rows, width), lambda i, which: (0, 0)),
        ),
        compiler_params=PARAMS,
        name="pick_other",
    )(place, *pieces)
    return swap_cores(picked)


def whole(shape):
    return pl.BlockSpec(shape, lambda *args: (0,) * len(shape))


def cost(rows, keys, size):
    return pl.CostEstimate(
        flops=12 * rows * keys * size, bytes_accessed=4 * keys * size, transcendentals=rows * keys
    )


def on_device(
    queries,
    suffix_kv,
    own_cache,
    ctx_len,
    prefix_cache,
    owners,
    readers,
    kv_pool,
    mig_target,
    mig_block,
    mig_count,
):
    replicas = lax.axis_size("replica")
    size = suffix_kv.shape[1] // 2
    tokens = queries.shape[0]
    heads = queries.shape[1] // size
    factor = size ** (-0.5) * LOG2E
    row_count = tokens * heads
    state = jax.ShapeDtypeStruct((2, row_count, size), jnp.float32)
    result = jax.ShapeDtypeStruct(queries.shape, queries.dtype)

    work = [
        pltpu.VMEM((row_count, size), queries.dtype),
        *[pltpu.VMEM((row_count, size), jnp.float32)] * 3,
    ]

    entries = mig_target.shape[1]
    slots = jax.ShapeDtypeStruct((replicas, *kv_pool.shape[1:]), kv_pool.dtype)
    outgoing = pl.pallas_call(
        pack_kernel,
        out_shape=slots,
        in_specs=[IN_SMEM] * 3 + [IN_HBM],
        out_specs=IN_HBM,
        scratch_shapes=[
            pltpu.VMEM((entries, *kv_pool.shape[1:]), kv_pool.dtype),
            pltpu.VMEM(kv_pool.shape[1:], kv_pool.dtype),
            pltpu.SemaphoreType.DMA((entries,)),
            pltpu.SemaphoreType.DMA((entries,)),
        ],
        compiler_params=COPY_PARAMS,
        name="pack_moved",
    )(mig_target, mig_block, mig_count, kv_pool)
    def fold_local(after):
        return pl.pallas_call(
            functools.partial(local_kernel, factor),
            out_shape=state,
            grid=(1,),
            in_specs=[
                IN_SMEM,
                whole(queries.shape),
                whole(suffix_kv.shape),
                whole(own_cache.shape),
                IN_HBM,
            ],
            out_specs=whole(state.shape),
            scratch_shapes=work,
            compiler_params=PARAMS,
            cost_estimate=cost(row_count, tokens + own_cache.shape[0], size),
            name="local_keys",
        )(ctx_len, queries, suffix_kv, own_cache, after)

    def fold_moved(arrived, state_now, part):
        rows = arrived.shape[1]
        group = max(n for n in range(1, replicas + 1) if replicas % n == 0 and n * rows <= CHUNK)
        steps = replicas // group // 2
        return pl.pallas_call(
            functools.partial(moved_kernel, factor, steps),
            out_shape=state,
            grid=(steps,),
            in_specs=[
                whole(queries.shape),
                pl.BlockSpec((group, rows, 2 * size), lambda i: (part * steps + i, 0, 0)),
                whole(state.shape),
            ],
            out_specs=whole(state.shape),
            scratch_shapes=work,
            compiler_params=PARAMS,
            cost_estimate=cost(row_count, steps * group * rows, size),
            name="moved_keys",
        )(queries, arrived, state_now)

    def fold_prefix(pieces, state_now, last=False):
        others = from_other(pieces, place)
        rows = pieces[0].shape[1]
        keys = 2 * len(pieces) * rows
        steps = max(1, keys // CHUNK)
        while keys % (steps * size):
            steps -= 1
        target = result if last else state
        return pl.pallas_call(
            functools.partial(prefix_kernel, factor, last, len(pieces) + 1, steps),
            out_shape=target,
            grid_spec=pltpu.PrefetchScalarGridSpec(
                num_scalar_prefetch=1,
                grid=(steps,),
                in_specs=[
                    whole(queries.shape),
                    *[pl.BlockSpec((None, rows, 2 * size), lambda i, which: (which[0], 0, 0))]
                    * len(pieces),
                    whole(others.shape),
                    whole(state.shape),
                ],
                out_specs=whole(target.shape),
                scratch_shapes=[*work, pltpu.VMEM((keys, 2 * size), jnp.bfloat16)],
            ),
            compiler_params=PARAMS,
            cost_estimate=cost(row_count, keys, size),
            name="prefix_keys",
        )(place, queries, *pieces, others, state_now)

    held, place, state_now, arrived = multicast(
        prefix_cache, owners, readers, outgoing, fold_local, fold_moved
    )
    gathered = {0: held}
    ready = [held]
    rounds = (replicas // 4).bit_length() - 1
    for near in range(1, rounds + 1):
        steps = [step for step in range(1, replicas // 4) if step.bit_count() == near]
        coming = [gather_step(gathered, step) for step in steps]
        if near == 1:
            state_now = fold_moved(arrived, state_now, 1)
        else:
            state_now = fold_prefix(ready, state_now)
            ready = []
        *coming, state_now = lax.optimization_barrier((*coming, state_now))
        gathered.update(zip(steps, coming))
        ready += coming
    return fold_prefix(ready, state_now, True)


def solution(mesh):
    in_specs = (
        P(("groups", "replica"), None),
        P(("groups", "replica"), None),
        P(("groups", "replica"), None),
        P(("groups", "replica")),
        P(("groups", "replica"), None),
        P("groups"),
        P("groups"),
        P(("groups", "replica"), None, None),
        P(("groups", "replica"), None),
        P(("groups", "replica"), None),
        P(("groups", "replica")),
    )
    out_specs = P(("groups", "replica"), None)
    return jax.shard_map(
        on_device, mesh=mesh, in_specs=in_specs, out_specs=out_specs, check_vma=False
    )
```

```python
import functools

import jax
import jax.numpy as jnp
from jax import lax
from jax.experimental import pallas as pl
from jax.experimental.pallas import tpu as pltpu
from jax.sharding import PartitionSpec as P

LOG2E = 1.4426950408889634
DEAD_MARK = 1024.0
DEAD_ABOVE = 512.0
NEG = -1e30
CHUNK = 1024
ROWS = 256
PARAMS = pltpu.CompilerParams(vmem_limit_bytes=44 * 1024 * 1024)
COPY_PARAMS = pltpu.CompilerParams(vmem_limit_bytes=62 * 1024 * 1024)

IN_SMEM = pl.BlockSpec(memory_space=pltpu.SMEM)
IN_HBM = pl.BlockSpec(memory_space=pltpu.HBM)


def fold_keys(work, keys, values, factor, bias=None):
    q_ref, max_ref, lanes_ref, sums_ref = work
    count, size = sums_ref.shape
    block = min(ROWS, count)
    groups = keys.shape[0] // size

    def score(first):
        scores = lax.dot_general(
            q_ref[first:first + block, :],
            keys,
            (((1,), (1,)), ((), ())),
            preferred_element_type=jnp.float32,
        )
        return scores if bias is None else scores + bias

    following = score(0)
    for first in range(0, count, block):
        here = slice(first, first + block)
        scores, following = following, score(first + block) if first + block < count else None
        old_max = max_ref[here]
        new_max = jnp.maximum(old_max, jnp.max(scores, axis=1, keepdims=True))
        shrink = jnp.exp2((old_max - new_max) * factor)
        weights = jnp.exp2((scores - jnp.tile(new_max, (1, groups))) * factor)
        lanes = weights[:, :size]
        for group in range(1, groups):
            lanes += weights[:, group * size:(group + 1) * size]
        max_ref[here] = new_max
        lanes_ref[here] = lanes_ref[here] * shrink + lanes
        sums_ref[here] = sums_ref[here] * shrink + jnp.dot(
            weights.astype(jnp.bfloat16), values, preferred_element_type=jnp.float32
        )


def stack_queries(q_ref, stacked_ref):
    tokens, width = q_ref.shape
    size = stacked_ref.shape[1]
    for head in range(width // size):
        stacked_ref[head * tokens:(head + 1) * tokens, :] = q_ref[:, head * size:(head + 1) * size]


def load_state(loaded_ref, max_ref, lanes_ref, sums_ref):
    count, size = max_ref.shape
    lane = lax.broadcasted_iota(jnp.int32, (count, size), 1)
    sums_ref[...] = loaded_ref[0]
    lanes_ref[...] = jnp.where(lane == 0, loaded_ref[1], 0.0)
    max_ref[...] = jnp.broadcast_to(loaded_ref[1, :, size - 1:], (count, size))


def save_state(max_ref, lanes_ref, sums_ref, saved_ref):
    count, size = max_ref.shape
    left = lax.broadcasted_iota(jnp.int32, (count, size), 1) < size // 2
    saved_ref[0] = sums_ref[...]
    saved_ref[1] = jnp.where(left, jnp.sum(lanes_ref[...], axis=1, keepdims=True), max_ref[...])


def finish(lanes_ref, sums_ref, out_ref):
    tokens = out_ref.shape[0]
    size = sums_ref.shape[1]
    for head in range(out_ref.shape[1] // size):
        here = slice(head * tokens, (head + 1) * tokens)
        out_ref[:, head * size:(head + 1) * size] = (
            sums_ref[here] / jnp.sum(lanes_ref[here], axis=1, keepdims=True)
        ).astype(out_ref.dtype)


def local_kernel(factor, len_ref, q_ref, suffix_ref, own_ref, after_ref, out_ref, *work):
    q_stacked, max_ref, lanes_ref, sums_ref = work
    size = sums_ref.shape[1]
    suffix, own = suffix_ref.shape[0], own_ref.shape[0]
    stack_queries(q_ref, q_stacked)
    max_ref[...] = jnp.full(max_ref.shape, NEG, jnp.float32)
    lanes_ref[...] = jnp.zeros(lanes_ref.shape, jnp.float32)
    sums_ref[...] = jnp.zeros(sums_ref.shape, jnp.float32)
    block = min(ROWS, sums_ref.shape[0])
    token = lax.broadcasted_iota(jnp.int32, (block, suffix), 0) % suffix
    key = lax.broadcasted_iota(jnp.int32, (block, suffix), 1)
    causal = jnp.where(key <= token, 0.0, NEG)
    fold_keys(work, suffix_ref[:, :size], suffix_ref[:, size:], factor, causal)
    dead = jnp.where(lax.broadcasted_iota(jnp.int32, (1, own), 1) < len_ref[0], 0.0, NEG)
    fold_keys(work, own_ref[:, :size], own_ref[:, size:], factor, dead)
    save_state(max_ref, lanes_ref, sums_ref, out_ref)


def moved_kernel(factor, steps, q_ref, kv_ref, loaded_ref, out_ref, *work):
    step = pl.program_id(0)
    size = work[3].shape[1]

    @pl.when(step == 0)
    def _():
        stack_queries(q_ref, work[0])
        load_state(loaded_ref, *work[1:])

    rows = kv_ref[...].reshape(-1, kv_ref.shape[-1])
    dead = jnp.where(rows[:, size:].astype(jnp.float32) > DEAD_ABOVE, NEG, 0.0).T[:1]
    fold_keys(work, rows[:, :size], rows[:, size:], factor, dead)

    @pl.when(step == steps - 1)
    def _():
        save_state(*work[1:], out_ref)


def prefix_kernel(factor, last, count, steps, which_ref, q_ref, *refs):
    pieces = refs[:count]
    loaded_ref, out_ref, *work, rows_ref = refs[count:]
    step = pl.program_id(0)
    size = work[3].shape[1]
    chunk = rows_ref.shape[0] // steps

    @pl.when(step == 0)
    def _():
        stack_queries(q_ref, work[0])
        place = 0
        for piece in pieces:
            rows_ref[pl.ds(place, piece.shape[0]), :] = piece[...]
            place += piece.shape[0]
        load_state(loaded_ref, *work[1:])

    rows = pl.ds(pl.multiple_of(step * chunk, size), chunk)
    fold_keys(work, rows_ref[rows, :size], rows_ref[rows, size:], factor)

    @pl.when(step == steps - 1)
    def _():
        if last:
            finish(*work[2:], out_ref)
        else:
            save_state(*work[1:], out_ref)


def start_all(copies):
    for copy in copies:
        copy.start()


def wait_all(copies):
    for copy in copies:
        copy.wait()


def pick_kernel(which_ref, *refs):
    pieces, out_ref = refs[:-1], refs[-1]
    for place, piece in enumerate(pieces):
        out_ref[pl.ds(place * piece.shape[0], piece.shape[0]), :] = piece[...]


def pack_kernel(target_ref, block_ref, count_ref, pool_ref, *refs):
    parts, (held_ref, mark_ref, in_sems, out_sems) = refs[:-4], refs[-4:]
    entries = target_ref.shape[1]
    mark_ref[...] = jnp.full(mark_ref.shape, DEAD_MARK, mark_ref.dtype)

    def load(entry):
        return pltpu.make_async_copy(
            pool_ref.at[block_ref[0, entry]], held_ref.at[entry], in_sems.at[entry]
        )

    def stores(entry, source):
        rows = parts[0].shape[1]
        return [
            pltpu.make_async_copy(
                source.at[pl.ds(place * rows, rows)],
                part.at[target_ref[0, entry]],
                out_sems.at[place, entry],
            )
            for place, part in enumerate(parts)
        ]

    @pl.loop(0, entries)
    def _(entry):
        live = entry < count_ref[0]
        pl.when(live)(lambda: load(entry).start())
        pl.when(jnp.logical_not(live))(lambda: start_all(stores(entry, mark_ref)))

    @pl.loop(0, entries)
    def _(entry):
        @pl.when(entry < count_ref[0])
        def _():
            load(entry).wait()
            start_all(stores(entry, held_ref.at[entry]))

    @pl.loop(0, entries)
    def _(entry):
        wait_all(stores(entry, mark_ref))


def gate_kernel(*refs):
    pass


def gate(rows, *after):
    return pl.pallas_call(
        gate_kernel,
        out_shape=jax.ShapeDtypeStruct(rows.shape, rows.dtype),
        in_specs=[IN_HBM] * (1 + len(after)),
        out_specs=IN_HBM,
        input_output_aliases={0: 0},
        compiler_params=PARAMS,
        name="gate",
    )(rows, *after)


def stage_kernel(owner_ref, reader_ref, kept_ref, swapped_ref, *refs):
    mine_ref, other_ref, known_away_ref, away_ref, same_ref, *refs = refs
    outs, (sought_ref, known_ref, in_sems, out_sems) = refs[:-4], refs[-4:]
    chips, sought = sought_ref.shape[:2]
    replicas = 4 * chips
    me = lax.axis_index("replica")
    core, chip, is_last = me % 2, me // 2 % chips, me // 2 == replicas // 2 - 1
    owners = [owner_ref[prefix] for prefix in range(sought + 1)]
    known = sum(
        jnp.where(owner == replicas - 1, prefix, 0) for prefix, owner in enumerate(owners)
    )
    owners = [
        jnp.where(known <= prefix, owners[prefix + 1], owners[prefix]) for prefix in range(sought)
    ]

    def load(source, step, prefix):
        target = sought_ref.at[step, prefix] if prefix < sought else known_ref.at[step, 0]
        return pltpu.make_async_copy(source.at[core, chip ^ step], target, in_sems.at[step, prefix])

    def start(step, prefix, here):
        pl.when(here)(lambda: load(kept_ref, step, prefix).start())
        pl.when(jnp.logical_not(here))(lambda: load(swapped_ref, step, prefix).start())

    def store(place):
        source = sought_ref.at[place] if place < chips else known_ref.at[place - chips]
        return pltpu.make_async_copy(source, outs[place], out_sems.at[place])

    for step in range(chips):
        for prefix in range(sought):
            start(step, prefix, owners[prefix] % 2 == core)

    @pl.when(is_last)
    def _():
        for step in range(chips):
            start(step, sought, core == 1)

    for place_ref, wanted in ((mine_ref, reader_ref[me]), (other_ref, reader_ref[me ^ 1])):
        ahead = jnp.where(wanted < known, wanted + 1, wanted)
        place_ref[0] = jnp.where(wanted == known, 0, ahead)
    known_away_ref[0] = chip ^ (chips - 1)
    for place, owner in enumerate([replicas - 1, *owners]):
        if place:
            away_ref[place - 1] = chip ^ (owner // 2 % chips)
        same = owner // (replicas // 2) == me // (replicas // 2)
        same_ref[place] = jnp.where(same, 1, 0)

    for step in range(chips):
        for prefix in range(sought):
            load(kept_ref, step, prefix).wait()
        store(step).start()

    @pl.when(is_last)
    def _():
        for step in range(chips):
            load(kept_ref, step, sought).wait()
            store(chips + step).start()
        wait_all([store(chips + step) for step in range(chips)])

    wait_all([store(step) for step in range(chips)])


def multicast(prefix_cache, owners, readers, outgoing, fold_local, fold_moved):
    replicas = lax.axis_size("replica")
    half = replicas // 2
    chips = half // 2
    width = prefix_cache.shape[1]
    prefixes = owners.shape[0]

    split = prefix_cache.reshape(2, chips, -1, width)
    swapped, *outgoing = lax.optimization_barrier((swap_cores(prefix_cache), *outgoing))
    arrived = send_blocks(outgoing[0])
    swapped = swapped.reshape(split.shape)
    pieces = jax.ShapeDtypeStruct((owners.shape[0] - 1, *split.shape[2:]), split.dtype)
    piece = jax.ShapeDtypeStruct((1, *split.shape[2:]), split.dtype)
    small = (1, 1, 1, prefixes - 1, prefixes)
    mine, other, known_away, away, same_half, *staged = pl.pallas_call(
        stage_kernel,
        out_shape=tuple(jax.ShapeDtypeStruct((count,), jnp.int32) for count in small)
        + (pieces,) * chips
        + (piece,) * chips,
        in_specs=[IN_SMEM] * 2 + [IN_HBM] * 2,
        out_specs=(IN_SMEM,) * len(small) + (IN_HBM,) * (2 * chips),
        scratch_shapes=[
            pltpu.VMEM((chips, *pieces.shape), split.dtype),
            pltpu.VMEM((chips, *piece.shape), split.dtype),
            pltpu.SemaphoreType.DMA((chips, owners.shape[0])),
            pltpu.SemaphoreType.DMA((2 * chips,)),
        ],
        compiler_params=COPY_PARAMS,
        name="stage_prefix",
    )(owners, readers, split, swapped)

    def to_peers(staged, senders):
        return [
            lax.ppermute(rows, "replica", [(i, i ^ (2 * step)) for i in senders])
            for step, rows in enumerate(staged)
            if step
        ]

    def choose(own, passed, away):
        for step, rows in enumerate(passed, 1):
            own = jnp.where((away == step)[:, None, None], rows, own)
        return own

    passed = to_peers(staged[:chips], range(replicas))
    passed[0], local, *known_staged = lax.optimization_barrier(
        (passed[0], fold_local(staged[0]), *staged[chips:])
    )
    passed_known = to_peers(known_staged, (replicas - 2, replicas - 1))
    found = choose(staged[0], passed, away)
    passed = lax.ppermute(found, "replica", [(i, (i + half) % replicas) for i in range(replicas)])
    found_known = choose(known_staged[0], passed_known, known_away)
    passed_known = lax.ppermute(found_known, "replica", [(i + half, i) for i in range(half)])
    later = send_blocks(gate(outgoing[1], passed, passed_known))
    passed, passed_known, state_now = lax.optimization_barrier(
        (passed, passed_known, fold_moved(arrived, local))
    )
    held = jnp.where(
        (same_half == 1)[:, None, None],
        jnp.concatenate([found_known, found]),
        jnp.concatenate([passed_known, passed]),
    )
    return held, mine, other, state_now, later


def send_blocks(rows):
    return lax.all_to_all(rows, "replica", split_axis=0, concat_axis=0, tiled=True)


def swap_cores(rows):
    return lax.ppermute(rows, "replica", [(i, i ^ 1) for i in range(lax.axis_size("replica"))])


def gather_step(gathered, step):
    replicas = lax.axis_size("replica")
    bits = (replicas // 4).bit_length() - 1
    members = [bit for bit in range(bits) if step >> bit & 1]
    linked = [bit for bit in members if step >> ((bit - 1) % bits) & 1]
    last = min(linked or members)
    pairs = [(i, i ^ (2 << last)) for i in range(replicas)]
    return lax.ppermute(gathered[step ^ 1 << last], "replica", pairs)


def from_other(pieces, place):
    rows, width = pieces[0].shape[1:]
    spec = pl.BlockSpec((None, rows, width), lambda i, which: (which[0], 0, 0))
    picked = pl.pallas_call(
        pick_kernel,
        out_shape=jax.ShapeDtypeStruct((len(pieces) * rows, width), pieces[0].dtype),
        grid_spec=pltpu.PrefetchScalarGridSpec(
            num_scalar_prefetch=1,
            grid=(1,),
            in_specs=[spec] * len(pieces),
            out_specs=pl.BlockSpec((len(pieces) * rows, width), lambda i, which: (0, 0)),
        ),
        compiler_params=PARAMS,
        name="pick_other",
    )(place, *pieces)
    return swap_cores(picked)


def whole(shape):
    return pl.BlockSpec(shape, lambda *args: (0,) * len(shape))


def cost(rows, keys, size):
    return pl.CostEstimate(
        flops=12 * rows * keys * size, bytes_accessed=4 * keys * size, transcendentals=rows * keys
    )


def on_device(
    queries,
    suffix_kv,
    own_cache,
    ctx_len,
    prefix_cache,
    owners,
    readers,
    kv_pool,
    mig_target,
    mig_block,
    mig_count,
):
    replicas = lax.axis_size("replica")
    size = suffix_kv.shape[1] // 2
    tokens = queries.shape[0]
    heads = queries.shape[1] // size
    factor = size ** (-0.5) * LOG2E
    row_count = tokens * heads
    state = jax.ShapeDtypeStruct((2, row_count, size), jnp.float32)
    result = jax.ShapeDtypeStruct(queries.shape, queries.dtype)

    work = [
        pltpu.VMEM((row_count, size), queries.dtype),
        *[pltpu.VMEM((row_count, size), jnp.float32)] * 3,
    ]

    entries = mig_target.shape[1]
    half_block = (replicas, kv_pool.shape[1] // 2, kv_pool.shape[2])
    slots = (jax.ShapeDtypeStruct(half_block, kv_pool.dtype),) * 2
    outgoing = pl.pallas_call(
        pack_kernel,
        out_shape=slots,
        in_specs=[IN_SMEM] * 3 + [IN_HBM],
        out_specs=(IN_HBM,) * 2,
        scratch_shapes=[
            pltpu.VMEM((entries, *kv_pool.shape[1:]), kv_pool.dtype),
            pltpu.VMEM(kv_pool.shape[1:], kv_pool.dtype),
            pltpu.SemaphoreType.DMA((entries,)),
            pltpu.SemaphoreType.DMA((2, entries)),
        ],
        compiler_params=COPY_PARAMS,
        name="pack_moved",
    )(mig_target, mig_block, mig_count, kv_pool)
    def fold_local(after):
        return pl.pallas_call(
            functools.partial(local_kernel, factor),
            out_shape=state,
            grid=(1,),
            in_specs=[
                IN_SMEM,
                whole(queries.shape),
                whole(suffix_kv.shape),
                whole(own_cache.shape),
                IN_HBM,
            ],
            out_specs=whole(state.shape),
            scratch_shapes=work,
            compiler_params=PARAMS,
            cost_estimate=cost(row_count, tokens + own_cache.shape[0], size),
            name="local_keys",
        )(ctx_len, queries, suffix_kv, own_cache, after)

    def fold_moved(arrived, state_now):
        rows = arrived.shape[1]
        group = max(n for n in range(1, replicas + 1) if replicas % n == 0 and n * rows <= CHUNK)
        steps = replicas // group
        return pl.pallas_call(
            functools.partial(moved_kernel, factor, steps),
            out_shape=state,
            grid=(steps,),
            in_specs=[
                whole(queries.shape),
                pl.BlockSpec((group, rows, 2 * size), lambda i: (i, 0, 0)),
                whole(state.shape),
            ],
            out_specs=whole(state.shape),
            scratch_shapes=work,
            compiler_params=PARAMS,
            cost_estimate=cost(row_count, steps * group * rows, size),
            name="moved_keys",
        )(queries, arrived, state_now)

    def fold_prefix(pieces, state_now, last=False):
        others = from_other(pieces, other)
        rows = pieces[0].shape[1]
        keys = 2 * len(pieces) * rows
        steps = max(1, keys // CHUNK)
        while keys % (steps * size):
            steps -= 1
        target = result if last else state
        return pl.pallas_call(
            functools.partial(prefix_kernel, factor, last, len(pieces) + 1, steps),
            out_shape=target,
            grid_spec=pltpu.PrefetchScalarGridSpec(
                num_scalar_prefetch=1,
                grid=(steps,),
                in_specs=[
                    whole(queries.shape),
                    *[pl.BlockSpec((None, rows, 2 * size), lambda i, which: (which[0], 0, 0))]
                    * len(pieces),
                    whole(others.shape),
                    whole(state.shape),
                ],
                out_specs=whole(target.shape),
                scratch_shapes=[*work, pltpu.VMEM((keys, 2 * size), jnp.bfloat16)],
            ),
            compiler_params=PARAMS,
            cost_estimate=cost(row_count, keys, size),
            name="prefix_keys",
        )(mine, queries, *pieces, others, state_now)

    held, mine, other, state_now, later = multicast(
        prefix_cache, owners, readers, outgoing, fold_local, fold_moved
    )
    gathered = {0: held}
    ready = [held]
    rounds = (replicas // 4).bit_length() - 1
    for near in range(1, rounds + 1):
        steps = [step for step in range(1, replicas // 4) if step.bit_count() == near]
        coming = [gather_step(gathered, step) for step in steps]
        if near > 1:
            *coming, state_now = lax.optimization_barrier(
                (*coming, fold_prefix(ready, state_now))
            )
            ready = []
        gathered.update(zip(steps, coming))
        ready += coming
    return fold_prefix(ready, fold_moved(later, state_now), True)


def solution(mesh):
    in_specs = (
        P(("groups", "replica"), None),
        P(("groups", "replica"), None),
        P(("groups", "replica"), None),
        P(("groups", "replica")),
        P(("groups", "replica"), None),
        P("groups"),
        P("groups"),
        P(("groups", "replica"), None, None),
        P(("groups", "replica"), None),
        P(("groups", "replica"), None),
        P(("groups", "replica")),
    )
    out_specs = P(("groups", "replica"), None)
    return jax.shard_map(
        on_device, mesh=mesh, in_specs=in_specs, out_specs=out_specs, check_vma=False
    )
```

```python
import functools

import jax
import jax.numpy as jnp
from jax import lax
from jax.experimental import pallas as pl
from jax.experimental.pallas import tpu as pltpu
from jax.sharding import PartitionSpec as P

LOG2E = 1.4426950408889634
DEAD_MARK = 1024.0
DEAD_ABOVE = 512.0
NEG = -1e30
CHUNK = 1280
ROWS = 256
PARAMS = pltpu.CompilerParams(vmem_limit_bytes=44 * 1024 * 1024)
COPY_PARAMS = pltpu.CompilerParams(vmem_limit_bytes=62 * 1024 * 1024)

IN_SMEM = pl.BlockSpec(memory_space=pltpu.SMEM)
IN_HBM = pl.BlockSpec(memory_space=pltpu.HBM)


def fold_keys(work, keys, values, factor, bias=None):
    q_ref, max_ref, lanes_ref, sums_ref = work
    count, size = sums_ref.shape
    block = min(ROWS, count)
    groups = keys.shape[0] // size

    def score(first):
        scores = lax.dot_general(
            q_ref[first:first + block, :],
            keys,
            (((1,), (1,)), ((), ())),
            preferred_element_type=jnp.float32,
        )
        return scores if bias is None else scores + bias

    following = score(0)
    for first in range(0, count, block):
        here = slice(first, first + block)
        scores, following = following, score(first + block) if first + block < count else None
        old_max = max_ref[here]
        new_max = jnp.maximum(old_max, jnp.max(scores, axis=1, keepdims=True))
        shrink = jnp.exp2((old_max - new_max) * factor)
        weights = jnp.exp2((scores - jnp.tile(new_max, (1, groups))) * factor)
        lanes = weights[:, :size]
        for group in range(1, groups):
            lanes += weights[:, group * size:(group + 1) * size]
        max_ref[here] = new_max
        lanes_ref[here] = lanes_ref[here] * shrink + lanes
        sums_ref[here] = sums_ref[here] * shrink + jnp.dot(
            weights.astype(jnp.bfloat16), values, preferred_element_type=jnp.float32
        )


def stack_queries(q_ref, stacked_ref):
    tokens, width = q_ref.shape
    size = stacked_ref.shape[1]
    for head in range(width // size):
        stacked_ref[head * tokens:(head + 1) * tokens, :] = q_ref[:, head * size:(head + 1) * size]


def load_state(loaded_ref, max_ref, lanes_ref, sums_ref):
    count, size = max_ref.shape
    lane = lax.broadcasted_iota(jnp.int32, (count, size), 1)
    sums_ref[...] = loaded_ref[0]
    lanes_ref[...] = jnp.where(lane == 0, loaded_ref[1], 0.0)
    max_ref[...] = jnp.broadcast_to(loaded_ref[1, :, size - 1:], (count, size))


def save_state(max_ref, lanes_ref, sums_ref, saved_ref):
    count, size = max_ref.shape
    left = lax.broadcasted_iota(jnp.int32, (count, size), 1) < size // 2
    saved_ref[0] = sums_ref[...]
    saved_ref[1] = jnp.where(left, jnp.sum(lanes_ref[...], axis=1, keepdims=True), max_ref[...])


def finish(lanes_ref, sums_ref, out_ref):
    tokens = out_ref.shape[0]
    size = sums_ref.shape[1]
    for head in range(out_ref.shape[1] // size):
        here = slice(head * tokens, (head + 1) * tokens)
        out_ref[:, head * size:(head + 1) * size] = (
            sums_ref[here] / jnp.sum(lanes_ref[here], axis=1, keepdims=True)
        ).astype(out_ref.dtype)


def local_kernel(factor, len_ref, q_ref, suffix_ref, own_ref, after_ref, out_ref, *work):
    q_stacked, max_ref, lanes_ref, sums_ref = work
    size = sums_ref.shape[1]
    suffix, own = suffix_ref.shape[0], own_ref.shape[0]
    stack_queries(q_ref, q_stacked)
    max_ref[...] = jnp.full(max_ref.shape, NEG, jnp.float32)
    lanes_ref[...] = jnp.zeros(lanes_ref.shape, jnp.float32)
    sums_ref[...] = jnp.zeros(sums_ref.shape, jnp.float32)
    block = min(ROWS, sums_ref.shape[0])
    token = lax.broadcasted_iota(jnp.int32, (block, suffix), 0) % suffix
    key = lax.broadcasted_iota(jnp.int32, (block, suffix), 1)
    causal = jnp.where(key <= token, 0.0, NEG)
    fold_keys(work, suffix_ref[:, :size], suffix_ref[:, size:], factor, causal)
    dead = jnp.where(lax.broadcasted_iota(jnp.int32, (1, own), 1) < len_ref[0], 0.0, NEG)
    fold_keys(work, own_ref[:, :size], own_ref[:, size:], factor, dead)
    save_state(max_ref, lanes_ref, sums_ref, out_ref)


def moved_kernel(factor, steps, q_ref, kv_ref, loaded_ref, out_ref, *work):
    step = pl.program_id(0)
    size = work[3].shape[1]

    @pl.when(step == 0)
    def _():
        stack_queries(q_ref, work[0])
        load_state(loaded_ref, *work[1:])

    rows = kv_ref[...].reshape(-1, kv_ref.shape[-1])
    dead = jnp.where(rows[:, size:].astype(jnp.float32) > DEAD_ABOVE, NEG, 0.0).T[:1]
    fold_keys(work, rows[:, :size], rows[:, size:], factor, dead)

    @pl.when(step == steps - 1)
    def _():
        save_state(*work[1:], out_ref)


def prefix_kernel(factor, last, count, steps, which_ref, q_ref, *refs):
    pieces = refs[:count]
    loaded_ref, out_ref, *work, rows_ref = refs[count:]
    step = pl.program_id(0)
    size = work[3].shape[1]
    chunk = rows_ref.shape[0] // steps

    @pl.when(step == 0)
    def _():
        stack_queries(q_ref, work[0])
        place = 0
        for piece in pieces:
            rows_ref[pl.ds(place, piece.shape[0]), :] = piece[...]
            place += piece.shape[0]
        load_state(loaded_ref, *work[1:])

    rows = pl.ds(pl.multiple_of(step * chunk, size), chunk)
    fold_keys(work, rows_ref[rows, :size], rows_ref[rows, size:], factor)

    @pl.when(step == steps - 1)
    def _():
        if last:
            finish(*work[2:], out_ref)
        else:
            save_state(*work[1:], out_ref)


def start_all(copies):
    for copy in copies:
        copy.start()


def wait_all(copies):
    for copy in copies:
        copy.wait()


def pick_kernel(which_ref, *refs):
    pieces, out_ref = refs[:-1], refs[-1]
    for place, piece in enumerate(pieces):
        out_ref[pl.ds(place * piece.shape[0], piece.shape[0]), :] = piece[...]


def pack_kernel(target_ref, block_ref, count_ref, pool_ref, *refs):
    parts, (held_ref, mark_ref, in_sems, out_sems) = refs[:-4], refs[-4:]
    entries = target_ref.shape[1]
    mark_ref[...] = jnp.full(mark_ref.shape, DEAD_MARK, mark_ref.dtype)

    def load(entry):
        return pltpu.make_async_copy(
            pool_ref.at[block_ref[0, entry]], held_ref.at[entry], in_sems.at[entry]
        )

    def stores(entry, source):
        early = parts[0].shape[1]
        return [
            pltpu.make_async_copy(
                source.at[pl.ds(place * early, part.shape[1])],
                part.at[target_ref[0, entry]],
                out_sems.at[place, entry],
            )
            for place, part in enumerate(parts)
        ]

    @pl.loop(0, entries)
    def _(entry):
        live = entry < count_ref[0]
        pl.when(live)(lambda: load(entry).start())
        pl.when(jnp.logical_not(live))(lambda: start_all(stores(entry, mark_ref)))

    @pl.loop(0, entries)
    def _(entry):
        @pl.when(entry < count_ref[0])
        def _():
            load(entry).wait()
            start_all(stores(entry, held_ref.at[entry]))

    @pl.loop(0, entries)
    def _(entry):
        wait_all(stores(entry, mark_ref))


def gate_kernel(*refs):
    pass


def gate(rows, *after):
    return pl.pallas_call(
        gate_kernel,
        out_shape=jax.ShapeDtypeStruct(rows.shape, rows.dtype),
        in_specs=[IN_HBM] * (1 + len(after)),
        out_specs=IN_HBM,
        input_output_aliases={0: 0},
        compiler_params=PARAMS,
        name="gate",
    )(rows, *after)


def stage_kernel(owner_ref, kept_ref, swapped_ref, *refs):
    outs, (sought_ref, known_ref, in_sems, out_sems) = refs[:-4], refs[-4:]
    chips, sought = sought_ref.shape[:2]
    replicas = 4 * chips
    me = lax.axis_index("replica")
    core, chip, is_last = me % 2, me // 2 % chips, me // 2 == replicas // 2 - 1
    owners = [owner_ref[prefix] for prefix in range(sought + 1)]
    known = sum(
        jnp.where(owner == replicas - 1, prefix, 0) for prefix, owner in enumerate(owners)
    )
    owners = [
        jnp.where(known <= prefix, owners[prefix + 1], owners[prefix]) for prefix in range(sought)
    ]

    def load(source, step, prefix):
        target = sought_ref.at[step, prefix] if prefix < sought else known_ref.at[step, 0]
        return pltpu.make_async_copy(source.at[core, chip ^ step], target, in_sems.at[step, prefix])

    def start(step, prefix, here):
        pl.when(here)(lambda: load(kept_ref, step, prefix).start())
        pl.when(jnp.logical_not(here))(lambda: load(swapped_ref, step, prefix).start())

    def store(place):
        source = sought_ref.at[place] if place < chips else known_ref.at[place - chips]
        return pltpu.make_async_copy(source, outs[place], out_sems.at[place])

    for step in range(chips):
        for prefix in range(sought):
            start(step, prefix, owners[prefix] % 2 == core)

    @pl.when(is_last)
    def _():
        for step in range(chips):
            start(step, sought, core == 1)

    for step in range(chips):
        for prefix in range(sought):
            load(kept_ref, step, prefix).wait()
        store(step).start()

    @pl.when(is_last)
    def _():
        for step in range(chips):
            load(kept_ref, step, sought).wait()
            store(chips + step).start()
        wait_all([store(chips + step) for step in range(chips)])

    wait_all([store(step) for step in range(chips)])


def multicast(prefix_cache, owners, readers, outgoing, fold_local, fold_moved):
    replicas = lax.axis_size("replica")
    half = replicas // 2
    chips = half // 2
    width = prefix_cache.shape[1]
    prefixes = owners.shape[0]

    split = prefix_cache.reshape(2, chips, -1, width)
    swapped, *outgoing = lax.optimization_barrier((swap_cores(prefix_cache), *outgoing))
    arrived = send_blocks(outgoing[0])
    swapped = swapped.reshape(split.shape)
    pieces = jax.ShapeDtypeStruct((owners.shape[0] - 1, *split.shape[2:]), split.dtype)
    piece = jax.ShapeDtypeStruct((1, *split.shape[2:]), split.dtype)
    staged = pl.pallas_call(
        stage_kernel,
        out_shape=(pieces,) * chips
        + (piece,) * chips,
        in_specs=[IN_SMEM] + [IN_HBM] * 2,
        out_specs=(IN_HBM,) * (2 * chips),
        scratch_shapes=[
            pltpu.VMEM((chips, *pieces.shape), split.dtype),
            pltpu.VMEM((chips, *piece.shape), split.dtype),
            pltpu.SemaphoreType.DMA((chips, owners.shape[0])),
            pltpu.SemaphoreType.DMA((2 * chips,)),
        ],
        compiler_params=COPY_PARAMS,
        name="stage_prefix",
    )(owners, split, swapped)

    me = lax.axis_index("replica")
    chip = me // 2 % chips
    owners = gate(owners, staged[0])
    ids = jnp.arange(prefixes, dtype=jnp.int32)
    known = jnp.sum(jnp.where(owners == replicas - 1, ids, 0))
    sought = jnp.where(ids[:-1] >= known, owners[1:], owners[:-1])
    away, known_away = chip ^ (sought // 2 % chips), (chip ^ (chips - 1))[None]
    held_by = jnp.concatenate([jnp.full((1,), replicas - 1, jnp.int32), sought])
    same_half = held_by // half == me // half
    wanted = jnp.stack([readers[me], readers[me ^ 1]])
    place = jnp.where(wanted == known, 0, wanted + (wanted < known))
    mine, other = place[:1], place[1:]

    def to_peers(staged, senders):
        return [
            lax.ppermute(rows, "replica", [(i, i ^ (2 * step)) for i in senders])
            for step, rows in enumerate(staged)
            if step
        ]

    def choose(own, passed, away):
        for step, rows in enumerate(passed, 1):
            own = jnp.where((away == step)[:, None, None], rows, own)
        return own

    passed = to_peers(staged[:chips], range(replicas))
    passed[0], local, *known_staged = lax.optimization_barrier(
        (passed[0], fold_local(staged[0]), *staged[chips:])
    )
    passed_known = to_peers(known_staged, (replicas - 2, replicas - 1))
    found = choose(staged[0], passed, away)
    passed = lax.ppermute(found, "replica", [(i, (i + half) % replicas) for i in range(replicas)])
    found_known = choose(known_staged[0], passed_known, known_away)
    passed_known = lax.ppermute(found_known, "replica", [(i + half, i) for i in range(half)])
    later = send_blocks(gate(outgoing[1], passed, passed_known))
    passed, passed_known, state_now = lax.optimization_barrier(
        (passed, passed_known, fold_moved(arrived, local))
    )
    held = jnp.where(
        same_half[:, None, None],
        jnp.concatenate([found_known, found]),
        jnp.concatenate([passed_known, passed]),
    )
    return held, mine, other, state_now, later


def send_blocks(rows):
    return lax.all_to_all(rows, "replica", split_axis=0, concat_axis=0, tiled=True)


def swap_cores(rows):
    return lax.ppermute(rows, "replica", [(i, i ^ 1) for i in range(lax.axis_size("replica"))])


def gather_step(gathered, step):
    replicas = lax.axis_size("replica")
    bits = (replicas // 4).bit_length() - 1
    members = [bit for bit in range(bits) if step >> bit & 1]
    linked = [bit for bit in members if step >> ((bit - 1) % bits) & 1]
    last = min(linked or members)
    pairs = [(i, i ^ (2 << last)) for i in range(replicas)]
    return lax.ppermute(gathered[step ^ 1 << last], "replica", pairs)


def from_other(pieces, place):
    rows, width = pieces[0].shape[1:]
    spec = pl.BlockSpec((None, rows, width), lambda i, which: (which[0], 0, 0))
    picked = pl.pallas_call(
        pick_kernel,
        out_shape=jax.ShapeDtypeStruct((len(pieces) * rows, width), pieces[0].dtype),
        grid_spec=pltpu.PrefetchScalarGridSpec(
            num_scalar_prefetch=1,
            grid=(1,),
            in_specs=[spec] * len(pieces),
            out_specs=pl.BlockSpec((len(pieces) * rows, width), lambda i, which: (0, 0)),
        ),
        compiler_params=PARAMS,
        name="pick_other",
    )(place, *pieces)
    return swap_cores(picked)


def whole(shape):
    return pl.BlockSpec(shape, lambda *args: (0,) * len(shape))


def cost(rows, keys, size):
    return pl.CostEstimate(
        flops=12 * rows * keys * size, bytes_accessed=4 * keys * size, transcendentals=rows * keys
    )


def on_device(
    queries,
    suffix_kv,
    own_cache,
    ctx_len,
    prefix_cache,
    owners,
    readers,
    kv_pool,
    mig_target,
    mig_block,
    mig_count,
):
    replicas = lax.axis_size("replica")
    size = suffix_kv.shape[1] // 2
    tokens = queries.shape[0]
    heads = queries.shape[1] // size
    factor = size ** (-0.5) * LOG2E
    row_count = tokens * heads
    state = jax.ShapeDtypeStruct((2, row_count, size), jnp.float32)
    result = jax.ShapeDtypeStruct(queries.shape, queries.dtype)

    work = [
        pltpu.VMEM((row_count, size), queries.dtype),
        *[pltpu.VMEM((row_count, size), jnp.float32)] * 3,
    ]

    entries = mig_target.shape[1]
    block = kv_pool.shape[1]
    early = block * 5 // 8
    slots = tuple(
        jax.ShapeDtypeStruct((replicas, rows, kv_pool.shape[2]), kv_pool.dtype)
        for rows in (early, block - early)
    )
    outgoing = pl.pallas_call(
        pack_kernel,
        out_shape=slots,
        in_specs=[IN_SMEM] * 3 + [IN_HBM],
        out_specs=(IN_HBM,) * 2,
        scratch_shapes=[
            pltpu.VMEM((entries, *kv_pool.shape[1:]), kv_pool.dtype),
            pltpu.VMEM(kv_pool.shape[1:], kv_pool.dtype),
            pltpu.SemaphoreType.DMA((entries,)),
            pltpu.SemaphoreType.DMA((2, entries)),
        ],
        compiler_params=COPY_PARAMS,
        name="pack_moved",
    )(mig_target, mig_block, mig_count, kv_pool)
    def fold_local(after):
        return pl.pallas_call(
            functools.partial(local_kernel, factor),
            out_shape=state,
            grid=(1,),
            in_specs=[
                IN_SMEM,
                whole(queries.shape),
                whole(suffix_kv.shape),
                whole(own_cache.shape),
                IN_HBM,
            ],
            out_specs=whole(state.shape),
            scratch_shapes=work,
            compiler_params=PARAMS,
            cost_estimate=cost(row_count, tokens + own_cache.shape[0], size),
            name="local_keys",
        )(ctx_len, queries, suffix_kv, own_cache, after)

    def fold_moved(arrived, state_now):
        rows = arrived.shape[1]
        group = max(n for n in range(1, replicas + 1) if replicas % n == 0 and n * rows <= CHUNK)
        steps = replicas // group
        return pl.pallas_call(
            functools.partial(moved_kernel, factor, steps),
            out_shape=state,
            grid=(steps,),
            in_specs=[
                whole(queries.shape),
                pl.BlockSpec((group, rows, 2 * size), lambda i: (i, 0, 0)),
                whole(state.shape),
            ],
            out_specs=whole(state.shape),
            scratch_shapes=work,
            compiler_params=PARAMS,
            cost_estimate=cost(row_count, steps * group * rows, size),
            name="moved_keys",
        )(queries, arrived, state_now)

    def fold_prefix(pieces, state_now, last=False):
        others = from_other(pieces, other)
        rows = pieces[0].shape[1]
        keys = 2 * len(pieces) * rows
        steps = max(1, keys // CHUNK)
        while keys % (steps * size):
            steps -= 1
        target = result if last else state
        return pl.pallas_call(
            functools.partial(prefix_kernel, factor, last, len(pieces) + 1, steps),
            out_shape=target,
            grid_spec=pltpu.PrefetchScalarGridSpec(
                num_scalar_prefetch=1,
                grid=(steps,),
                in_specs=[
                    whole(queries.shape),
                    *[pl.BlockSpec((None, rows, 2 * size), lambda i, which: (which[0], 0, 0))]
                    * len(pieces),
                    whole(others.shape),
                    whole(state.shape),
                ],
                out_specs=whole(target.shape),
                scratch_shapes=[*work, pltpu.VMEM((keys, 2 * size), jnp.bfloat16)],
            ),
            compiler_params=PARAMS,
            cost_estimate=cost(row_count, keys, size),
            name="prefix_keys",
        )(mine, queries, *pieces, others, state_now)

    held, mine, other, state_now, later = multicast(
        prefix_cache, owners, readers, outgoing, fold_local, fold_moved
    )
    gathered = {0: held}
    ready = [held]
    rounds = (replicas // 4).bit_length() - 1
    for near in range(1, rounds + 1):
        steps = [step for step in range(1, replicas // 4) if step.bit_count() == near]
        coming = [gather_step(gathered, step) for step in steps]
        if near > 1:
            *coming, state_now = lax.optimization_barrier(
                (*coming, fold_prefix(ready, state_now))
            )
            ready = []
        gathered.update(zip(steps, coming))
        ready += coming
    return fold_prefix(ready, fold_moved(later, state_now), True)


def solution(mesh):
    in_specs = (
        P(("groups", "replica"), None),
        P(("groups", "replica"), None),
        P(("groups", "replica"), None),
        P(("groups", "replica")),
        P(("groups", "replica"), None),
        P("groups"),
        P("groups"),
        P(("groups", "replica"), None, None),
        P(("groups", "replica"), None),
        P(("groups", "replica"), None),
        P(("groups", "replica")),
    )
    out_specs = P(("groups", "replica"), None)
    return jax.shard_map(
        on_device, mesh=mesh, in_specs=in_specs, out_specs=out_specs, check_vma=False
    )
```

```python
import functools

import jax
import jax.numpy as jnp
from jax import lax
from jax.experimental import pallas as pl
from jax.experimental.pallas import tpu as pltpu
from jax.sharding import PartitionSpec as P

LOG2E = 1.4426950408889634
DEAD_MARK = 1024.0
DEAD_ABOVE = 512.0
NEG = -1e30
CHUNK = 1024
ROWS = 256
PARAMS = pltpu.CompilerParams(vmem_limit_bytes=44 * 1024 * 1024)
COPY_PARAMS = pltpu.CompilerParams(vmem_limit_bytes=62 * 1024 * 1024)

IN_SMEM = pl.BlockSpec(memory_space=pltpu.SMEM)
IN_HBM = pl.BlockSpec(memory_space=pltpu.HBM)


def fold_keys(work, keys, values, factor, bias=None):
    q_ref, max_ref, lanes_ref, sums_ref = work
    count, size = sums_ref.shape
    block = min(ROWS, count)
    groups = keys.shape[0] // size

    def score(first):
        scores = lax.dot_general(
            q_ref[first:first + block, :],
            keys,
            (((1,), (1,)), ((), ())),
            preferred_element_type=jnp.float32,
        )
        return scores if bias is None else scores + bias

    following = score(0)
    for first in range(0, count, block):
        here = slice(first, first + block)
        scores, following = following, score(first + block) if first + block < count else None
        old_max = max_ref[here]
        new_max = jnp.maximum(old_max, jnp.max(scores, axis=1, keepdims=True))
        shrink = jnp.exp2((old_max - new_max) * factor)
        weights = jnp.exp2((scores - jnp.tile(new_max, (1, groups))) * factor)
        lanes = weights[:, :size]
        for group in range(1, groups):
            lanes += weights[:, group * size:(group + 1) * size]
        max_ref[here] = new_max
        lanes_ref[here] = lanes_ref[here] * shrink + lanes
        sums_ref[here] = sums_ref[here] * shrink + jnp.dot(
            weights.astype(jnp.bfloat16), values, preferred_element_type=jnp.float32
        )


def stack_queries(q_ref, stacked_ref):
    tokens, width = q_ref.shape
    size = stacked_ref.shape[1]
    for head in range(width // size):
        stacked_ref[head * tokens:(head + 1) * tokens, :] = q_ref[:, head * size:(head + 1) * size]


def load_state(loaded_ref, max_ref, lanes_ref, sums_ref):
    count, size = max_ref.shape
    lane = lax.broadcasted_iota(jnp.int32, (count, size), 1)
    sums_ref[...] = loaded_ref[0]
    lanes_ref[...] = jnp.where(lane == 0, loaded_ref[1], 0.0)
    max_ref[...] = jnp.broadcast_to(loaded_ref[1, :, size - 1:], (count, size))


def save_state(max_ref, lanes_ref, sums_ref, saved_ref):
    count, size = max_ref.shape
    left = lax.broadcasted_iota(jnp.int32, (count, size), 1) < size // 2
    saved_ref[0] = sums_ref[...]
    saved_ref[1] = jnp.where(left, jnp.sum(lanes_ref[...], axis=1, keepdims=True), max_ref[...])


def finish(lanes_ref, sums_ref, out_ref):
    tokens = out_ref.shape[0]
    size = sums_ref.shape[1]
    for head in range(out_ref.shape[1] // size):
        here = slice(head * tokens, (head + 1) * tokens)
        out_ref[:, head * size:(head + 1) * size] = (
            sums_ref[here] / jnp.sum(lanes_ref[here], axis=1, keepdims=True)
        ).astype(out_ref.dtype)


def local_kernel(factor, len_ref, q_ref, suffix_ref, own_ref, after_ref, out_ref, *work):
    q_stacked, max_ref, lanes_ref, sums_ref = work
    size = sums_ref.shape[1]
    suffix, own = suffix_ref.shape[0], own_ref.shape[0]
    stack_queries(q_ref, q_stacked)
    max_ref[...] = jnp.full(max_ref.shape, NEG, jnp.float32)
    lanes_ref[...] = jnp.zeros(lanes_ref.shape, jnp.float32)
    sums_ref[...] = jnp.zeros(sums_ref.shape, jnp.float32)
    block = min(ROWS, sums_ref.shape[0])
    token = lax.broadcasted_iota(jnp.int32, (block, suffix), 0) % suffix
    key = lax.broadcasted_iota(jnp.int32, (block, suffix), 1)
    causal = jnp.where(key <= token, 0.0, NEG)
    fold_keys(work, suffix_ref[:, :size], suffix_ref[:, size:], factor, causal)
    dead = jnp.where(lax.broadcasted_iota(jnp.int32, (1, own), 1) < len_ref[0], 0.0, NEG)
    fold_keys(work, own_ref[:, :size], own_ref[:, size:], factor, dead)
    save_state(max_ref, lanes_ref, sums_ref, out_ref)


def moved_kernel(factor, steps, q_ref, kv_ref, loaded_ref, out_ref, *work):
    step = pl.program_id(0)
    size = work[3].shape[1]

    @pl.when(step == 0)
    def _():
        stack_queries(q_ref, work[0])
        load_state(loaded_ref, *work[1:])

    rows = kv_ref[...].reshape(-1, kv_ref.shape[-1])
    dead = jnp.where(rows[:, size:].astype(jnp.float32) > DEAD_ABOVE, NEG, 0.0).T[:1]
    fold_keys(work, rows[:, :size], rows[:, size:], factor, dead)

    @pl.when(step == steps - 1)
    def _():
        save_state(*work[1:], out_ref)


def prefix_kernel(factor, last, count, steps, owner_ref, reader_ref, me_ref, q_ref, *refs):
    pieces = refs[:count]
    loaded_ref, out_ref, *work, rows_ref = refs[count:]
    step = pl.program_id(0)
    size = work[3].shape[1]
    chunk = rows_ref.shape[0] // steps

    @pl.when(step == 0)
    def _():
        stack_queries(q_ref, work[0])
        place = 0
        for piece in pieces:
            rows_ref[pl.ds(place, piece.shape[0]), :] = piece[...]
            place += piece.shape[0]
        load_state(loaded_ref, *work[1:])

    rows = pl.ds(pl.multiple_of(step * chunk, size), chunk)
    fold_keys(work, rows_ref[rows, :size], rows_ref[rows, size:], factor)

    @pl.when(step == steps - 1)
    def _():
        if last:
            finish(*work[2:], out_ref)
        else:
            save_state(*work[1:], out_ref)


def start_all(copies):
    for copy in copies:
        copy.start()


def wait_all(copies):
    for copy in copies:
        copy.wait()


def pick_kernel(owner_ref, reader_ref, me_ref, *refs):
    pieces, out_ref = refs[:-1], refs[-1]
    for place, piece in enumerate(pieces):
        out_ref[pl.ds(place * piece.shape[0], piece.shape[0]), :] = piece[...]


def pack_kernel(target_ref, block_ref, count_ref, pool_ref, *refs):
    parts, (held_ref, mark_ref, in_sems, out_sems) = refs[:-4], refs[-4:]
    entries = target_ref.shape[1]
    mark_ref[...] = jnp.full(mark_ref.shape, DEAD_MARK, mark_ref.dtype)

    def load(entry):
        return pltpu.make_async_copy(
            pool_ref.at[block_ref[0, entry]], held_ref.at[entry], in_sems.at[entry]
        )

    def stores(entry, source):
        rows = parts[0].shape[1]
        return [
            pltpu.make_async_copy(
                source.at[pl.ds(place * rows, rows)],
                part.at[target_ref[0, entry]],
                out_sems.at[place, entry],
            )
            for place, part in enumerate(parts)
        ]

    @pl.loop(0, entries)
    def _(entry):
        live = entry < count_ref[0]
        pl.when(live)(lambda: load(entry).start())
        pl.when(jnp.logical_not(live))(lambda: start_all(stores(entry, mark_ref)))

    @pl.loop(0, entries)
    def _(entry):
        @pl.when(entry < count_ref[0])
        def _():
            load(entry).wait()
            start_all(stores(entry, held_ref.at[entry]))

    @pl.loop(0, entries)
    def _(entry):
        wait_all(stores(entry, mark_ref))


def gate_kernel(*refs):
    pass


def gate(rows, *after):
    return pl.pallas_call(
        gate_kernel,
        out_shape=jax.ShapeDtypeStruct(rows.shape, rows.dtype),
        in_specs=[IN_HBM] * (1 + len(after)),
        out_specs=IN_HBM,
        input_output_aliases={0: 0},
        compiler_params=PARAMS,
        name="gate",
    )(rows, *after)


def stage_kernel(owner_ref, kept_ref, swapped_ref, *refs):
    outs, (sought_ref, known_ref, in_sems, out_sems) = refs[:-4], refs[-4:]
    chips, sought = sought_ref.shape[:2]
    replicas = 4 * chips
    me = lax.axis_index("replica")
    core, chip, is_last = me % 2, me // 2 % chips, me // 2 == replicas // 2 - 1
    owners = [owner_ref[prefix] for prefix in range(sought + 1)]
    known = sum(
        jnp.where(owner == replicas - 1, prefix, 0) for prefix, owner in enumerate(owners)
    )
    owners = [
        jnp.where(known <= prefix, owners[prefix + 1], owners[prefix]) for prefix in range(sought)
    ]

    def load(source, step, prefix):
        target = sought_ref.at[step, prefix] if prefix < sought else known_ref.at[step, 0]
        return pltpu.make_async_copy(source.at[core, chip ^ step], target, in_sems.at[step, prefix])

    def start(step, prefix, here):
        pl.when(here)(lambda: load(kept_ref, step, prefix).start())
        pl.when(jnp.logical_not(here))(lambda: load(swapped_ref, step, prefix).start())

    def store(place):
        source = sought_ref.at[place] if place < chips else known_ref.at[place - chips]
        return pltpu.make_async_copy(source, outs[place], out_sems.at[place])

    for step in range(chips):
        for prefix in range(sought):
            start(step, prefix, owners[prefix] % 2 == core)

    @pl.when(is_last)
    def _():
        for step in range(chips):
            start(step, sought, core == 1)

    for step in range(chips):
        for prefix in range(sought):
            load(kept_ref, step, prefix).wait()
        store(step).start()

    @pl.when(is_last)
    def _():
        for step in range(chips):
            load(kept_ref, step, sought).wait()
            store(chips + step).start()
        wait_all([store(chips + step) for step in range(chips)])

    wait_all([store(step) for step in range(chips)])


def multicast(prefix_cache, owners, outgoing, fold_local, fold_moved):
    replicas = lax.axis_size("replica")
    half = replicas // 2
    chips = half // 2
    width = prefix_cache.shape[1]
    prefixes = owners.shape[0]

    split = prefix_cache.reshape(2, chips, -1, width)
    swapped, *outgoing = lax.optimization_barrier((swap_cores(prefix_cache), *outgoing))
    arrived = send_blocks(outgoing[0])
    swapped = swapped.reshape(split.shape)
    pieces = jax.ShapeDtypeStruct((owners.shape[0] - 1, *split.shape[2:]), split.dtype)
    piece = jax.ShapeDtypeStruct((1, *split.shape[2:]), split.dtype)
    staged = pl.pallas_call(
        stage_kernel,
        out_shape=(pieces,) * chips
        + (piece,) * chips,
        in_specs=[IN_SMEM] + [IN_HBM] * 2,
        out_specs=(IN_HBM,) * (2 * chips),
        scratch_shapes=[
            pltpu.VMEM((chips, *pieces.shape), split.dtype),
            pltpu.VMEM((chips, *piece.shape), split.dtype),
            pltpu.SemaphoreType.DMA((chips, owners.shape[0])),
            pltpu.SemaphoreType.DMA((2 * chips,)),
        ],
        compiler_params=COPY_PARAMS,
        name="stage_prefix",
    )(owners, split, swapped)

    me = lax.axis_index("replica")
    chip = me // 2 % chips
    ids = jnp.arange(prefixes, dtype=jnp.int32)
    known = jnp.sum(jnp.where(owners == replicas - 1, ids, 0))
    sought = jnp.where(ids[:-1] >= known, owners[1:], owners[:-1])
    away, known_away = chip ^ (sought // 2 % chips), (chip ^ (chips - 1))[None]
    held_by = jnp.concatenate([jnp.full((1,), replicas - 1, jnp.int32), sought])
    same_half = held_by // half == me // half

    def to_peers(staged, senders):
        return [
            lax.ppermute(rows, "replica", [(i, i ^ (2 * step)) for i in senders])
            for step, rows in enumerate(staged)
            if step
        ]

    def choose(own, passed, away):
        for step, rows in enumerate(passed, 1):
            own = jnp.where((away == step)[:, None, None], rows, own)
        return own

    passed = to_peers(staged[:chips], range(replicas))
    passed[0], local, *known_staged = lax.optimization_barrier(
        (passed[0], fold_local(staged[0]), *staged[chips:])
    )
    passed_known = to_peers(known_staged, (replicas - 2, replicas - 1))
    found = choose(staged[0], passed, away)
    passed = lax.ppermute(found, "replica", [(i, (i + half) % replicas) for i in range(replicas)])
    found_known = choose(known_staged[0], passed_known, known_away)
    passed_known = lax.ppermute(found_known, "replica", [(i + half, i) for i in range(half)])
    later = send_blocks(gate(outgoing[1], passed, passed_known))
    passed, passed_known, state_now = lax.optimization_barrier(
        (passed, passed_known, fold_moved(arrived, local))
    )
    held = jnp.where(
        same_half[:, None, None],
        jnp.concatenate([found_known, found]),
        jnp.concatenate([passed_known, passed]),
    )
    return held, state_now, later


def send_blocks(rows):
    return lax.all_to_all(rows, "replica", split_axis=0, concat_axis=0, tiled=True)


def swap_cores(rows):
    return lax.ppermute(rows, "replica", [(i, i ^ 1) for i in range(lax.axis_size("replica"))])


def gather_step(gathered, step):
    replicas = lax.axis_size("replica")
    bits = (replicas // 4).bit_length() - 1
    members = [bit for bit in range(bits) if step >> bit & 1]
    linked = [bit for bit in members if step >> ((bit - 1) % bits) & 1]
    last = min(linked or members)
    pairs = [(i, i ^ (2 << last)) for i in range(replicas)]
    return lax.ppermute(gathered[step ^ 1 << last], "replica", pairs)


def wanted_place(owner_ref, reader_ref, who):
    last = reader_ref.shape[0] - 1
    known = sum(
        jnp.where(owner_ref[prefix] == last, prefix, 0) for prefix in range(owner_ref.shape[0])
    )
    wanted = reader_ref[who]
    return jnp.where(wanted == known, 0, jnp.where(wanted < known, wanted + 1, wanted))


def from_other(pieces, scalars):
    rows, width = pieces[0].shape[1:]
    spec = pl.BlockSpec(
        (None, rows, width),
        lambda i, owner, reader, me: (wanted_place(owner, reader, me[0] ^ 1), 0, 0),
    )
    picked = pl.pallas_call(
        pick_kernel,
        out_shape=jax.ShapeDtypeStruct((len(pieces) * rows, width), pieces[0].dtype),
        grid_spec=pltpu.PrefetchScalarGridSpec(
            num_scalar_prefetch=3,
            grid=(1,),
            in_specs=[spec] * len(pieces),
            out_specs=whole((len(pieces) * rows, width)),
        ),
        compiler_params=PARAMS,
        name="pick_other",
    )(*scalars, *pieces)
    return swap_cores(picked)


def whole(shape):
    return pl.BlockSpec(shape, lambda *args: (0,) * len(shape))


def cost(rows, keys, size):
    return pl.CostEstimate(
        flops=12 * rows * keys * size, bytes_accessed=4 * keys * size, transcendentals=rows * keys
    )


def on_device(
    queries,
    suffix_kv,
    own_cache,
    ctx_len,
    prefix_cache,
    owners,
    readers,
    kv_pool,
    mig_target,
    mig_block,
    mig_count,
):
    replicas = lax.axis_size("replica")
    size = suffix_kv.shape[1] // 2
    tokens = queries.shape[0]
    heads = queries.shape[1] // size
    factor = size ** (-0.5) * LOG2E
    row_count = tokens * heads
    state = jax.ShapeDtypeStruct((2, row_count, size), jnp.float32)
    result = jax.ShapeDtypeStruct(queries.shape, queries.dtype)

    work = [
        pltpu.VMEM((row_count, size), queries.dtype),
        *[pltpu.VMEM((row_count, size), jnp.float32)] * 3,
    ]

    entries = mig_target.shape[1]
    half_block = (replicas, kv_pool.shape[1] // 2, kv_pool.shape[2])
    slots = (jax.ShapeDtypeStruct(half_block, kv_pool.dtype),) * 2
    outgoing = pl.pallas_call(
        pack_kernel,
        out_shape=slots,
        in_specs=[IN_SMEM] * 3 + [IN_HBM],
        out_specs=(IN_HBM,) * 2,
        scratch_shapes=[
            pltpu.VMEM((entries, *kv_pool.shape[1:]), kv_pool.dtype),
            pltpu.VMEM(kv_pool.shape[1:], kv_pool.dtype),
            pltpu.SemaphoreType.DMA((entries,)),
            pltpu.SemaphoreType.DMA((2, entries)),
        ],
        compiler_params=COPY_PARAMS,
        name="pack_moved",
    )(mig_target, mig_block, mig_count, kv_pool)
    def fold_local(after):
        return pl.pallas_call(
            functools.partial(local_kernel, factor),
            out_shape=state,
            grid=(1,),
            in_specs=[
                IN_SMEM,
                whole(queries.shape),
                whole(suffix_kv.shape),
                whole(own_cache.shape),
                IN_HBM,
            ],
            out_specs=whole(state.shape),
            scratch_shapes=work,
            compiler_params=PARAMS,
            cost_estimate=cost(row_count, tokens + own_cache.shape[0], size),
            name="local_keys",
        )(ctx_len, queries, suffix_kv, own_cache, after)

    def fold_moved(arrived, state_now):
        rows = arrived.shape[1]
        group = max(n for n in range(1, replicas + 1) if replicas % n == 0 and n * rows <= CHUNK)
        steps = replicas // group
        return pl.pallas_call(
            functools.partial(moved_kernel, factor, steps),
            out_shape=state,
            grid=(steps,),
            in_specs=[
                whole(queries.shape),
                pl.BlockSpec((group, rows, 2 * size), lambda i: (i, 0, 0)),
                whole(state.shape),
            ],
            out_specs=whole(state.shape),
            scratch_shapes=work,
            compiler_params=PARAMS,
            cost_estimate=cost(row_count, steps * group * rows, size),
            name="moved_keys",
        )(queries, arrived, state_now)

    def fold_prefix(pieces, state_now, last=False):
        others = from_other(pieces, scalars)
        rows = pieces[0].shape[1]
        keys = 2 * len(pieces) * rows
        steps = max(1, keys // CHUNK)
        while keys % (steps * size):
            steps -= 1
        target = result if last else state
        return pl.pallas_call(
            functools.partial(prefix_kernel, factor, last, len(pieces) + 1, steps),
            out_shape=target,
            grid_spec=pltpu.PrefetchScalarGridSpec(
                num_scalar_prefetch=3,
                grid=(steps,),
                in_specs=[
                    whole(queries.shape),
                    *[
                        pl.BlockSpec(
                            (None, rows, 2 * size),
                            lambda i, owner, reader, me: (wanted_place(owner, reader, me[0]), 0, 0),
                        )
                    ]
                    * len(pieces),
                    whole(others.shape),
                    whole(state.shape),
                ],
                out_specs=whole(target.shape),
                scratch_shapes=[*work, pltpu.VMEM((keys, 2 * size), jnp.bfloat16)],
            ),
            compiler_params=PARAMS,
            cost_estimate=cost(row_count, keys, size),
            name="prefix_keys",
        )(*scalars, queries, *pieces, others, state_now)

    held, state_now, later = multicast(prefix_cache, owners, outgoing, fold_local, fold_moved)
    scalars = (owners, readers, lax.axis_index("replica")[None])
    gathered = {0: held}
    ready = [held]
    rounds = (replicas // 4).bit_length() - 1
    for near in range(1, rounds + 1):
        steps = [step for step in range(1, replicas // 4) if step.bit_count() == near]
        coming = [gather_step(gathered, step) for step in steps]
        if near > 1:
            *coming, state_now = lax.optimization_barrier(
                (*coming, fold_prefix(ready, state_now))
            )
            ready = []
        gathered.update(zip(steps, coming))
        ready += coming
    return fold_prefix(ready, fold_moved(later, state_now), True)


def solution(mesh):
    in_specs = (
        P(("groups", "replica"), None),
        P(("groups", "replica"), None),
        P(("groups", "replica"), None),
        P(("groups", "replica")),
        P(("groups", "replica"), None),
        P("groups"),
        P("groups"),
        P(("groups", "replica"), None, None),
        P(("groups", "replica"), None),
        P(("groups", "replica"), None),
        P(("groups", "replica")),
    )
    out_specs = P(("groups", "replica"), None)
    return jax.shard_map(
        on_device, mesh=mesh, in_specs=in_specs, out_specs=out_specs, check_vma=False
    )
```

```python
import functools

import jax
import jax.numpy as jnp
from jax import lax
from jax.experimental import pallas as pl
from jax.experimental.pallas import tpu as pltpu
from jax.sharding import PartitionSpec as P

LOG2E = 1.4426950408889634
DEAD_MARK = 1024.0
DEAD_ABOVE = 512.0
NEG = -1e30
CHUNK = 1024
ROWS = 256
PARAMS = pltpu.CompilerParams(vmem_limit_bytes=44 * 1024 * 1024)
COPY_PARAMS = pltpu.CompilerParams(vmem_limit_bytes=62 * 1024 * 1024)

IN_SMEM = pl.BlockSpec(memory_space=pltpu.SMEM)
IN_HBM = pl.BlockSpec(memory_space=pltpu.HBM)


def fold_keys(work, keys, values, factor, bias=None):
    q_ref, max_ref, lanes_ref, sums_ref = work
    count, size = sums_ref.shape
    block = min(ROWS, count)
    groups = keys.shape[0] // size

    def score(first):
        scores = lax.dot_general(
            q_ref[first:first + block, :],
            keys,
            (((1,), (1,)), ((), ())),
            preferred_element_type=jnp.float32,
        )
        return scores if bias is None else scores + bias

    following = score(0)
    for first in range(0, count, block):
        here = slice(first, first + block)
        scores, following = following, score(first + block) if first + block < count else None
        old_max = max_ref[here]
        new_max = jnp.maximum(old_max, jnp.max(scores, axis=1, keepdims=True))
        shrink = jnp.exp2((old_max - new_max) * factor)
        weights = jnp.exp2((scores - jnp.tile(new_max, (1, groups))) * factor)
        lanes = weights[:, :size]
        for group in range(1, groups):
            lanes += weights[:, group * size:(group + 1) * size]
        max_ref[here] = new_max
        lanes_ref[here] = lanes_ref[here] * shrink + lanes
        sums_ref[here] = sums_ref[here] * shrink + jnp.dot(
            weights.astype(jnp.bfloat16), values, preferred_element_type=jnp.float32
        )


def stack_queries(q_ref, stacked_ref):
    tokens, width = q_ref.shape
    size = stacked_ref.shape[1]
    for head in range(width // size):
        stacked_ref[head * tokens:(head + 1) * tokens, :] = q_ref[:, head * size:(head + 1) * size]


def load_state(loaded_ref, max_ref, lanes_ref, sums_ref):
    count, size = max_ref.shape
    lane = lax.broadcasted_iota(jnp.int32, (count, size), 1)
    sums_ref[...] = loaded_ref[0]
    lanes_ref[...] = jnp.where(lane == 0, loaded_ref[1], 0.0)
    max_ref[...] = jnp.broadcast_to(loaded_ref[1, :, size - 1:], (count, size))


def save_state(max_ref, lanes_ref, sums_ref, saved_ref):
    count, size = max_ref.shape
    left = lax.broadcasted_iota(jnp.int32, (count, size), 1) < size // 2
    saved_ref[0] = sums_ref[...]
    saved_ref[1] = jnp.where(left, jnp.sum(lanes_ref[...], axis=1, keepdims=True), max_ref[...])


def finish(lanes_ref, sums_ref, out_ref):
    tokens = out_ref.shape[0]
    size = sums_ref.shape[1]
    for head in range(out_ref.shape[1] // size):
        here = slice(head * tokens, (head + 1) * tokens)
        out_ref[:, head * size:(head + 1) * size] = (
            sums_ref[here] / jnp.sum(lanes_ref[here], axis=1, keepdims=True)
        ).astype(out_ref.dtype)


def local_kernel(factor, len_ref, q_ref, suffix_ref, own_ref, after_ref, out_ref, *work):
    q_stacked, max_ref, lanes_ref, sums_ref = work
    size = sums_ref.shape[1]
    suffix, own = suffix_ref.shape[0], own_ref.shape[0]
    stack_queries(q_ref, q_stacked)
    max_ref[...] = jnp.full(max_ref.shape, NEG, jnp.float32)
    lanes_ref[...] = jnp.zeros(lanes_ref.shape, jnp.float32)
    sums_ref[...] = jnp.zeros(sums_ref.shape, jnp.float32)
    block = min(ROWS, sums_ref.shape[0])
    token = lax.broadcasted_iota(jnp.int32, (block, suffix), 0) % suffix
    key = lax.broadcasted_iota(jnp.int32, (block, suffix), 1)
    causal = jnp.where(key <= token, 0.0, NEG)
    fold_keys(work, suffix_ref[:, :size], suffix_ref[:, size:], factor, causal)
    dead = jnp.where(lax.broadcasted_iota(jnp.int32, (1, own), 1) < len_ref[0], 0.0, NEG)
    fold_keys(work, own_ref[:, :size], own_ref[:, size:], factor, dead)
    save_state(max_ref, lanes_ref, sums_ref, out_ref)


def moved_kernel(factor, steps, q_ref, kv_ref, loaded_ref, out_ref, *work):
    step = pl.program_id(0)
    size = work[3].shape[1]

    @pl.when(step == 0)
    def _():
        stack_queries(q_ref, work[0])
        load_state(loaded_ref, *work[1:])

    rows = kv_ref[...].reshape(-1, kv_ref.shape[-1])
    dead = jnp.where(rows[:, size:].astype(jnp.float32) > DEAD_ABOVE, NEG, 0.0).T[:1]
    fold_keys(work, rows[:, :size], rows[:, size:], factor, dead)

    @pl.when(step == steps - 1)
    def _():
        save_state(*work[1:], out_ref)


def prefix_kernel(factor, count, steps, owner_ref, reader_ref, me_ref, q_ref, *refs):
    pieces = refs[:count]
    loaded_ref, out_ref, *work, rows_ref = refs[count:]
    step = pl.program_id(0)
    size = work[3].shape[1]
    chunk = rows_ref.shape[0] // steps

    @pl.when(step == 0)
    def _():
        stack_queries(q_ref, work[0])
        place = 0
        for piece in pieces:
            rows_ref[pl.ds(place, piece.shape[0]), :] = piece[...]
            place += piece.shape[0]
        load_state(loaded_ref, *work[1:])

    rows = pl.ds(pl.multiple_of(step * chunk, size), chunk)
    fold_keys(work, rows_ref[rows, :size], rows_ref[rows, size:], factor)

    @pl.when(step == steps - 1)
    def _():
        save_state(*work[1:], out_ref)


def wait_all(copies):
    for copy in copies:
        copy.wait()


def last_kernel(factor, steps, owner_ref, reader_ref, me_ref, q_ref, kv_ref, *refs):
    *pieces, loaded_ref, out_ref = refs[:-5]
    *work, rows_ref = refs[-5:]
    step = pl.program_id(0)
    size = work[3].shape[1]

    @pl.when(step == 0)
    def _():
        stack_queries(q_ref, work[0])
        load_state(loaded_ref, *work[1:])
        place = 0
        for piece in pieces:
            rows_ref[pl.ds(place, piece.shape[0]), :] = piece[...]
            place += piece.shape[0]

    rows = kv_ref[...].reshape(-1, kv_ref.shape[-1])
    dead = jnp.where(rows[:, size:].astype(jnp.float32) > DEAD_ABOVE, NEG, 0.0).T[:1]
    fold_keys(work, rows[:, :size], rows[:, size:], factor, dead)

    @pl.when(step == steps - 1)
    def _():
        fold_keys(work, rows_ref[:, :size], rows_ref[:, size:], factor)
        finish(*work[2:], out_ref)


def pick_kernel(owner_ref, reader_ref, me_ref, *refs):
    pieces, out_ref = refs[:-1], refs[-1]
    for place, piece in enumerate(pieces):
        out_ref[pl.ds(place * piece.shape[0], piece.shape[0]), :] = piece[...]


def pack_kernel(first, target_ref, block_ref, count_ref, pool_ref, *refs):
    out_ref, held_ref, mark_ref, in_sems, out_sems = refs[-5:]
    entries, rows = held_ref.shape[:2]
    mark_ref[...] = jnp.full(mark_ref.shape, DEAD_MARK, mark_ref.dtype)

    def load(entry):
        source = pool_ref.at[block_ref[0, entry], pl.ds(first, rows)]
        return pltpu.make_async_copy(source, held_ref.at[entry], in_sems.at[entry])

    def store(entry, source):
        return pltpu.make_async_copy(source, out_ref.at[target_ref[0, entry]], out_sems.at[entry])

    @pl.loop(0, entries)
    def _(entry):
        live = entry < count_ref[0]
        pl.when(live)(lambda: load(entry).start())
        pl.when(jnp.logical_not(live))(lambda: store(entry, mark_ref).start())

    @pl.loop(0, entries)
    def _(entry):
        @pl.when(entry < count_ref[0])
        def _():
            load(entry).wait()
            store(entry, held_ref.at[entry]).start()

    @pl.loop(0, entries)
    def _(entry):
        store(entry, mark_ref).wait()


def gate_kernel(*refs):
    pass


def gate(rows, *after):
    return pl.pallas_call(
        gate_kernel,
        out_shape=jax.ShapeDtypeStruct(rows.shape, rows.dtype),
        in_specs=[IN_HBM] * (1 + len(after)),
        out_specs=IN_HBM,
        input_output_aliases={0: 0},
        compiler_params=PARAMS,
        name="gate",
    )(rows, *after)


def stage_kernel(owner_ref, kept_ref, swapped_ref, *refs):
    outs, (sought_ref, known_ref, in_sems, out_sems) = refs[:-4], refs[-4:]
    chips, sought = sought_ref.shape[:2]
    replicas = 4 * chips
    me = lax.axis_index("replica")
    core, chip, is_last = me % 2, me // 2 % chips, me // 2 == replicas // 2 - 1
    owners = [owner_ref[prefix] for prefix in range(sought + 1)]
    known = sum(
        jnp.where(owner == replicas - 1, prefix, 0) for prefix, owner in enumerate(owners)
    )
    owners = [
        jnp.where(known <= prefix, owners[prefix + 1], owners[prefix]) for prefix in range(sought)
    ]

    def load(source, step, prefix):
        target = sought_ref.at[step, prefix] if prefix < sought else known_ref.at[step, 0]
        return pltpu.make_async_copy(source.at[core, chip ^ step], target, in_sems.at[step, prefix])

    def start(step, prefix, here):
        pl.when(here)(lambda: load(kept_ref, step, prefix).start())
        pl.when(jnp.logical_not(here))(lambda: load(swapped_ref, step, prefix).start())

    def store(place):
        source = sought_ref.at[place] if place < chips else known_ref.at[place - chips]
        return pltpu.make_async_copy(source, outs[place], out_sems.at[place])

    for step in range(chips):
        for prefix in range(sought):
            start(step, prefix, owners[prefix] % 2 == core)

    @pl.when(is_last)
    def _():
        for step in range(chips):
            start(step, sought, core == 1)

    for step in range(chips):
        for prefix in range(sought):
            load(kept_ref, step, prefix).wait()
        store(step).start()

    @pl.when(is_last)
    def _():
        for step in range(chips):
            load(kept_ref, step, sought).wait()
            store(chips + step).start()
        wait_all([store(chips + step) for step in range(chips)])

    wait_all([store(step) for step in range(chips)])


def multicast(prefix_cache, owners, pack, fold_local, fold_moved):
    replicas = lax.axis_size("replica")
    half = replicas // 2
    chips = half // 2
    width = prefix_cache.shape[1]
    prefixes = owners.shape[0]

    split = prefix_cache.reshape(2, chips, -1, width)
    swapped, outgoing = lax.optimization_barrier((swap_cores(prefix_cache), pack(0)))
    arrived = send_blocks(outgoing)
    swapped = swapped.reshape(split.shape)
    pieces = jax.ShapeDtypeStruct((owners.shape[0] - 1, *split.shape[2:]), split.dtype)
    piece = jax.ShapeDtypeStruct((1, *split.shape[2:]), split.dtype)
    staged = pl.pallas_call(
        stage_kernel,
        out_shape=(pieces,) * chips
        + (piece,) * chips,
        in_specs=[IN_SMEM] + [IN_HBM] * 2,
        out_specs=(IN_HBM,) * (2 * chips),
        scratch_shapes=[
            pltpu.VMEM((chips, *pieces.shape), split.dtype),
            pltpu.VMEM((chips, *piece.shape), split.dtype),
            pltpu.SemaphoreType.DMA((chips, owners.shape[0])),
            pltpu.SemaphoreType.DMA((2 * chips,)),
        ],
        compiler_params=COPY_PARAMS,
        name="stage_prefix",
    )(owners, split, swapped)

    me = lax.axis_index("replica")
    chip = me // 2 % chips
    ids = jnp.arange(prefixes, dtype=jnp.int32)
    known = jnp.sum(jnp.where(owners == replicas - 1, ids, 0))
    sought = jnp.where(ids[:-1] >= known, owners[1:], owners[:-1])
    away, known_away = chip ^ (sought // 2 % chips), (chip ^ (chips - 1))[None]
    held_by = jnp.concatenate([jnp.full((1,), replicas - 1, jnp.int32), sought])
    same_half = held_by // half == me // half

    def to_peers(staged, senders):
        return [
            lax.ppermute(rows, "replica", [(i, i ^ (2 * step)) for i in senders])
            for step, rows in enumerate(staged)
            if step
        ]

    def choose(own, passed, away):
        for step, rows in enumerate(passed, 1):
            own = jnp.where((away == step)[:, None, None], rows, own)
        return own

    passed = to_peers(staged[:chips], range(replicas))
    passed[0], local, *known_staged = lax.optimization_barrier(
        (passed[0], fold_local(staged[0]), *staged[chips:])
    )
    passed_known = to_peers(known_staged, (replicas - 2, replicas - 1))
    found = choose(staged[0], passed, away)
    passed = lax.ppermute(found, "replica", [(i, (i + half) % replicas) for i in range(replicas)])
    found_known = choose(known_staged[0], passed_known, known_away)
    passed_known = lax.ppermute(found_known, "replica", [(i + half, i) for i in range(half)])
    later = send_blocks(gate(pack(1, staged[0]), passed, passed_known))
    passed, passed_known, state_now = lax.optimization_barrier(
        (passed, passed_known, fold_moved(arrived, local))
    )
    held = jnp.where(
        same_half[:, None, None],
        jnp.concatenate([found_known, found]),
        jnp.concatenate([passed_known, passed]),
    )
    return held, state_now, later


def send_blocks(rows):
    return lax.all_to_all(rows, "replica", split_axis=0, concat_axis=0, tiled=True)


def swap_cores(rows):
    return lax.ppermute(rows, "replica", [(i, i ^ 1) for i in range(lax.axis_size("replica"))])


def gather_step(gathered, step):
    replicas = lax.axis_size("replica")
    bits = (replicas // 4).bit_length() - 1
    members = [bit for bit in range(bits) if step >> bit & 1]
    linked = [bit for bit in members if step >> ((bit - 1) % bits) & 1]
    last = min(linked or members)
    pairs = [(i, i ^ (2 << last)) for i in range(replicas)]
    return lax.ppermute(gathered[step ^ 1 << last], "replica", pairs)


def wanted_place(owner_ref, reader_ref, who):
    last = reader_ref.shape[0] - 1
    known = sum(
        jnp.where(owner_ref[prefix] == last, prefix, 0) for prefix in range(owner_ref.shape[0])
    )
    wanted = reader_ref[who]
    return jnp.where(wanted == known, 0, jnp.where(wanted < known, wanted + 1, wanted))


def from_other(pieces, scalars):
    rows, width = pieces[0].shape[1:]
    spec = pl.BlockSpec(
        (None, rows, width),
        lambda i, owner, reader, me: (wanted_place(owner, reader, me[0] ^ 1), 0, 0),
    )
    picked = pl.pallas_call(
        pick_kernel,
        out_shape=jax.ShapeDtypeStruct((len(pieces) * rows, width), pieces[0].dtype),
        grid_spec=pltpu.PrefetchScalarGridSpec(
            num_scalar_prefetch=3,
            grid=(1,),
            in_specs=[spec] * len(pieces),
            out_specs=whole((len(pieces) * rows, width)),
        ),
        compiler_params=PARAMS,
        name="pick_other",
    )(*scalars, *pieces)
    return swap_cores(picked)


def whole(shape):
    return pl.BlockSpec(shape, lambda *args: (0,) * len(shape))


def cost(rows, keys, size):
    return pl.CostEstimate(
        flops=12 * rows * keys * size, bytes_accessed=4 * keys * size, transcendentals=rows * keys
    )


def on_device(
    queries,
    suffix_kv,
    own_cache,
    ctx_len,
    prefix_cache,
    owners,
    readers,
    kv_pool,
    mig_target,
    mig_block,
    mig_count,
):
    replicas = lax.axis_size("replica")
    size = suffix_kv.shape[1] // 2
    tokens = queries.shape[0]
    heads = queries.shape[1] // size
    factor = size ** (-0.5) * LOG2E
    row_count = tokens * heads
    state = jax.ShapeDtypeStruct((2, row_count, size), jnp.float32)
    result = jax.ShapeDtypeStruct(queries.shape, queries.dtype)

    work = [
        pltpu.VMEM((row_count, size), queries.dtype),
        *[pltpu.VMEM((row_count, size), jnp.float32)] * 3,
    ]

    entries = mig_target.shape[1]
    half_block = (kv_pool.shape[1] // 2, kv_pool.shape[2])

    def pack(part, *after):
        return pl.pallas_call(
            functools.partial(pack_kernel, part * half_block[0]),
            out_shape=jax.ShapeDtypeStruct((replicas, *half_block), kv_pool.dtype),
            in_specs=[IN_SMEM] * 3 + [IN_HBM] * (1 + len(after)),
            out_specs=IN_HBM,
            scratch_shapes=[
                pltpu.VMEM((entries, *half_block), kv_pool.dtype),
                pltpu.VMEM(half_block, kv_pool.dtype),
                pltpu.SemaphoreType.DMA((entries,)),
                pltpu.SemaphoreType.DMA((entries,)),
            ],
            compiler_params=COPY_PARAMS,
            name="pack_moved",
        )(mig_target, mig_block, mig_count, kv_pool, *after)

    def fold_local(after):
        return pl.pallas_call(
            functools.partial(local_kernel, factor),
            out_shape=state,
            grid=(1,),
            in_specs=[
                IN_SMEM,
                whole(queries.shape),
                whole(suffix_kv.shape),
                whole(own_cache.shape),
                IN_HBM,
            ],
            out_specs=whole(state.shape),
            scratch_shapes=work,
            compiler_params=PARAMS,
            cost_estimate=cost(row_count, tokens + own_cache.shape[0], size),
            name="local_keys",
        )(ctx_len, queries, suffix_kv, own_cache, after)

    def fold_moved(arrived, state_now):
        rows = arrived.shape[1]
        group = max(n for n in range(1, replicas + 1) if replicas % n == 0 and n * rows <= CHUNK)
        steps = replicas // group
        return pl.pallas_call(
            functools.partial(moved_kernel, factor, steps),
            out_shape=state,
            grid=(steps,),
            in_specs=[
                whole(queries.shape),
                pl.BlockSpec((group, rows, 2 * size), lambda i: (i, 0, 0)),
                whole(state.shape),
            ],
            out_specs=whole(state.shape),
            scratch_shapes=work,
            compiler_params=PARAMS,
            cost_estimate=cost(row_count, steps * group * rows, size),
            name="moved_keys",
        )(queries, arrived, state_now)

    def wanted_pieces(pieces):
        spec = pl.BlockSpec(
            (None, *pieces[0].shape[1:]),
            lambda i, owner, reader, me: (wanted_place(owner, reader, me[0]), 0, 0),
        )
        return [spec] * len(pieces)

    def fold_prefix(pieces, state_now):
        others = from_other(pieces, scalars)
        keys = 2 * len(pieces) * pieces[0].shape[1]
        steps = max(1, keys // CHUNK)
        while keys % (steps * size):
            steps -= 1
        return pl.pallas_call(
            functools.partial(prefix_kernel, factor, len(pieces) + 1, steps),
            out_shape=state,
            grid_spec=pltpu.PrefetchScalarGridSpec(
                num_scalar_prefetch=3,
                grid=(steps,),
                in_specs=[
                    whole(queries.shape),
                    *wanted_pieces(pieces),
                    whole(others.shape),
                    whole(state.shape),
                ],
                out_specs=whole(state.shape),
                scratch_shapes=[*work, pltpu.VMEM((keys, 2 * size), jnp.bfloat16)],
            ),
            compiler_params=PARAMS,
            cost_estimate=cost(row_count, keys, size),
            name="prefix_keys",
        )(*scalars, queries, *pieces, others, state_now)

    def fold_last(arrived, pieces, state_now):
        others = from_other(pieces, scalars)
        keys = 2 * len(pieces) * pieces[0].shape[1]
        rows = arrived.shape[1]
        group = max(n for n in range(1, replicas + 1) if replicas % n == 0 and n * rows <= CHUNK)
        steps = replicas // group
        return pl.pallas_call(
            functools.partial(last_kernel, factor, steps),
            out_shape=result,
            grid_spec=pltpu.PrefetchScalarGridSpec(
                num_scalar_prefetch=3,
                grid=(steps,),
                in_specs=[
                    whole(queries.shape),
                    pl.BlockSpec((group, rows, 2 * size), lambda i, *scalars: (i, 0, 0)),
                    *wanted_pieces(pieces),
                    whole(others.shape),
                    whole(state.shape),
                ],
                out_specs=whole(queries.shape),
                scratch_shapes=[*work, pltpu.VMEM((keys, 2 * size), jnp.bfloat16)],
            ),
            compiler_params=PARAMS,
            cost_estimate=cost(row_count, replicas * rows + keys, size),
            name="last_keys",
        )(*scalars, queries, arrived, *pieces, others, state_now)

    held, state_now, later = multicast(prefix_cache, owners, pack, fold_local, fold_moved)
    scalars = (owners, readers, lax.axis_index("replica")[None])
    gathered = {0: held}
    ready = [held]
    rounds = (replicas // 4).bit_length() - 1
    for near in range(1, rounds + 1):
        steps = [step for step in range(1, replicas // 4) if step.bit_count() == near]
        coming = [gather_step(gathered, step) for step in steps]
        if near > 1:
            *coming, state_now = lax.optimization_barrier(
                (*coming, fold_prefix(ready, state_now))
            )
            ready = []
        gathered.update(zip(steps, coming))
        ready += coming
    return fold_last(later, ready, state_now)


def solution(mesh):
    in_specs = (
        P(("groups", "replica"), None),
        P(("groups", "replica"), None),
        P(("groups", "replica"), None),
        P(("groups", "replica")),
        P(("groups", "replica"), None),
        P("groups"),
        P("groups"),
        P(("groups", "replica"), None, None),
        P(("groups", "replica"), None),
        P(("groups", "replica"), None),
        P(("groups", "replica")),
    )
    out_specs = P(("groups", "replica"), None)
    return jax.shard_map(
        on_device, mesh=mesh, in_specs=in_specs, out_specs=out_specs, check_vma=False
    )
```

```python
import functools

import jax
import jax.numpy as jnp
from jax import lax
from jax.experimental import pallas as pl
from jax.experimental.pallas import tpu as pltpu
from jax.sharding import PartitionSpec as P

LOG2E = 1.4426950408889634
DEAD_MARK = 1024.0
DEAD_ABOVE = 512.0
NEG = -1e30
CHUNK = 1024
ROWS = 256
PARAMS = pltpu.CompilerParams(vmem_limit_bytes=44 * 1024 * 1024)
COPY_PARAMS = pltpu.CompilerParams(vmem_limit_bytes=62 * 1024 * 1024)

IN_SMEM = pl.BlockSpec(memory_space=pltpu.SMEM)
IN_HBM = pl.BlockSpec(memory_space=pltpu.HBM)


def fold_keys(work, keys, values, factor, bias=None):
    q_ref, max_ref, lanes_ref, sums_ref = work
    count, size = sums_ref.shape
    block = min(ROWS, count)
    groups = keys.shape[0] // size

    def score(first):
        scores = lax.dot_general(
            q_ref[first:first + block, :],
            keys,
            (((1,), (1,)), ((), ())),
            preferred_element_type=jnp.float32,
        )
        return scores if bias is None else scores + bias

    following = score(0)
    for first in range(0, count, block):
        here = slice(first, first + block)
        scores, following = following, score(first + block) if first + block < count else None
        old_max = max_ref[here]
        new_max = jnp.maximum(old_max, jnp.max(scores, axis=1, keepdims=True))
        shrink = jnp.exp2((old_max - new_max) * factor)
        weights = jnp.exp2((scores - jnp.tile(new_max, (1, groups))) * factor)
        lanes = weights[:, :size]
        for group in range(1, groups):
            lanes += weights[:, group * size:(group + 1) * size]
        max_ref[here] = new_max
        lanes_ref[here] = lanes_ref[here] * shrink + lanes
        sums_ref[here] = sums_ref[here] * shrink + jnp.dot(
            weights.astype(jnp.bfloat16), values, preferred_element_type=jnp.float32
        )


def stack_queries(q_ref, stacked_ref):
    tokens, width = q_ref.shape
    size = stacked_ref.shape[1]
    for head in range(width // size):
        stacked_ref[head * tokens:(head + 1) * tokens, :] = q_ref[:, head * size:(head + 1) * size]


def load_state(loaded_ref, max_ref, lanes_ref, sums_ref):
    count, size = max_ref.shape
    lane = lax.broadcasted_iota(jnp.int32, (count, size), 1)
    sums_ref[...] = loaded_ref[0]
    lanes_ref[...] = jnp.where(lane == 0, loaded_ref[1], 0.0)
    max_ref[...] = jnp.broadcast_to(loaded_ref[1, :, size - 1:], (count, size))


def save_state(max_ref, lanes_ref, sums_ref, saved_ref):
    count, size = max_ref.shape
    left = lax.broadcasted_iota(jnp.int32, (count, size), 1) < size // 2
    saved_ref[0] = sums_ref[...]
    saved_ref[1] = jnp.where(left, jnp.sum(lanes_ref[...], axis=1, keepdims=True), max_ref[...])


def finish(lanes_ref, sums_ref, out_ref):
    tokens = out_ref.shape[0]
    size = sums_ref.shape[1]
    for head in range(out_ref.shape[1] // size):
        here = slice(head * tokens, (head + 1) * tokens)
        out_ref[:, head * size:(head + 1) * size] = (
            sums_ref[here] / jnp.sum(lanes_ref[here], axis=1, keepdims=True)
        ).astype(out_ref.dtype)


def local_kernel(factor, len_ref, q_ref, suffix_ref, own_ref, after_ref, out_ref, *work):
    q_stacked, max_ref, lanes_ref, sums_ref = work
    size = sums_ref.shape[1]
    suffix, own = suffix_ref.shape[0], own_ref.shape[0]
    stack_queries(q_ref, q_stacked)
    max_ref[...] = jnp.full(max_ref.shape, NEG, jnp.float32)
    lanes_ref[...] = jnp.zeros(lanes_ref.shape, jnp.float32)
    sums_ref[...] = jnp.zeros(sums_ref.shape, jnp.float32)
    block = min(ROWS, sums_ref.shape[0])
    token = lax.broadcasted_iota(jnp.int32, (block, suffix), 0) % suffix
    key = lax.broadcasted_iota(jnp.int32, (block, suffix), 1)
    causal = jnp.where(key <= token, 0.0, NEG)
    fold_keys(work, suffix_ref[:, :size], suffix_ref[:, size:], factor, causal)
    dead = jnp.where(lax.broadcasted_iota(jnp.int32, (1, own), 1) < len_ref[0], 0.0, NEG)
    fold_keys(work, own_ref[:, :size], own_ref[:, size:], factor, dead)
    save_state(max_ref, lanes_ref, sums_ref, out_ref)


def moved_kernel(factor, steps, q_ref, kv_ref, loaded_ref, out_ref, *work):
    step = pl.program_id(0)
    size = work[3].shape[1]

    @pl.when(step == 0)
    def _():
        stack_queries(q_ref, work[0])
        load_state(loaded_ref, *work[1:])

    rows = kv_ref[...].reshape(-1, kv_ref.shape[-1])
    dead = jnp.where(rows[:, size:].astype(jnp.float32) > DEAD_ABOVE, NEG, 0.0).T[:1]
    fold_keys(work, rows[:, :size], rows[:, size:], factor, dead)

    @pl.when(step == steps - 1)
    def _():
        save_state(*work[1:], out_ref)


def prefix_kernel(factor, count, steps, owner_ref, reader_ref, me_ref, q_ref, *refs):
    pieces = refs[:count]
    loaded_ref, out_ref, *work, rows_ref = refs[count:]
    step = pl.program_id(0)
    size = work[3].shape[1]
    chunk = rows_ref.shape[0] // steps

    @pl.when(step == 0)
    def _():
        stack_queries(q_ref, work[0])
        place = 0
        for piece in pieces:
            rows_ref[pl.ds(place, piece.shape[0]), :] = piece[...]
            place += piece.shape[0]
        load_state(loaded_ref, *work[1:])

    rows = pl.ds(pl.multiple_of(step * chunk, size), chunk)
    fold_keys(work, rows_ref[rows, :size], rows_ref[rows, size:], factor)

    @pl.when(step == steps - 1)
    def _():
        save_state(*work[1:], out_ref)


def start_all(copies):
    for copy in copies:
        copy.start()


def wait_all(copies):
    for copy in copies:
        copy.wait()


def last_kernel(factor, steps, owner_ref, reader_ref, me_ref, q_ref, kv_ref, *refs):
    *pieces, loaded_ref, out_ref = refs[:-5]
    *work, rows_ref = refs[-5:]
    step = pl.program_id(0)
    size = work[3].shape[1]

    @pl.when(step == 0)
    def _():
        stack_queries(q_ref, work[0])
        load_state(loaded_ref, *work[1:])
        place = 0
        for piece in pieces:
            rows_ref[pl.ds(place, piece.shape[0]), :] = piece[...]
            place += piece.shape[0]

    rows = kv_ref[...].reshape(-1, kv_ref.shape[-1])
    dead = jnp.where(rows[:, size:].astype(jnp.float32) > DEAD_ABOVE, NEG, 0.0).T[:1]
    fold_keys(work, rows[:, :size], rows[:, size:], factor, dead)

    @pl.when(step == steps - 1)
    def _():
        fold_keys(work, rows_ref[:, :size], rows_ref[:, size:], factor)
        finish(*work[2:], out_ref)


def pick_kernel(owner_ref, reader_ref, me_ref, *refs):
    pieces, out_ref = refs[:-1], refs[-1]
    for place, piece in enumerate(pieces):
        out_ref[pl.ds(place * piece.shape[0], piece.shape[0]), :] = piece[...]


def pack_kernel(target_ref, block_ref, count_ref, pool_ref, *refs):
    parts, (held_ref, mark_ref, in_sems, out_sems) = refs[:-4], refs[-4:]
    entries = target_ref.shape[1]
    mark_ref[...] = jnp.full(mark_ref.shape, DEAD_MARK, mark_ref.dtype)

    def load(entry):
        return pltpu.make_async_copy(
            pool_ref.at[block_ref[0, entry]], held_ref.at[entry], in_sems.at[entry]
        )

    def stores(entry, source):
        rows = parts[0].shape[1]
        return [
            pltpu.make_async_copy(
                source.at[pl.ds(place * rows, rows)],
                part.at[target_ref[0, entry]],
                out_sems.at[place, entry],
            )
            for place, part in enumerate(parts)
        ]

    @pl.loop(0, entries)
    def _(entry):
        live = entry < count_ref[0]
        pl.when(live)(lambda: load(entry).start())
        pl.when(jnp.logical_not(live))(lambda: start_all(stores(entry, mark_ref)))

    @pl.loop(0, entries)
    def _(entry):
        @pl.when(entry < count_ref[0])
        def _():
            load(entry).wait()
            start_all(stores(entry, held_ref.at[entry]))

    @pl.loop(0, entries)
    def _(entry):
        wait_all(stores(entry, mark_ref))


def gate_kernel(*refs):
    pass


def gate(rows, *after):
    return pl.pallas_call(
        gate_kernel,
        out_shape=jax.ShapeDtypeStruct(rows.shape, rows.dtype),
        in_specs=[IN_HBM] * (1 + len(after)),
        out_specs=IN_HBM,
        input_output_aliases={0: 0},
        compiler_params=PARAMS,
        name="gate",
    )(rows, *after)


def stage_kernel(owner_ref, kept_ref, swapped_ref, *refs):
    outs, (sought_ref, known_ref, in_sems, out_sems) = refs[:-4], refs[-4:]
    chips, sought = sought_ref.shape[:2]
    replicas = 4 * chips
    me = lax.axis_index("replica")
    core, chip, is_last = me % 2, me // 2 % chips, me // 2 == replicas // 2 - 1
    owners = [owner_ref[prefix] for prefix in range(sought + 1)]
    known = sum(
        jnp.where(owner == replicas - 1, prefix, 0) for prefix, owner in enumerate(owners)
    )
    owners = [
        jnp.where(known <= prefix, owners[prefix + 1], owners[prefix]) for prefix in range(sought)
    ]

    def load(source, step, prefix):
        target = sought_ref.at[step, prefix] if prefix < sought else known_ref.at[step, 0]
        return pltpu.make_async_copy(source.at[core, chip ^ step], target, in_sems.at[step, prefix])

    def start(step, prefix, here):
        pl.when(here)(lambda: load(kept_ref, step, prefix).start())
        pl.when(jnp.logical_not(here))(lambda: load(swapped_ref, step, prefix).start())

    def store(place):
        source = sought_ref.at[place] if place < chips else known_ref.at[place - chips]
        return pltpu.make_async_copy(source, outs[place], out_sems.at[place])

    for step in range(chips):
        for prefix in range(sought):
            start(step, prefix, owners[prefix] % 2 == core)

    @pl.when(is_last)
    def _():
        for step in range(chips):
            start(step, sought, core == 1)

    for step in range(chips):
        for prefix in range(sought):
            load(kept_ref, step, prefix).wait()
        store(step).start()

    @pl.when(is_last)
    def _():
        for step in range(chips):
            load(kept_ref, step, sought).wait()
            store(chips + step).start()
        wait_all([store(chips + step) for step in range(chips)])

    wait_all([store(step) for step in range(chips)])


def multicast(prefix_cache, owners, outgoing, fold_local, fold_moved):
    replicas = lax.axis_size("replica")
    half = replicas // 2
    chips = half // 2
    width = prefix_cache.shape[1]
    prefixes = owners.shape[0]

    split = prefix_cache.reshape(2, chips, -1, width)
    swapped, *outgoing = lax.optimization_barrier((swap_cores(prefix_cache), *outgoing))
    arrived = send_blocks(outgoing[0])
    swapped = swapped.reshape(split.shape)
    pieces = jax.ShapeDtypeStruct((owners.shape[0] - 1, *split.shape[2:]), split.dtype)
    piece = jax.ShapeDtypeStruct((1, *split.shape[2:]), split.dtype)
    staged = pl.pallas_call(
        stage_kernel,
        out_shape=(pieces,) * chips
        + (piece,) * chips,
        in_specs=[IN_SMEM] + [IN_HBM] * 2,
        out_specs=(IN_HBM,) * (2 * chips),
        scratch_shapes=[
            pltpu.VMEM((chips, *pieces.shape), split.dtype),
            pltpu.VMEM((chips, *piece.shape), split.dtype),
            pltpu.SemaphoreType.DMA((chips, owners.shape[0])),
            pltpu.SemaphoreType.DMA((2 * chips,)),
        ],
        compiler_params=COPY_PARAMS,
        name="stage_prefix",
    )(owners, split, swapped)

    me = lax.axis_index("replica")
    chip = me // 2 % chips
    ids = jnp.arange(prefixes, dtype=jnp.int32)
    known = jnp.sum(jnp.where(owners == replicas - 1, ids, 0))
    sought = jnp.where(ids[:-1] >= known, owners[1:], owners[:-1])
    away, known_away = chip ^ (sought // 2 % chips), (chip ^ (chips - 1))[None]
    held_by = jnp.concatenate([jnp.full((1,), replicas - 1, jnp.int32), sought])
    same_half = held_by // half == me // half

    def to_peers(staged, senders):
        return [
            lax.ppermute(rows, "replica", [(i, i ^ (2 * step)) for i in senders])
            for step, rows in enumerate(staged)
            if step
        ]

    def choose(own, passed, away):
        for step, rows in enumerate(passed, 1):
            own = jnp.where((away == step)[:, None, None], rows, own)
        return own

    passed = to_peers(staged[:chips], range(replicas))
    passed[0], local, *known_staged = lax.optimization_barrier(
        (passed[0], fold_local(staged[0]), *staged[chips:])
    )
    passed_known = to_peers(known_staged, (replicas - 2, replicas - 1))
    found = choose(staged[0], passed, away)
    passed = lax.ppermute(found, "replica", [(i, (i + half) % replicas) for i in range(replicas)])
    found_known = choose(known_staged[0], passed_known, known_away)
    passed_known = lax.ppermute(found_known, "replica", [(i + half, i) for i in range(half)])
    later = send_blocks(gate(outgoing[1], passed, passed_known))
    passed, passed_known, state_now = lax.optimization_barrier(
        (passed, passed_known, fold_moved(arrived, local))
    )
    held = jnp.where(
        same_half[:, None, None],
        jnp.concatenate([found_known, found]),
        jnp.concatenate([passed_known, passed]),
    )
    return held, state_now, later


def send_blocks(rows):
    return lax.all_to_all(rows, "replica", split_axis=0, concat_axis=0, tiled=True)


def swap_cores(rows):
    return lax.ppermute(rows, "replica", [(i, i ^ 1) for i in range(lax.axis_size("replica"))])


def gather_step(gathered, step):
    replicas = lax.axis_size("replica")
    bits = (replicas // 4).bit_length() - 1
    members = [bit for bit in range(bits) if step >> bit & 1]
    linked = [bit for bit in members if step >> ((bit - 1) % bits) & 1]
    last = min(linked or members)
    pairs = [(i, i ^ (2 << last)) for i in range(replicas)]
    return lax.ppermute(gathered[step ^ 1 << last], "replica", pairs)


def wanted_place(owner_ref, reader_ref, who):
    last = reader_ref.shape[0] - 1
    known = sum(
        jnp.where(owner_ref[prefix] == last, prefix, 0) for prefix in range(owner_ref.shape[0])
    )
    wanted = reader_ref[who]
    return jnp.where(wanted == known, 0, jnp.where(wanted < known, wanted + 1, wanted))


def from_other(pieces, scalars):
    rows, width = pieces[0].shape[1:]
    spec = pl.BlockSpec(
        (None, rows, width),
        lambda i, owner, reader, me: (wanted_place(owner, reader, me[0] ^ 1), 0, 0),
    )
    picked = pl.pallas_call(
        pick_kernel,
        out_shape=jax.ShapeDtypeStruct((len(pieces) * rows, width), pieces[0].dtype),
        grid_spec=pltpu.PrefetchScalarGridSpec(
            num_scalar_prefetch=3,
            grid=(1,),
            in_specs=[spec] * len(pieces),
            out_specs=whole((len(pieces) * rows, width)),
        ),
        compiler_params=PARAMS,
        name="pick_other",
    )(*scalars, *pieces)
    return swap_cores(picked)


def whole(shape):
    return pl.BlockSpec(shape, lambda *args: (0,) * len(shape))


def cost(rows, keys, size):
    return pl.CostEstimate(
        flops=12 * rows * keys * size, bytes_accessed=4 * keys * size, transcendentals=rows * keys
    )


def on_device(
    queries,
    suffix_kv,
    own_cache,
    ctx_len,
    prefix_cache,
    owners,
    readers,
    kv_pool,
    mig_target,
    mig_block,
    mig_count,
):
    replicas = lax.axis_size("replica")
    size = suffix_kv.shape[1] // 2
    tokens = queries.shape[0]
    heads = queries.shape[1] // size
    factor = size ** (-0.5) * LOG2E
    row_count = tokens * heads
    state = jax.ShapeDtypeStruct((2, row_count, size), jnp.float32)
    result = jax.ShapeDtypeStruct(queries.shape, queries.dtype)

    work = [
        pltpu.VMEM((row_count, size), queries.dtype),
        *[pltpu.VMEM((row_count, size), jnp.float32)] * 3,
    ]

    entries = mig_target.shape[1]
    half_block = (replicas, kv_pool.shape[1] // 2, kv_pool.shape[2])
    slots = (jax.ShapeDtypeStruct(half_block, kv_pool.dtype),) * 2
    outgoing = pl.pallas_call(
        pack_kernel,
        out_shape=slots,
        in_specs=[IN_SMEM] * 3 + [IN_HBM],
        out_specs=(IN_HBM,) * 2,
        scratch_shapes=[
            pltpu.VMEM((entries, *kv_pool.shape[1:]), kv_pool.dtype),
            pltpu.VMEM(kv_pool.shape[1:], kv_pool.dtype),
            pltpu.SemaphoreType.DMA((entries,)),
            pltpu.SemaphoreType.DMA((2, entries)),
        ],
        compiler_params=COPY_PARAMS,
        name="pack_moved",
    )(mig_target, mig_block, mig_count, kv_pool)
    def fold_local(after):
        return pl.pallas_call(
            functools.partial(local_kernel, factor),
            out_shape=state,
            grid=(1,),
            in_specs=[
                IN_SMEM,
                whole(queries.shape),
                whole(suffix_kv.shape),
                whole(own_cache.shape),
                IN_HBM,
            ],
            out_specs=whole(state.shape),
            scratch_shapes=work,
            compiler_params=PARAMS,
            cost_estimate=cost(row_count, tokens + own_cache.shape[0], size),
            name="local_keys",
        )(ctx_len, queries, suffix_kv, own_cache, after)

    def fold_moved(arrived, state_now):
        rows = arrived.shape[1]
        group = max(n for n in range(1, replicas + 1) if replicas % n == 0 and n * rows <= CHUNK)
        steps = replicas // group
        return pl.pallas_call(
            functools.partial(moved_kernel, factor, steps),
            out_shape=state,
            grid=(steps,),
            in_specs=[
                whole(queries.shape),
                pl.BlockSpec((group, rows, 2 * size), lambda i: (i, 0, 0)),
                whole(state.shape),
            ],
            out_specs=whole(state.shape),
            scratch_shapes=work,
            compiler_params=PARAMS,
            cost_estimate=cost(row_count, steps * group * rows, size),
            name="moved_keys",
        )(queries, arrived, state_now)

    def wanted_pieces(pieces):
        spec = pl.BlockSpec(
            (None, *pieces[0].shape[1:]),
            lambda i, owner, reader, me: (wanted_place(owner, reader, me[0]), 0, 0),
        )
        return [spec] * len(pieces)

    def fold_prefix(pieces, state_now):
        others = from_other(pieces, scalars)
        keys = 2 * len(pieces) * pieces[0].shape[1]
        steps = max(1, keys // CHUNK)
        while keys % (steps * size):
            steps -= 1
        return pl.pallas_call(
            functools.partial(prefix_kernel, factor, len(pieces) + 1, steps),
            out_shape=state,
            grid_spec=pltpu.PrefetchScalarGridSpec(
                num_scalar_prefetch=3,
                grid=(steps,),
                in_specs=[
                    whole(queries.shape),
                    *wanted_pieces(pieces),
                    whole(others.shape),
                    whole(state.shape),
                ],
                out_specs=whole(state.shape),
                scratch_shapes=[*work, pltpu.VMEM((keys, 2 * size), jnp.bfloat16)],
            ),
            compiler_params=PARAMS,
            cost_estimate=cost(row_count, keys, size),
            name="prefix_keys",
        )(*scalars, queries, *pieces, others, state_now)

    def fold_last(arrived, pieces, state_now):
        others = from_other(pieces, scalars)
        keys = 2 * len(pieces) * pieces[0].shape[1]
        rows = arrived.shape[1]
        group = max(n for n in range(1, replicas + 1) if replicas % n == 0 and n * rows <= CHUNK)
        steps = replicas // group
        return pl.pallas_call(
            functools.partial(last_kernel, factor, steps),
            out_shape=result,
            grid_spec=pltpu.PrefetchScalarGridSpec(
                num_scalar_prefetch=3,
                grid=(steps,),
                in_specs=[
                    whole(queries.shape),
                    pl.BlockSpec((group, rows, 2 * size), lambda i, *scalars: (i, 0, 0)),
                    *wanted_pieces(pieces),
                    whole(others.shape),
                    whole(state.shape),
                ],
                out_specs=whole(queries.shape),
                scratch_shapes=[*work, pltpu.VMEM((keys, 2 * size), jnp.bfloat16)],
            ),
            compiler_params=PARAMS,
            cost_estimate=cost(row_count, replicas * rows + keys, size),
            name="last_keys",
        )(*scalars, queries, arrived, *pieces, others, state_now)

    held, state_now, later = multicast(prefix_cache, owners, outgoing, fold_local, fold_moved)
    scalars = (owners, readers, lax.axis_index("replica")[None])
    gathered = {0: held}
    ready = [held]
    rounds = (replicas // 4).bit_length() - 1
    for near in range(1, rounds + 1):
        steps = [step for step in range(1, replicas // 4) if step.bit_count() == near]
        coming = [gather_step(gathered, step) for step in steps]
        if near > 1:
            *coming, state_now = lax.optimization_barrier(
                (*coming, fold_prefix(ready, state_now))
            )
            ready = []
        gathered.update(zip(steps, coming))
        ready += coming
    return fold_last(later, ready, state_now)


def solution(mesh):
    in_specs = (
        P(("groups", "replica"), None),
        P(("groups", "replica"), None),
        P(("groups", "replica"), None),
        P(("groups", "replica")),
        P(("groups", "replica"), None),
        P("groups"),
        P("groups"),
        P(("groups", "replica"), None, None),
        P(("groups", "replica"), None),
        P(("groups", "replica"), None),
        P(("groups", "replica")),
    )
    out_specs = P(("groups", "replica"), None)
    return jax.shard_map(
        on_device, mesh=mesh, in_specs=in_specs, out_specs=out_specs, check_vma=False
    )
```
